32 devices in a mesh: dp: 4 (over x, core), fsdp: 8 (over z, y).
Axes of the slice: x: 2, y: 2, z: 4, core: 2. Of those that a mesh axis runs over, the one named last changes fastest.
Arguments:
- tokens: bfloat16 [32768, 1024], P(('dp', 'fsdp')), may hold values from -6 to 6
- lengths: int32 [32, 16], P(('dp', 'fsdp')), may hold values from 0 to 1024, as said below
- buckets: int32 [32, 16], P(('dp', 'fsdp')), may hold values from 0 to 999
- w_mod: bfloat16 [1024, 4096], P('fsdp'), may hold values from -0.09375 to 0.09375
- b_mod: bfloat16 [4096], P('fsdp'), may hold values from -1.5 to 1.5
- w_qkv: bfloat16 [1024, 3072], P('fsdp'), may hold values from -0.25 to 0.25
- w_out: bfloat16 [1024, 1024], P('fsdp'), may hold values from -0.75 to 0.75
- b_out: bfloat16 [1024], P('fsdp'), may hold values from -1.5 to 1.5
- w_up: bfloat16 [1024, 4096], P('fsdp'), may hold values from -0.1875 to 0.1875
- b_up: bfloat16 [4096], P('fsdp'), may hold values from -2.5 to 2.5
- w_down: bfloat16 [4096, 1024], P('fsdp'), may hold values from -0.125 to 0.125
- b_down: bfloat16 [1024], P('fsdp'), may hold values from -1.5 to 1.5
- cotangent: bfloat16 [32768, 1024], P(('dp', 'fsdp')), may hold values from -6 to 6
Outputs:
- output: bfloat16 [32768, 1024], P(('dp', 'fsdp'))
- grad_tokens: float32 [32768, 1024], P(('dp', 'fsdp'))
- grad_w_mod: float32 [1024, 4096], P('fsdp')
- grad_b_mod: float32 [4096], P('fsdp')
- grad_w_qkv: float32 [1024, 3072], P('fsdp')
- grad_w_out: float32 [1024, 1024], P('fsdp')
- grad_b_out: float32 [1024], P('fsdp')
- grad_w_up: float32 [1024, 4096], P('fsdp')
- grad_b_up: float32 [4096], P('fsdp')
- grad_w_down: float32 [4096, 1024], P('fsdp')
- grad_b_down: float32 [1024], P('fsdp')
The draws below stay inside these ranges and needn't reach their ends.
Inputs may be any that keep to these rules, and one draw needn't show every extreme that they name: `lengths`: each row lists one device's sequences in order: live entries are multiples of 64, empty slots hold 0 and follow the live ones; a row sums to between 512 and 1024, and the rows of tokens past that sum are padding. In every draw some device holds a single sequence of 1024. `buckets`: entries of empty slots are not used.
All inputs are finite; a program needn't handle non-finite values.
Results may differ from the reference program's by a relative error of at most 0.018.
Values may be sent and summed in bfloat16 or wider, within the bound.
A program may use at most 256 MiB of HBM per device.

```python
import math
import jax
import jax.numpy as jnp
from jax import lax

D = 1024
HEADS = 16
HEAD_DIM = 64
FF = 4096
TOK_DEV = 1024
MINLEN = 64
BUCKETS = 1000
SLOTS = 16
TOKENS = 32768
N_DP = 4
N_FSDP = 8
DEVICES = 32


def draw_lengths(key, part):
    key = jax.random.fold_in(key, 11)
    units = TOK_DEV // MINLEN
    fill_key, cut_key, full_key = jax.random.split(key, 3)
    filled = jax.random.randint(fill_key, (DEVICES,), units // 2, units + 1)
    cut_draw = jax.random.randint(cut_key, (DEVICES, units), 0, 3) == 0
    full_row = jax.random.randint(full_key, (), 0, DEVICES)
    is_full = jnp.arange(DEVICES) == full_row
    filled = jnp.where(is_full, units, filled)
    position = jnp.arange(units)
    cut_marks = cut_draw & (position[None, :] > 0) & (position[None, :] < filled[:, None]) & jnp.logical_not(is_full)[:, None]
    seq_of_unit = jnp.cumsum(cut_marks.astype(jnp.int32), axis=1, dtype=jnp.int32)
    live_units = position[None, :] < filled[:, None]
    slot_ids = jnp.arange(units)
    member = (seq_of_unit[:, :, None] == slot_ids[None, None, :]) & live_units[:, :, None]
    counted = jnp.sum(member.astype(jnp.int32), axis=1, dtype=jnp.int32)
    return (counted * MINLEN).astype(jnp.int32)


def place_ends(values, own_key, low, high):
    spot = [jax.random.randint(jax.random.fold_in(own_key, axis), (), 0, length) for axis, length in enumerate(values.shape)]
    longest = values.shape.index(max(values.shape))
    neighbour = spot[:longest] + [(spot[longest] + 1) % values.shape[longest]] + spot[longest + 1:]
    return values.at[tuple(spot)].set(low).at[tuple(neighbour)].set(high)


def level_of(own_key, extent, cuts, low, top_value):
    def one(axis_at, shards_of):
        draws = jax.random.uniform(jax.random.fold_in(jax.random.fold_in(own_key, 6), axis_at), (shards_of,), jnp.float32, low / len(cuts), top_value / len(cuts))
        return jnp.repeat(jnp.exp(draws), extent[axis_at] // shards_of).reshape((-1,) + (1,) * (len(extent) - axis_at - 1))

    factor_of = one(*cuts[0])
    for cut in cuts[1:]:
        factor_of = factor_of * one(*cut)
    return factor_of


def noise(stream_key, shape, scale, most, cuts=(), held_as=jnp.bfloat16):
    array = scale * jax.random.normal(stream_key, shape, jnp.float32)
    if cuts:
        array = array * level_of(stream_key, shape, cuts, -0.22, 0.18)
    return jnp.clip(array, -most, most).astype(held_as)


def setup_inputs(seed: int = 0) -> dict:
    streams_of = jax.random.split(jax.random.key(seed), 14)
    tokens = noise(streams_of[0], (TOKENS, D), 1.0, 6.0, ((0, 32),))
    lengths = draw_lengths(jax.random.fold_in(streams_of[13], 71), 0)
    buckets = place_ends(jax.random.randint(streams_of[2], (N_DP * N_FSDP, SLOTS), 0, BUCKETS), jax.random.fold_in(streams_of[2], 1), 0, BUCKETS - 1).astype(jnp.int32)
    w_mod = noise(streams_of[3], (D, 4 * D), (4 * D) ** -0.5, 0.09375, ((0, 8),))
    b_mod = noise(streams_of[4], (4 * D,), 0.3, 1.5, ((0, 8),))
    w_qkv = noise(streams_of[5], (D, 3 * D), (D // 2) ** -0.5, 0.25, ((0, 8),))
    w_out = noise(streams_of[6], (D, D), (D // 16) ** -0.5, 0.75, ((0, 8),))
    b_out = noise(streams_of[7], (D,), 0.3, 1.5, ((0, 8),))
    w_up = noise(streams_of[8], (D, FF), D ** -0.5, 0.1875, ((0, 8),))
    b_up = noise(streams_of[9], (FF,), 0.5, 2.5, ((0, 8),))
    w_down = noise(streams_of[10], (FF, D), (FF // 2) ** -0.5, 0.125, ((0, 8),))
    b_down = noise(streams_of[11], (D,), 0.3, 1.5, ((0, 8),))
    cotangent = noise(streams_of[12], (TOKENS, D), 1.0, 6.0, ((0, 32),))
    return {"tokens": tokens, "lengths": lengths, "buckets": buckets, "w_mod": w_mod, "b_mod": b_mod, "w_qkv": w_qkv, "w_out": w_out, "b_out": b_out, "w_up": w_up, "b_up": b_up, "w_down": w_down, "b_down": b_down, "cotangent": cotangent}


EPSILON = 1e-05
HIGHEST = lax.Precision.HIGHEST

@jax.custom_vjp
def low(v):
    return lax.optimization_barrier(v.astype(jnp.bfloat16)).astype(jnp.float32)

@jax.custom_vjp
def low_back(v):
    return v

def low_keep(v):
    return (low(v), None)

def low_pass(kept, grad):
    return (grad,)

def back_keep(v):
    return (v, None)

def back_low(kept, grad):
    return (low(grad),)
low.defvjp(low_keep, low_pass)
low_back.defvjp(back_keep, back_low)

def matmul(left, right):
    return jnp.dot(left, right, precision=HIGHEST)

def layout(lengths, tok_rows):
    seq_ends = jnp.cumsum(lengths, dtype=jnp.int32)
    position = jnp.arange(tok_rows, dtype=jnp.int32)
    segment = lax.optimization_barrier(jnp.sum((position[:, None] >= seq_ends[None, :]).astype(jnp.int32), axis=1, dtype=jnp.int32))
    slot_ids = jnp.arange(lengths.shape[0], dtype=jnp.int32)
    slot_table = (segment[:, None] == slot_ids[None, :]).astype(jnp.float32)
    live_rows = (segment < lengths.shape[0]).astype(jnp.float32)
    return (segment, live_rows, slot_table)

def time_features(buckets):
    half_width = D // 2
    frequency = jnp.exp(-math.log(10000.0) * jnp.arange(half_width, dtype=jnp.float32) / half_width)
    angles = buckets.astype(jnp.float32)[:, None] * frequency[None, :]
    return jnp.concatenate([jnp.sin(angles), jnp.cos(angles)], axis=1)

def normalize(values):
    centred = values - lax.optimization_barrier(jnp.mean(values, axis=1, keepdims=True))
    spread = lax.optimization_barrier(jnp.mean(centred * centred, axis=1, keepdims=True))
    return centred * lax.rsqrt(spread + EPSILON)

def layer_block(inputs, lengths, buckets, params):
    w_mod, b_mod, w_qkv, w_out, b_out, w_up, b_up, w_down, b_down = params
    tok_rows = inputs.shape[0]
    segment, live_rows, slot_table = layout(lengths, tok_rows)
    time_feats = low(time_features(buckets))
    modulation = low_back(matmul(time_feats, w_mod) + b_mod)
    per_row = matmul(slot_table, modulation)
    scale_one = per_row[:, :D]
    shift_one = per_row[:, D:2 * D]
    scale_two = per_row[:, 2 * D:3 * D]
    shift_two = per_row[:, 3 * D:]
    hidden_attn = low(normalize(inputs) * (1.0 + scale_one) + shift_one)
    projected = low(low_back(matmul(hidden_attn, w_qkv)))
    queries = projected[:, :D].reshape(tok_rows, HEADS, HEAD_DIM)
    key_rows = projected[:, D:2 * D].reshape(tok_rows, HEADS, HEAD_DIM)
    value_rows = projected[:, 2 * D:].reshape(tok_rows, HEADS, HEAD_DIM)
    scores = low_back(jnp.einsum('qhd,khd->hqk', queries, key_rows, precision=HIGHEST) * HEAD_DIM ** (-0.5))
    allowed = segment[:, None] == segment[None, :]
    scores = jnp.where(allowed[None], scores, -1e+30)
    attn_probs = jax.nn.softmax(scores, axis=-1)
    mixed = jnp.einsum('hqk,khd->qhd', low(attn_probs), value_rows, precision=HIGHEST)
    attn_out = low(low_back(mixed.reshape(tok_rows, D)))
    branch_one = low_back(matmul(attn_out, w_out) + b_out)
    middle = inputs + live_rows[:, None] * branch_one
    hidden_mlp = low(normalize(middle) * (1.0 + scale_two) + shift_two)
    up_pre = low_back(matmul(hidden_mlp, w_up) + b_up)
    up_act = low(jax.nn.gelu(up_pre))
    branch_two = low_back(matmul(up_act, w_down) + b_down)
    return middle + live_rows[:, None] * branch_two

def layer_all(inputs, params, lengths, buckets):
    blocks = inputs.reshape(-1, TOK_DEV, D)

    def one_block(packed):
        return layer_block(packed[0], packed[1], packed[2], params)
    outputs = lax.map(jax.checkpoint(one_block), (blocks, lengths, buckets))
    return outputs.reshape(inputs.shape)

def reference(tokens, lengths, buckets, w_mod, b_mod, w_qkv, w_out, b_out, w_up, b_up, w_down, b_down, cotangent):
    params = tuple((weight.astype(jnp.float32) for weight in (w_mod, b_mod, w_qkv, w_out, b_out, w_up, b_up, w_down, b_down)))
    inputs = tokens.astype(jnp.float32)

    def whole(inputs_f, params_f):
        return layer_all(inputs_f, params_f, lengths, buckets)
    result, pullback = jax.vjp(whole, inputs, params)
    grad_inputs, grads = pullback(cotangent.astype(jnp.float32))
    grad_w_mod, grad_b_mod, grad_w_qkv, grad_w_out, grad_b_out, grad_w_up, grad_b_up, grad_w_down, grad_b_down = grads
    return (result.astype(jnp.bfloat16), grad_inputs, grad_w_mod, grad_b_mod, grad_w_qkv, grad_w_out, grad_b_out, grad_w_up, grad_b_up, grad_w_down, grad_b_down)
```

```python
import functools
import math

import jax
import jax.numpy as jnp
from jax import lax
from jax.experimental import pallas as pl
from jax.experimental.pallas import tpu as pltpu
from jax.sharding import PartitionSpec as P

D = 1024
HEADS = 16
HEAD_DIM = 64
EPSILON = 1e-05
UNIT = 64
ROWS = 512
ROWS_F = 512
ROWS_B = 512
FF_BLOCK = 512
LSE_LANE = 24
VMEM_LIMIT = 62 * 2**20
HIGHEST = lax.Precision.HIGHEST
MESH = pl.DeviceIdType.MESH


def layout(lengths, tok_rows):
    slots = lengths.shape[0]
    upto = jnp.arange(slots)[:, None] <= jnp.arange(slots)[None, :]
    seq_ends = jnp.sum(jnp.where(upto, lengths[:, None], 0), axis=0, dtype=jnp.int32)
    position = jnp.arange(0, tok_rows, UNIT, dtype=jnp.int32)
    segment = jnp.sum((position[:, None] >= seq_ends[None, :]).astype(jnp.int32), axis=1, dtype=jnp.int32)
    unit_table = (segment[:, None] == jnp.arange(slots, dtype=jnp.int32)[None, :]).astype(jnp.float32)
    return segment, (segment < slots).astype(jnp.float32), unit_table


def time_features(buckets):
    half_width = D // 2
    frequency = jnp.exp(-math.log(10000.0) * jnp.arange(half_width, dtype=jnp.float32) / half_width)
    angles = buckets.astype(jnp.float32)[:, None] * frequency[None, :]
    return jnp.concatenate([jnp.sin(angles), jnp.cos(angles)], axis=1)


def place():
    dp, fsdp = lax.axis_index("dp"), lax.axis_index("fsdp")
    return dp // 2, dp % 2, fsdp // 2, fsdp % 2


def device(x, core, z, y):
    return (x * 2 + core, z * 2 + y)


class Links:
    def __init__(self, send_sems, recv_sems):
        self.send_sems, self.recv_sems, self.used, self.begun = send_sems, recv_sems, 0, []

    def copy(self, src, dst, target):
        slot = self.used
        self.used += 1
        made = pltpu.make_async_remote_copy(
            src_ref=src,
            dst_ref=dst,
            send_sem=self.send_sems.at[slot],
            recv_sem=self.recv_sems.at[slot],
            device_id=target,
            device_id_type=MESH,
        )
        made.start()
        self.begun.append(made)
        return made

    def drain(self):
        for made in self.begun:
            made.wait_send()


def split(extent, unit, share):
    half = extent // 2
    outer = int(half * share / 2) // unit * unit
    return half, outer, half - 2 * outer


def cut(ref, block, rows, axis, start, width):
    if axis == 0:
        first = pl.multiple_of(block * rows + start, 16)
        return ref.at[pl.ds(first, width), :]
    return ref.at[pl.ds(pl.multiple_of(block * rows, 16), rows), pl.ds(pl.multiple_of(start, 128), width)]


def gather_one(shard, whole, links, me, base, extent):
    x, core, z, y = me
    rows = shard.shape[0]
    axis = 1 if shard.shape[1] > rows * 2 else 0
    half, outer, inner = split(extent, 128 if axis else 16, 0.75)
    own = (base + core * half + x * outer, outer + inner)
    crossing = (base + core * half + x * (outer + inner), outer)
    full = (base + core * half, half)
    mine = z * 2 + y

    def part(block, piece):
        return cut(whole, block, rows, axis, *piece)

    first = cut(shard, 0, rows, axis, *own)
    along_z = [None] + [
        links.copy(first, part(mine, own), device(x, core, (z + k) % 4, y)) for k in (1, 2, 3)
    ]
    along_y = [links.copy(first, part(mine, own), device(x, core, z, 1 - y))]
    yield
    order = [("z", 1), ("y", 0), ("z", 2), ("y", 1), ("z", 3), ("y", 2), ("y", 3)]
    crossed, handed = [], []

    def hand_on(j):
        crossed[j][1].wait_recv()
        block = crossed[j][0]
        handed.append(links.copy(part(block, full), part(block, full), device(x, 1 - core, z, y)))

    for j, (way, k) in enumerate(order):
        source_z = (z - k + 4) % 4
        if way == "z":
            block = source_z * 2 + y
            along_z[k].wait_recv()
            along_y.append(links.copy(part(block, own), part(block, own), device(x, core, z, 1 - y)))
        else:
            block = source_z * 2 + 1 - y
            along_y[k].wait_recv()
        crossed.append((block, links.copy(part(block, crossing), part(block, crossing), device(1 - x, core, z, y))))
        if j >= 2:
            hand_on(j - 2)
        yield
    hand_on(5)
    yield
    hand_on(6)
    yield
    for made in handed:
        made.wait_recv()
    yield


GATHER_COPIES = 21


def take_turns(parts):
    parts = list(parts)
    while parts:
        left = []
        for one in parts:
            try:
                next(one)
                left.append(one)
            except StopIteration:
                pass
        parts = left


def staggered(parts, every):
    parts = list(parts)
    turn, active = 0, []
    while parts or active:
        if parts and turn % every == 0:
            active.append(parts.pop(0))
        left = []
        for one in active:
            try:
                next(one)
                left.append(one)
            except StopIteration:
                pass
        active = left
        turn += 1


EVERY = 3


def pieces_of(shape):
    along = shape[1] if shape[1] > shape[0] * 2 else shape[0]
    count = 2 if shape[0] * shape[1] > 2**18 else 1
    return [(i * along // count, along // count) for i in range(count)]


def exchange_small(small, small_all, links, local_sem, me):
    x, core, z, y = me
    number = (x * 2 + core) * 8 + z * 2 + y
    keep = pltpu.make_async_copy(small.at[z * 2 + y], small_all.at[number], local_sem)
    keep.start()
    few = []
    for k in range(1, 32):
        to = (number + k) % 32
        few.append(links.copy(small.at[to % 8], small_all.at[number], (to // 8, to % 8)))
    return keep, few


def gather_kernel(count, *refs):
    small, shards, small_all, wholes = refs[0], refs[1 : 1 + count], refs[1 + count], refs[2 + count : 2 + 2 * count]
    send_sems, recv_sems, local_sems = refs[2 + 2 * count :]
    me = place()
    x, core, z, y = me
    links = Links(send_sems, recv_sems)
    mine = z * 2 + y
    keep, few = exchange_small(small, small_all, links, local_sems.at[count], me)
    kept = []
    for i in range(count):
        rows = shards[i].shape[0]
        kept.append(pltpu.make_async_copy(shards[i], wholes[i].at[pl.ds(pl.multiple_of(mine * rows, 16), rows), :], local_sems.at[i]))
    parts = [
        gather_one(shards[i], wholes[i], links, me, base, extent) for i in range(count) for base, extent in pieces_of(shards[i].shape)
    ]
    for made in kept:
        made.start()
    staggered(parts, EVERY)
    for made in kept:
        made.wait()
    for made in few:
        made.wait_recv()
    keep.wait()
    links.drain()


def gather_all(small, shards):
    count = len(shards)
    copies = 31 + GATHER_COPIES * sum(len(pieces_of(s.shape)) for s in shards)
    out = pl.pallas_call(
        functools.partial(gather_kernel, count),
        out_shape=[jax.ShapeDtypeStruct((32,) + small.shape[1:], small.dtype)]
        + [jax.ShapeDtypeStruct((8 * s.shape[0], s.shape[1]), s.dtype) for s in shards],
        in_specs=[pl.BlockSpec(memory_space=pl.ANY)] * (1 + count),
        out_specs=[pl.BlockSpec(memory_space=pl.ANY)] * (1 + count),
        scratch_shapes=[
            pltpu.SemaphoreType.DMA((copies,)),
            pltpu.SemaphoreType.DMA((copies,)),
            pltpu.SemaphoreType.DMA((count + 1,)),
        ],
        compiler_params=pltpu.CompilerParams(has_side_effects=True),
    )(small, *shards)
    return out[0], out[1:]


def reduce_buffers(shape):
    rows, width = shape[0] // 8, shape[1]
    axis = 1 if width > rows * 2 else 0
    half, outer, inner = split((rows, width)[axis], 128 if axis else 16, 0.5)

    def sized(extent):
        return (extent, width) if axis == 0 else (rows, extent)

    return [
        (8,) + sized(half),
        (8,) + sized(outer),
        (4,) + sized(outer + inner),
        (4,) + sized(outer + inner),
        sized(outer + inner),
    ]


def reduce_one(local, result, lands, links, me):
    x, core, z, y = me
    from_core, from_x, from_y, from_z, from_last = lands
    rows, width = local.shape[0] // 8, local.shape[1]
    axis = 1 if width > rows * 2 else 0
    half, outer, inner = split((rows, width)[axis], 128 if axis else 16, 0.5)
    own = (core * half + x * outer, outer + inner)
    crossing = (core * half + (1 - x) * (outer + inner), outer)
    kept = (core * half + x * (outer + inner), outer)

    def part(block, piece):
        return cut(local, block, rows, axis, *piece)

    def add(block, piece, landed):
        ref = part(block, piece)
        ref[...] = (ref[...].astype(jnp.float32) + landed[...].astype(jnp.float32)).astype(local.dtype)

    blocks = [((z + k) % 4) * 2 for k in (1, 2, 3, 0)]
    by_core = [
        [links.copy(part(b + o, ((1 - core) * half, half)), from_core.at[2 * t + o], device(x, 1 - core, z, y)) for o in (0, 1)]
        for t, b in enumerate(blocks)
    ]
    yield
    by_x, by_y, by_z = [], [], []
    for t in range(7):
        if t < 4:
            for o in (0, 1):
                by_core[t][o].wait_recv()
                add(blocks[t] + o, (core * half, half), from_core.at[2 * t + o])
            by_x.append([
                links.copy(part(blocks[t] + o, crossing), from_x.at[2 * t + o], device(1 - x, core, z, y)) for o in (0, 1)
            ])
        if 1 <= t < 5:
            for o in (0, 1):
                by_x[t - 1][o].wait_recv()
                add(blocks[t - 1] + o, kept, from_x.at[2 * (t - 1) + o])
            by_y.append(links.copy(part(blocks[t - 1] + 1 - y, own), from_y.at[t - 1], device(x, core, z, 1 - y)))
        if 2 <= t < 6:
            by_y[t - 2].wait_recv()
            add(blocks[t - 2] + y, own, from_y.at[t - 2])
            if t - 2 < 3:
                by_z.append(links.copy(part(blocks[t - 2] + y, own), from_z.at[t - 2], device(x, core, (z + t - 1) % 4, y)))
        yield
    mine = part(z * 2 + y, own)
    total = mine[...].astype(jnp.float32)
    for k in range(3):
        by_z[k].wait_recv()
        total = total + from_z[k].astype(jnp.float32)
    mine[...] = total.astype(local.dtype)
    last = links.copy(mine, from_last, device(1 - x, core, z, y))
    yield
    last.wait_recv()

    def place_in(start, size):
        if axis == 0:
            return result.at[pl.ds(pl.multiple_of(core * half + start, 16), size), :]
        return result.at[:, pl.ds(pl.multiple_of(core * half + start, 128), size)]

    def inside(ref, start, size):
        return ref.at[pl.ds(start, size), :] if axis == 0 else ref.at[:, pl.ds(start, size)]

    whole_own = cut(local, z * 2 + y, rows, axis, core * half, half)
    for plane in (0, 1):

        @pl.when(x == plane)
        def _():
            if plane == 0:
                a_mine, b_mine = inside(whole_own, 0, outer), inside(whole_own, outer, inner)
                b_other, a_other = inside(from_last, 0, inner), inside(from_last, inner, outer)
            else:
                b_mine, a_mine = inside(whole_own, outer, inner), inside(whole_own, outer + inner, outer)
                a_other, b_other = inside(from_last, 0, outer), inside(from_last, outer, inner)
            place_in(plane * (outer + inner), outer)[...] = a_mine[...]
            place_in((1 - plane) * (outer + inner), outer)[...] = a_other[...]
            place_in(outer, inner)[...] = (
                b_mine[...].astype(jnp.float32) + b_other[...].astype(jnp.float32)
            ).astype(result.dtype)

    final = links.copy(place_in(0, half), place_in(0, half), device(x, 1 - core, z, y))
    yield
    final.wait_recv()
    yield


REDUCE_COPIES = 8 + 8 + 4 + 3 + 1 + 1


def reduce_kernel(count, smalls, *refs):
    locals_, refs = refs[:count], refs[count:]
    small, refs = refs[:smalls], refs[smalls:]
    results, refs = refs[:count], refs[count:]
    small_all, refs = refs[:smalls], refs[smalls:]
    lands = refs[: 5 * count]
    send_sems, recv_sems, local_sems = refs[5 * count :]
    me = place()
    links = Links(send_sems, recv_sems)
    waiting = [exchange_small(small[i], small_all[i], links, local_sems.at[i], me) for i in range(smalls)]
    parts = [reduce_one(locals_[i], results[i], lands[5 * i : 5 * i + 5], links, me) for i in range(count)]
    take_turns(parts)
    for keep, few in waiting:
        for made in few:
            made.wait_recv()
        keep.wait()
    links.drain()


def reduce_all(grads, small=()):
    count, smalls = len(grads), len(small)
    lands = [pltpu.VMEM(s, jnp.bfloat16) for g in grads for s in reduce_buffers(g.shape)]
    copies = REDUCE_COPIES * count + 31 * smalls
    out = pl.pallas_call(
        functools.partial(reduce_kernel, count, smalls),
        out_shape=[jax.ShapeDtypeStruct((g.shape[0] // 8, g.shape[1]), g.dtype) for g in grads]
        + [jax.ShapeDtypeStruct((32,) + s.shape[1:], s.dtype) for s in small],
        in_specs=[pl.BlockSpec(memory_space=pltpu.VMEM)] * (count + smalls),
        out_specs=[pl.BlockSpec(memory_space=pltpu.VMEM)] * (count + smalls),
        scratch_shapes=lands
        + [pltpu.SemaphoreType.DMA((copies,)), pltpu.SemaphoreType.DMA((copies,)), pltpu.SemaphoreType.DMA((max(smalls, 1),))],
        compiler_params=pltpu.CompilerParams(has_side_effects=True, vmem_limit_bytes=VMEM_LIMIT),
    )(*grads, *small)
    return out[:count], out[count:]


def nt(a, b):
    return lax.dot_general(a, b, (((1,), (1,)), ((), ())), preferred_element_type=jnp.float32)


def tn(a, b):
    return lax.dot_general(a, b, (((0,), (0,)), ((), ())), preferred_element_type=jnp.float32)


def nn(a, b):
    return jnp.dot(a, b, preferred_element_type=jnp.float32)


def normalize(values):
    centred = values - jnp.mean(values, axis=1, keepdims=True)
    inverse = lax.rsqrt(jnp.mean(centred * centred, axis=1, keepdims=True) + EPSILON)
    return (centred * inverse, inverse)


def norm_back(grad_normed, normed, inverse):
    first_mean = jnp.mean(grad_normed, axis=1, keepdims=True)
    second_mean = jnp.mean(grad_normed * normed, axis=1, keepdims=True)
    return inverse * (grad_normed - first_mean - normed * second_mean)


def gelu_both(u):
    c = math.sqrt(2 / math.pi)
    square = u * u
    t = jnp.tanh(u * (c + (c * 0.044715) * square))
    half = 0.5 + 0.5 * t
    value = u * half
    return value, half + value * (1.0 - t) * (c + (3 * c * 0.044715) * square)


def loop(count, body):
    def step(i, carry):
        body(i)
        return carry

    lax.fori_loop(0, count, step, 0)


def mlp_kernel(
    attn_ref, tok_ref, cot_ref, wout_ref, bout_ref, scale_ref, shift_ref, live_ref, up_ref, bup_ref, down_ref, bdown_ref,
    out_ref, mid_grad_ref, attn_grad_ref, gout_ref, gbout_ref, gup_ref, gbup_ref, gdown_ref, gbdown_ref, gscale_ref, gshift_ref,
    middle, hidden, two, acc, back, act, pre,
):
    j = pl.program_id(0)
    rows = tok_ref.shape[0]
    blocks, units = rows // ROWS, ROWS // UNIT

    @pl.when(j == 0)
    def _():
        gbdown_ref[...] = jnp.zeros_like(gbdown_ref)

        def block(r):
            here = pl.ds(pl.multiple_of(r * ROWS, ROWS), ROWS)
            middle[here, :] = nn(attn_ref[here, :], wout_ref[...]) + bout_ref[...].astype(jnp.float32)

            for i in range(units):
                u = r * units + i
                at = pl.ds(pl.multiple_of(u * UNIT, UNIT), UNIT)
                live = live_ref[pl.ds(u, 1), :]
                value = tok_ref[at, :].astype(jnp.float32) + live * middle[at, :]
                middle[at, :] = value
                normed, _ = normalize(value)
                hidden[at, :] = (normed * (1.0 + scale_ref[pl.ds(u, 1), :]) + shift_ref[pl.ds(u, 1), :]).astype(jnp.bfloat16)
                grad = (live * cot_ref[at, :].astype(jnp.float32)).astype(jnp.bfloat16)
                two[at, :] = grad
                gbdown_ref[...] += jnp.sum(grad.astype(jnp.float32), axis=0, keepdims=True)

        loop(blocks, block)

    gbup_ref[...] = jnp.zeros_like(gbup_ref)

    def block(r):
        here = pl.ds(pl.multiple_of(r * ROWS, ROWS), ROWS)
        value, slope = gelu_both(nn(hidden[here, :], up_ref[...]) + bup_ref[...].astype(jnp.float32))
        value = value.astype(jnp.bfloat16)
        grad = (nt(two[here, :], down_ref[...]) * slope).astype(jnp.bfloat16)
        act[here, :] = value
        pre[here, :] = grad
        gbup_ref[...] += jnp.sum(grad.astype(jnp.float32), axis=0, keepdims=True)
        forward, backward = nn(value, down_ref[...]), nt(grad, up_ref[...])

        @pl.when(j == 0)
        def _():
            acc[here, :] = forward
            back[here, :] = backward

        @pl.when(j > 0)
        def _():
            acc[here, :] += forward
            back[here, :] += backward

    loop(blocks, block)
    gdown_ref[...] = tn(act[...], two[...]).astype(jnp.bfloat16)
    gup_ref[...] = tn(hidden[...], pre[...]).astype(jnp.bfloat16)

    @pl.when(j == pl.num_programs(0) - 1)
    def _():
        gbout_ref[...] = jnp.zeros_like(gbout_ref)

        def block(r):
            for i in range(units):
                u = r * units + i
                at = pl.ds(pl.multiple_of(u * UNIT, UNIT), UNIT)
                live = live_ref[pl.ds(u, 1), :]
                value = middle[at, :]
                out_ref[at, :] = (value + live * (acc[at, :] + bdown_ref[...].astype(jnp.float32))).astype(jnp.bfloat16)
                normed, inverse = normalize(value)
                grad = back[at, :]
                gshift_ref[pl.ds(u, 1), :] = jnp.sum(grad, axis=0, keepdims=True)
                gscale_ref[pl.ds(u, 1), :] = jnp.sum(grad * normed, axis=0, keepdims=True)
                passed = cot_ref[at, :].astype(jnp.float32) + norm_back(grad * (1.0 + scale_ref[pl.ds(u, 1), :]), normed, inverse)
                mid_grad_ref[at, :] = passed
                one = (live * passed).astype(jnp.bfloat16)
                two[at, :] = one
                gbout_ref[...] += jnp.sum(one.astype(jnp.float32), axis=0, keepdims=True)
            here = pl.ds(pl.multiple_of(r * ROWS, ROWS), ROWS)
            attn_grad_ref[here, :] = nt(two[here, :], wout_ref[...]).astype(jnp.bfloat16)

        loop(blocks, block)

        def part(r):
            here = pl.ds(pl.multiple_of(r * ROWS, ROWS), ROWS)
            gout_ref[here, :] = tn(attn_ref[:, here], two[...]).astype(jnp.bfloat16)

        loop(D // ROWS, part)


def feed_forward(attn_out, tokens, cotangent, w_out, b_out, scale, shift, live, w_up, b_up, w_down, b_down):
    rows, ff = tokens.shape[0], w_up.shape[1]
    once = lambda shape: pl.BlockSpec(shape, lambda j: (0, 0), pipeline_mode=pl.Buffered(1))
    wide = pl.BlockSpec((D, FF_BLOCK), lambda j: (0, j))
    tall = pl.BlockSpec((FF_BLOCK, D), lambda j: (j, 0))
    narrow = pl.BlockSpec((1, FF_BLOCK), lambda j: (0, j))
    row, whole, units = once((1, D)), once((rows, D)), once((rows // UNIT, D))
    f32, b16 = jnp.float32, jnp.bfloat16
    return pl.pallas_call(
        mlp_kernel,
        grid=(ff // FF_BLOCK,),
        out_shape=[
            jax.ShapeDtypeStruct((rows, D), b16), jax.ShapeDtypeStruct((rows, D), f32), jax.ShapeDtypeStruct((rows, D), b16),
            jax.ShapeDtypeStruct((D, D), b16), jax.ShapeDtypeStruct((1, D), f32),
            jax.ShapeDtypeStruct((D, ff), b16), jax.ShapeDtypeStruct((1, ff), f32),
            jax.ShapeDtypeStruct((ff, D), b16), jax.ShapeDtypeStruct((1, D), f32),
            jax.ShapeDtypeStruct((rows // UNIT, D), f32), jax.ShapeDtypeStruct((rows // UNIT, D), f32),
        ],
        in_specs=[whole, whole, whole, once((D, D)), row, units, units, units, wide, narrow, tall, row],
        out_specs=[whole, whole, whole, once((D, D)), row, wide, narrow, tall, row, units, units],
        scratch_shapes=[
            pltpu.VMEM((rows, D), f32), pltpu.VMEM((rows, D), b16), pltpu.VMEM((rows, D), b16),
            pltpu.VMEM((rows, D), f32), pltpu.VMEM((rows, D), f32),
            pltpu.VMEM((rows, FF_BLOCK), b16), pltpu.VMEM((rows, FF_BLOCK), b16),
        ],
        compiler_params=pltpu.CompilerParams(vmem_limit_bytes=VMEM_LIMIT),
    )(attn_out, tokens, cotangent, w_out, b_out, scale, shift, live, w_up, b_up, w_down, b_down)


def attention_lanes(segment, slots):
    lane = jnp.arange(128) % 64
    hot = segment[:, None] == lane[None, :]
    listed = lane[None, :] <= slots
    query_lanes = (hot & listed).astype(jnp.bfloat16)
    ones = (lane >= LSE_LANE) & (lane < LSE_LANE + 3)
    key_lanes = jnp.where(listed & ~hot, -1e30, jnp.where(ones[None, :], 1.0, 0.0)).astype(jnp.bfloat16)
    return query_lanes, key_lanes


def attend_pair(q_ref, k_ref, v_ref, ql_ref, kl_ref, out_ref, qa_ref):
    rows = q_ref.shape[0]
    block = min(ROWS_F, rows)
    low = lax.broadcasted_iota(jnp.int32, (1, 128), 1) < HEAD_DIM
    lane = lax.broadcasted_iota(jnp.int32, (1, 128), 1) % HEAD_DIM
    keys, vals = [], []
    for own in (low, ~low):
        keys.append(jnp.where(own, k_ref[...], kl_ref[...]))
        vals.append(jnp.where(own, v_ref[...], jnp.bfloat16(1)))
    for first in range(0, rows, block):
        here = pl.ds(first, block)
        queries = q_ref[here, :] * jnp.bfloat16(HEAD_DIM**-0.5)
        mixed = []
        for head, own in enumerate((low, ~low)):
            asked = jnp.where(own, queries, ql_ref[here, :])
            scores = nt(asked, keys[head])
            top = jnp.max(scores, axis=1, keepdims=True)
            weight = jnp.exp(scores - top).astype(jnp.bfloat16)
            both = nn(weight, vals[head])
            mixed.append(both)
            log_total = -(top + jnp.log(both))
            first_part = log_total.astype(jnp.bfloat16)
            rest = log_total - first_part.astype(jnp.float32)
            second = rest.astype(jnp.bfloat16)
            third = (rest - second.astype(jnp.float32)).astype(jnp.bfloat16)
            for at, part in enumerate((first_part, second, third)):
                asked = jnp.where(~own & (lane == LSE_LANE + at), part, asked)
            qa_ref[head, here, :] = asked
        total = pltpu.roll(jnp.where(low, mixed[1], mixed[0]), HEAD_DIM, 1)
        out_ref[here, :] = (jnp.where(low, mixed[0], mixed[1]) / total).astype(jnp.bfloat16)


def attend_back_pair(k_ref, v_ref, kl_ref, qa_ref, out_ref, go_ref, grad_ref, kt_ref, dqt_ref):
    rows = k_ref.shape[0]
    block = min(ROWS_B, rows)
    low = lax.broadcasted_iota(jnp.int32, (1, 128), 1) < HEAD_DIM
    grads = go_ref[...]
    product = pltpu.roll(-(grads.astype(jnp.float32) * out_ref[...].astype(jnp.float32)), HEAD_DIM, 1).astype(jnp.bfloat16)
    kt_ref[...] = k_ref[...].astype(jnp.float32).T.astype(jnp.bfloat16)
    given = [jnp.where(own, grads, product) for own in (low, ~low)]
    for first in range(0, rows, block):
        here = pl.ds(first, block)
        dks, dvs = [], []
        for head, own in enumerate((low, ~low)):
            keys = jnp.where(own, k_ref[here, :], kl_ref[here, :])
            vals = jnp.where(own, v_ref[here, :], jnp.bfloat16(1))
            probs = jnp.exp(nt(keys, qa_ref[head]))
            slopes = nt(vals, given[head])
            moved = (probs * slopes).astype(jnp.bfloat16)
            dvs.append(nn(probs.astype(jnp.bfloat16), grads))
            dks.append(nn(moved, qa_ref[head]))
            part = nn(kt_ref[head * HEAD_DIM : (head + 1) * HEAD_DIM, here], moved)
            where = pl.ds(head * HEAD_DIM, HEAD_DIM)
            if first == 0:
                dqt_ref[where, :] = part
            else:
                dqt_ref[where, :] += part
        grad_ref[1, here, :] = jnp.where(low, dks[0], dks[1]).astype(jnp.bfloat16)
        grad_ref[2, here, :] = jnp.where(low, dvs[0], dvs[1]).astype(jnp.bfloat16)
    grad_ref[0] = (dqt_ref[...].T * HEAD_DIM**-0.5).astype(jnp.bfloat16)


def attend(projected, query_lanes, key_lanes):
    rows = projected.shape[0]
    pairs = D // 128
    spec = lambda shift: pl.BlockSpec((rows, 128), lambda i: (0, i + shift))
    lanes = pl.BlockSpec((rows, 128), lambda i: (0, 0))
    return pl.pallas_call(
        attend_pair,
        grid=(pairs,),
        out_shape=[jax.ShapeDtypeStruct((rows, D), jnp.bfloat16), jax.ShapeDtypeStruct((HEADS, rows, 128), jnp.bfloat16)],
        in_specs=[spec(0), spec(pairs), spec(2 * pairs), lanes, lanes],
        out_specs=[spec(0), pl.BlockSpec((2, rows, 128), lambda i: (i, 0, 0))],
        compiler_params=pltpu.CompilerParams(vmem_limit_bytes=VMEM_LIMIT),
    )(projected, projected, projected, query_lanes, key_lanes)


def attend_back(projected, key_lanes, asked, attn_out, grad_attn):
    rows = projected.shape[0]
    pairs = D // 128
    spec = lambda shift: pl.BlockSpec((rows, 128), lambda i: (0, i + shift))
    lanes = pl.BlockSpec((rows, 128), lambda i: (0, 0))
    return pl.pallas_call(
        attend_back_pair,
        grid=(pairs,),
        out_shape=jax.ShapeDtypeStruct((3, rows, D), jnp.bfloat16),
        in_specs=[spec(pairs), spec(2 * pairs), lanes, pl.BlockSpec((2, rows, 128), lambda i: (i, 0, 0)), spec(0), spec(0)],
        out_specs=pl.BlockSpec((3, rows, 128), lambda i: (0, 0, i)),
        scratch_shapes=[pltpu.VMEM((128, rows), jnp.bfloat16), pltpu.VMEM((128, rows), jnp.float32)],
        compiler_params=pltpu.CompilerParams(vmem_limit_bytes=VMEM_LIMIT),
    )(projected, projected, key_lanes, asked, attn_out, grad_attn)


def head_kernel(tok_ref, scale_ref, shift_ref, w_ref, hidden_ref, out_ref):
    rows = tok_ref.shape[0]

    @pl.when(pl.program_id(0) == 0)
    def _():
        def unit(u):
            at = pl.ds(pl.multiple_of(u * UNIT, UNIT), UNIT)
            normed, _ = normalize(tok_ref[at, :].astype(jnp.float32))
            hidden_ref[at, :] = (normed * (1.0 + scale_ref[pl.ds(u, 1), :]) + shift_ref[pl.ds(u, 1), :]).astype(jnp.bfloat16)

        loop(rows // UNIT, unit)

    def block(r):
        here = pl.ds(pl.multiple_of(r * ROWS, ROWS), ROWS)
        out_ref[here, :] = nn(hidden_ref[here, :], w_ref[...]).astype(jnp.bfloat16)

    loop(rows // ROWS, block)


def project_in(tokens, scale, shift, w_qkv):
    rows = tokens.shape[0]
    whole = lambda shape: pl.BlockSpec(shape, lambda j: (0, 0))
    return pl.pallas_call(
        head_kernel,
        grid=(3,),
        out_shape=[jax.ShapeDtypeStruct((rows, D), jnp.bfloat16), jax.ShapeDtypeStruct((rows, 3 * D), jnp.bfloat16)],
        in_specs=[whole((rows, D)), whole((rows // UNIT, D)), whole((rows // UNIT, D)), pl.BlockSpec((D, D), lambda j: (0, j))],
        out_specs=[whole((rows, D)), pl.BlockSpec((rows, D), lambda j: (0, j))],
        compiler_params=pltpu.CompilerParams(vmem_limit_bytes=VMEM_LIMIT),
    )(tokens, scale, shift, w_qkv)


def tail_kernel(grad_ref, hidden_ref, w_ref, tok_ref, mid_ref, scale_ref, gw_ref, gtok_ref, gscale_ref, gshift_ref, back):
    p = pl.program_id(0)
    rows = tok_ref.shape[0]

    def block(r):
        here = pl.ds(pl.multiple_of(r * ROWS, ROWS), ROWS)
        part = nt(grad_ref[0, here, :], w_ref[...])

        @pl.when(p == 0)
        def _():
            back[here, :] = part

        @pl.when(p > 0)
        def _():
            back[here, :] += part

    loop(rows // ROWS, block)

    def columns(r):
        here = pl.ds(pl.multiple_of(r * ROWS, ROWS), ROWS)
        gw_ref[here, :] = tn(hidden_ref[:, here], grad_ref[0]).astype(jnp.bfloat16)

    loop(D // ROWS, columns)

    @pl.when(p == pl.num_programs(0) - 1)
    def _():
        def unit(u):
            at = pl.ds(pl.multiple_of(u * UNIT, UNIT), UNIT)
            normed, inverse = normalize(tok_ref[at, :].astype(jnp.float32))
            grad = back[at, :]
            gshift_ref[pl.ds(u, 1), :] = jnp.sum(grad, axis=0, keepdims=True)
            gscale_ref[pl.ds(u, 1), :] = jnp.sum(grad * normed, axis=0, keepdims=True)
            gtok_ref[at, :] = mid_ref[at, :] + norm_back(grad * (1.0 + scale_ref[pl.ds(u, 1), :]), normed, inverse)

        loop(rows // UNIT, unit)


def project_back(grad_proj, hidden, w_qkv, tokens, grad_mid, scale):
    rows = tokens.shape[0]
    once = lambda shape: pl.BlockSpec(shape, lambda p: (0, 0), pipeline_mode=pl.Buffered(1))
    units, whole = once((rows // UNIT, D)), once((rows, D))
    f32 = jnp.float32
    return pl.pallas_call(
        tail_kernel,
        grid=(3,),
        out_shape=[
            jax.ShapeDtypeStruct((D, 3 * D), jnp.bfloat16), jax.ShapeDtypeStruct((rows, D), f32),
            jax.ShapeDtypeStruct((rows // UNIT, D), f32), jax.ShapeDtypeStruct((rows // UNIT, D), f32),
        ],
        in_specs=[
            pl.BlockSpec((1, rows, D), lambda p: (p, 0, 0)), whole, pl.BlockSpec((D, D), lambda p: (0, p)), whole, whole, units,
        ],
        out_specs=[pl.BlockSpec((D, D), lambda p: (0, p)), whole, units, units],
        scratch_shapes=[pltpu.VMEM((rows, D), f32)],
        compiler_params=pltpu.CompilerParams(vmem_limit_bytes=VMEM_LIMIT),
    )(grad_proj, hidden, w_qkv, tokens, grad_mid, scale)


def tuned(sizes):
    return sizes == (4, 8)


def gathered(sizes, shards, biases, feats):
    n = sizes[1]
    if not tuned(sizes):
        every = lax.all_gather(feats, ("dp", "fsdp"), axis=0, tiled=True)
        return (
            [lax.all_gather(w, "fsdp", axis=0, tiled=True) for w in shards],
            [lax.all_gather(b, "fsdp", axis=0, tiled=True) for b in biases],
            lax.dynamic_slice(every, (0, lax.axis_index("fsdp") * (D // n)), (every.shape[0], D // n)),
        )
    slots = feats.shape[0]
    packed = jnp.concatenate(biases).reshape(-1, 128)
    packed = jnp.pad(packed, ((0, 16 - packed.shape[0]), (0, 0)))
    by_owner = feats.reshape(slots, n, 128).transpose(1, 0, 2)
    small = jnp.concatenate([jnp.broadcast_to(packed, (n, 16, 128)), by_owner], axis=1)
    small_all, weights = gather_all(small, shards)
    of_group = lax.dynamic_slice(small_all, (lax.axis_index("dp") * n, 0, 0), (n, 16, 128))
    wholes, first = [], 0
    for b in biases:
        count = b.shape[0] // 128
        wholes.append(of_group[:, first : first + count].reshape(-1))
        first += count
    return weights, wholes, small_all[:, 16:].reshape(-1, 128)


def reduced(sizes, grads, sums=None):
    n = sizes[1]
    if tuned(sizes):
        if sums is None:
            totals, _ = reduce_all(grads)
            shares = None
        else:
            packed = jnp.concatenate([s.reshape(n, -1, 128) for s in sums], axis=1)
            totals, [every] = reduce_all(grads, [jnp.pad(packed, ((0, 0), (0, 16 - packed.shape[1]), (0, 0)))])
            total, shares, first = jnp.sum(every, axis=0), [], 0
            for s in sums:
                count = s.shape[0] // n // 128
                shares.append(total[first : first + count].reshape(-1))
                first += count
    else:
        totals = [lax.psum(lax.psum_scatter(g, "fsdp", scatter_dimension=0, tiled=True), "dp") for g in grads]
        shares = sums
        if sums is not None:
            shares = [lax.psum(lax.psum_scatter(s, "fsdp", scatter_dimension=0, tiled=True), "dp") for s in sums]
    return [t.astype(jnp.float32) for t in totals], shares


def local(
    sizes, tokens, lengths, buckets, w_mod, b_mod, w_qkv, w_out, b_out, w_up, b_up, w_down, b_down, cotangent,
):
    rows, slots = tokens.shape[0], lengths.shape[1]
    segment, live, unit_table = layout(lengths[0], rows)
    feats = time_features(buckets[0]).astype(jnp.bfloat16)
    weights, biases, every_feats = gathered(sizes, (w_mod, w_qkv, w_out, w_up, w_down), (b_mod, b_out, b_up, b_down), feats)
    full_mod, full_qkv, full_out, full_up, full_down = weights
    full_bmod, full_bout, full_bup, full_bdown = biases
    modulation = jnp.dot(feats, full_mod, preferred_element_type=jnp.float32) + full_bmod
    per_unit = jnp.dot(unit_table, modulation, precision=HIGHEST)
    scale_one, shift_one, scale_two, shift_two = [per_unit[:, i * D : (i + 1) * D] for i in range(4)]
    live_units = jnp.broadcast_to(live[:, None], (rows // UNIT, D))
    hidden_attn, projected = project_in(tokens, scale_one, shift_one, full_qkv)
    query_lanes, key_lanes = attention_lanes(jnp.repeat(segment, UNIT), slots)
    attn_out, asked = attend(projected, query_lanes, key_lanes)
    (
        output, grad_mid, grad_attn, grad_w_out, grad_b_out, grad_w_up, grad_b_up, grad_w_down, grad_b_down, grad_scale_two, grad_shift_two,
    ) = feed_forward(
        attn_out, tokens, cotangent, full_out, full_bout[None], scale_two, shift_two, live_units,
        full_up, full_bup[None], full_down, full_bdown[None],
    )
    (sum_up, sum_down), _ = reduced(sizes, (grad_w_up, grad_w_down))
    grad_proj = attend_back(projected, key_lanes, asked, attn_out, grad_attn)
    grad_w_qkv, grad_tokens, grad_scale_one, grad_shift_one = project_back(
        grad_proj, hidden_attn, full_qkv, tokens, grad_mid, scale_one
    )
    by_unit = jnp.concatenate([grad_scale_one, grad_shift_one, grad_scale_two, grad_shift_two], axis=1)
    grad_mod = jnp.dot(unit_table.T, by_unit, precision=HIGHEST).astype(jnp.bfloat16)
    every_mod = lax.all_gather(grad_mod, ("dp", "fsdp"), axis=0, tiled=True)
    sum_mod = jnp.einsum("sd,sc->dc", every_feats, every_mod, preferred_element_type=jnp.float32)
    grad_b_mod = jnp.sum(grad_mod, axis=0, dtype=jnp.float32)
    (sum_qkv, sum_out), (sum_bmod, sum_bout, sum_bup, sum_bdown) = reduced(
        sizes, (grad_w_qkv, grad_w_out), (grad_b_mod, grad_b_out[0], grad_b_up[0], grad_b_down[0])
    )
    return output, grad_tokens, sum_mod, sum_bmod, sum_qkv, sum_out, sum_bout, sum_up, sum_bup, sum_down, sum_bdown


def solution(mesh):
    sizes = (mesh.shape["dp"], mesh.shape["fsdp"])
    rows, cut_rows, vector = P(("dp", "fsdp"), None), P("fsdp", None), P("fsdp")
    return jax.shard_map(
        functools.partial(local, sizes),
        mesh=mesh,
        in_specs=(rows, rows, rows, cut_rows, vector, cut_rows, cut_rows, vector, cut_rows, vector, cut_rows, vector, rows),
        out_specs=(rows, rows, cut_rows, vector, cut_rows, cut_rows, vector, cut_rows, vector, cut_rows, vector),
        check_vma=False,
    )
```

```python
import functools
import math

import jax
import jax.numpy as jnp
from jax import lax
from jax.experimental import pallas as pl
from jax.experimental.pallas import tpu as pltpu
from jax.sharding import PartitionSpec as P

D = 1024
HEADS = 16
HEAD_DIM = 64
EPSILON = 1e-05
UNIT = 64
ROWS = 512
ATTENTION_ROWS = 512
FF_BLOCKS = 4
EARLY = 2
LSE_LANE = 24
GATHER_EVERY = 1
REDUCE_EVERY = 1
GATHER_START, GATHER_LAGS = 3, (0, 5, 10, 15, 18)
REDUCE_START, REDUCE_LAGS = 3, (0, 3, 9, 16, 22, 26, 28)
VMEM_LIMIT = 62 * 2**20
HIGHEST = lax.Precision.HIGHEST
MESH = pl.DeviceIdType.MESH


def layout(lengths, tok_rows):
    slots = lengths.shape[0]
    upto = jnp.arange(slots)[:, None] <= jnp.arange(slots)[None, :]
    seq_ends = jnp.sum(jnp.where(upto, lengths[:, None], 0), axis=0, dtype=jnp.int32)
    position = jnp.arange(0, tok_rows, UNIT, dtype=jnp.int32)
    segment = jnp.sum((position[:, None] >= seq_ends[None, :]).astype(jnp.int32), axis=1, dtype=jnp.int32)
    unit_table = (segment[:, None] == jnp.arange(slots, dtype=jnp.int32)[None, :]).astype(jnp.float32)
    return segment, (segment < slots).astype(jnp.float32), unit_table


def time_features(buckets):
    half_width = D // 2
    frequency = jnp.exp(-math.log(10000.0) * jnp.arange(half_width, dtype=jnp.float32) / half_width)
    angles = buckets.astype(jnp.float32)[:, None] * frequency[None, :]
    return jnp.concatenate([jnp.sin(angles), jnp.cos(angles)], axis=1)


def place():
    dp, fsdp = lax.axis_index("dp"), lax.axis_index("fsdp")
    return dp // 2, dp % 2, fsdp // 2, fsdp % 2


def device(x, core, z, y):
    return (x * 2 + core, z * 2 + y)


class Hop:
    def __init__(self, links, src, dst, target):
        self.links, self.src, self.dst, self.target, self.gone = links, src, dst, target, False
        self.slot = links.used
        links.used += 1
        links.hops.append(self)

    def made(self):
        return pltpu.make_async_remote_copy(
            src_ref=self.src(),
            dst_ref=self.dst(),
            send_sem=self.links.send_sems.at[self.slot],
            recv_sem=self.links.recv_sems.at[self.slot],
            device_id=self.target(),
            device_id_type=MESH,
        )

    def start(self):
        self.made().start()

    def arrived(self):
        self.made().wait_recv()

    def left(self):
        self.gone = True
        self.made().wait_send()


class Near:
    def __init__(self, links, src, dst):
        self.links, self.src, self.dst = links, src, dst
        self.slot = links.used_near
        links.used_near += 1

    def made(self):
        return pltpu.make_async_copy(self.src(), self.dst(), self.links.near_sems.at[self.slot])

    def start(self):
        self.made().start()

    def arrived(self):
        self.made().wait()


class Links:
    def __init__(self, send_sems, recv_sems, near_sems):
        self.send_sems, self.recv_sems, self.near_sems = send_sems, recv_sems, near_sems
        self.used, self.used_near, self.hops, self.ends = 0, 0, [], []

    def drain(self):
        for hop in self.hops:
            if not hop.gone:
                hop.left()
        for near in self.ends:
            near.arrived()


def lanes(at, size):
    return pl.ds(pl.multiple_of(at, 128), size)


def lines(at, size):
    return pl.ds(pl.multiple_of(at, 16), size)


HALVES = (pl.ds(0, 64), pl.ds(64, 64))


def gather_turns(links, me, shard, whole, outer, at=None):
    x, core, z, y = me
    rows, width = shard.shape
    half = width // 2
    inner = half - 2 * outer

    def own():
        return lanes(core * half + x * outer, outer + inner)

    def crossing():
        return lanes(core * half + x * (outer + inner), outer)

    def full():
        return lanes(core * half, half)

    def block(way, k):
        return ((z - k + 4) % 4) * 2 + (y if way == "z" else 1 - y)

    def place_of(index):
        return lines(index * rows, rows) if at is None else lines(index * 128 + at, rows)

    def part(index, columns):
        return whole.at[place_of(index), columns]

    def mine():
        return z * 2 + y

    def from_shard(target):
        return Hop(links, lambda: shard.at[:, own()], lambda: part(mine(), own()), target)

    def pass_on(way, k, columns, target):
        def at():
            return part(block(way, k), columns())

        return Hop(links, at, at, target)

    to_y = lambda: device(x, core, z, 1 - y)
    keep = Near(links, lambda: shard, lambda: whole.at[place_of(mine()), :])
    along_z = {k: from_shard(lambda k=k: device(x, core, (z + k) % 4, y)) for k in (1, 2, 3)}
    along_y = {0: from_shard(to_y)}
    for k in (1, 2, 3):
        along_y[k] = pass_on("z", k, own, to_y)
    order = [("z", 1), ("y", 0), ("z", 2), ("y", 1), ("z", 3), ("y", 2), ("y", 3)]
    crossed = [pass_on(way, k, crossing, lambda: device(1 - x, core, z, y)) for way, k in order] if outer else None
    handed = [pass_on(way, k, full, lambda: device(x, 1 - core, z, y)) for way, k in order]

    def first():
        for k in (1, 2, 3):
            along_z[k].start()
        along_y[0].start()
        keep.start()

    def arrive(j):
        way, k = order[j]
        (along_z if way == "z" else along_y)[k].arrived()
        if way == "z":
            along_y[k].start()
        (crossed if outer else handed)[j].start()

    def hand_on(j):
        if outer:
            crossed[j].arrived()
            handed[j].start()

    def last():
        for hop in handed:
            hop.arrived()
        keep.arrived()

    return [
        first,
        lambda: [arrive(j) for j in (1, 0, 2, 4)],
        lambda: [arrive(j) for j in (3, 5, 6)] + [hand_on(j) for j in (1, 0, 2, 4)],
        lambda: [hand_on(j) for j in (3, 5, 6)],
        last,
    ]


GATHER_HOPS, GATHER_NEAR = 3 + 4 + 7 + 7, 1


def reduce_lands(rows, width=1024, far=True):
    half = width // 2
    outer = half // 4
    shapes = [
        (4, 2, rows, half), (4, 2, rows, outer), (4, rows, half - outer), (3, rows, half - outer), (rows, half - outer),
    ]
    if far:
        shapes.append((4, 2, rows, half))
    return [pltpu.VMEM(s, jnp.bfloat16) for s in shapes]


def reduce_turns(links, me, local, at, result, out, lands):
    x, core, z, y = me
    total, from_x, from_y, from_z, from_last = lands[:5]
    far = lands[5] if len(lands) > 5 else None
    rows, width = result.shape
    half = width // 2
    outer = half // 4
    wide = half - outer

    def own():
        return lanes(x * outer, wide)

    def kept():
        return lanes(x * wide, outer)

    def given():
        return lanes((1 - x) * wide, outer)

    def owners(t, side):
        return local.at[pl.ds(((z + t + 1) % 4) * 2, 2), pl.ds(at, rows), lanes(side * half, half)]

    turns4 = range(4)
    load = [Near(links, lambda t=t: owners(t, core), lambda t=t: far.at[t]) for t in turns4] if far is not None else []
    to_core = [Hop(links, lambda t=t: owners(t, 1 - core), lambda t=t: total.at[t], lambda: device(x, 1 - core, z, y)) for t in turns4]
    to_x = [
        Hop(links, lambda t=t: total.at[t, :, :, given()], lambda t=t: from_x.at[t], lambda: device(1 - x, core, z, y)) for t in turns4
    ]
    to_y = [
        Hop(links, lambda t=t: total.at[t, 1 - y, :, own()], lambda t=t: from_y.at[t], lambda: device(x, core, z, 1 - y)) for t in turns4
    ]
    to_z = [
        Hop(links, lambda t=t: total.at[t, y, :, own()], lambda t=t: from_z.at[t], lambda t=t: device(x, core, (z + t + 1) % 4, y))
        for t in range(3)
    ]
    to_last = Hop(links, lambda: total.at[3, y, :, own()], lambda: from_last, lambda: device(1 - x, core, z, y))
    mine = lambda: result.at[:, lanes(core * half, half)]
    to_final = Hop(links, mine, mine, lambda: device(x, 1 - core, z, y))
    store = Near(links, lambda: result, lambda: out)
    links.ends.append(store)

    def add(index, landed):
        total[index] = (total[index].astype(jnp.float32) + landed.astype(jnp.float32)).astype(total.dtype)

    def first():
        for t in turns4:
            to_core[t].start()
        for near in load:
            near.start()

    def core_turn():
        for t in turns4:
            to_core[t].arrived()
            if far is None:
                to_core[t].left()
                add(t, owners(t, core)[...])
            else:
                load[t].arrived()
                add(t, far[t])
            to_x[t].start()

    def x_turn():
        for t in turns4:
            to_x[t].arrived()
            add((t, slice(None), slice(None), kept()), from_x[t])
            to_y[t].start()

    def y_turn():
        for t in range(3):
            to_y[t].arrived()
            add((t, y, slice(None), own()), from_y[t])
            to_z[t].start()

    def z_turn():
        to_y[3].arrived()
        everything = total[3, y, :, own()].astype(jnp.float32) + from_y[3].astype(jnp.float32)
        for t in range(3):
            to_z[t].arrived()
            everything = everything + from_z[t].astype(jnp.float32)
        total[3, y, :, own()] = everything.astype(total.dtype)
        to_last.start()

    def last_turn():
        to_last.arrived()
        middle = half - 2 * outer
        shared = total[3, y, :, lanes(outer, middle)].astype(jnp.float32) + from_last[:, lanes(x * outer, middle)].astype(jnp.float32)
        result[:, lanes(core * half + outer, middle)] = shared.astype(result.dtype)
        result[:, lanes(core * half + x * wide, outer)] = total[3, y, :, kept()]
        result[:, lanes(core * half + (1 - x) * wide, outer)] = from_last[:, lanes((1 - x) * middle, outer)]
        to_final.start()

    def end():
        to_final.arrived()
        store.start()

    return [first, core_turn, x_turn, y_turn, z_turn, last_turn, end]


REDUCE_HOPS, REDUCE_NEAR = 4 + 4 + 4 + 3 + 2, 5


def merged(units, every, lag=1):
    turns = []
    for i, unit in enumerate(units):
        for k, turn in enumerate(unit):
            at = i * every + k * lag
            turns += [[] for _ in range(at + 1 - len(turns))]
            turns[at].insert(0, turn)
    return turns


def run(turn):
    for action in turn:
        action()


def semaphores(hops, near):
    return [pltpu.SemaphoreType.DMA((hops,)), pltpu.SemaphoreType.DMA((hops,)), pltpu.SemaphoreType.DMA((max(near, 1),))]


def exchange_small(small, small_all, links, me):
    x, core, z, y = me
    number = lambda: (x * 2 + core) * 8 + z * 2 + y
    keep = Near(links, lambda: small.at[z * 2 + y], lambda: small_all.at[number()])
    few = [
        Hop(
            links,
            lambda k=k: small.at[(number() + k) % 8],
            lambda: small_all.at[number()],
            lambda k=k: (((number() + k) % 32) // 8, (number() + k) % 8),
        )
        for k in range(1, 32)
    ]

    def begin():
        keep.start()
        for hop in few:
            hop.start()

    def end():
        keep.arrived()
        for hop in few:
            hop.arrived()

    return begin, end


def factors_turns(links, me, factors, group, whole):
    x, core, z, y = me
    slots = factors.shape[0]
    mine = lambda: group.at[lines((x * 2 + core) * slots, slots), :]
    keep = Near(links, lambda: factors, mine)
    peers = [
        Hop(links, lambda: factors, mine, lambda i=i, j=j: device((x + i) % 2, (core + j) % 2, z, y)) for i, j in ((0, 1), (1, 0), (1, 1))
    ]

    def first():
        keep.start()
        for hop in peers:
            hop.start()

    def second():
        keep.arrived()
        for hop in peers:
            hop.arrived()

    turns = gather_turns(links, me, group, whole, 256)
    return [first, lambda: (second(), turns[0]())] + turns[1:]


FACTOR_HOPS, FACTOR_NEAR = 3 + GATHER_HOPS, 1 + GATHER_NEAR


def nt(a, b):
    return lax.dot_general(a, b, (((1,), (1,)), ((), ())), preferred_element_type=jnp.float32)


def tn(a, b):
    return lax.dot_general(a, b, (((0,), (0,)), ((), ())), preferred_element_type=jnp.float32)


def nn(a, b):
    return jnp.dot(a, b, preferred_element_type=jnp.float32)


def normalize(values):
    centred = values - jnp.mean(values, axis=1, keepdims=True)
    inverse = lax.rsqrt(jnp.mean(centred * centred, axis=1, keepdims=True) + EPSILON)
    return (centred * inverse, inverse)


def norm_back(grad_normed, normed, inverse):
    first_mean = jnp.mean(grad_normed, axis=1, keepdims=True)
    second_mean = jnp.mean(grad_normed * normed, axis=1, keepdims=True)
    return inverse * (grad_normed - first_mean - normed * second_mean)


def gelu_both(u):
    c = math.sqrt(2 / math.pi)
    square = u * u
    t = jnp.tanh(u * (c + (c * 0.044715) * square))
    half = 0.5 + 0.5 * t
    value = u * half
    return value, half + value * (1.0 - t) * (c + (3 * c * 0.044715) * square)


def loop(count, body):
    def step(i, carry):
        body(i)
        return carry

    lax.fori_loop(0, count, step, 0)


def attention_lanes(segment, slots):
    lane = jnp.arange(128) % 64
    hot = segment[:, None] == lane[None, :]
    listed = lane[None, :] <= slots
    query_lanes = (hot & listed).astype(jnp.bfloat16)
    ones = (lane >= LSE_LANE) & (lane < LSE_LANE + 3)
    key_lanes = jnp.where(listed & ~hot, -1e30, jnp.where(ones[None, :], 1.0, 0.0)).astype(jnp.bfloat16)
    return query_lanes, key_lanes


class Host:
    def __init__(self, links, turns, steps, per_step):
        self.links, self.turns, self.steps, self.per_step = links, turns, steps, per_step
        self.step = pl.program_id(0)

    def turn(self, index):
        for hook, turn in sorted(self.turns.items()):
            if hook < self.steps * self.per_step and hook % self.per_step == index:
                pl.when(self.step == hook // self.per_step)(functools.partial(run, turn))

    def finish(self):
        @pl.when(self.step == self.steps - 1)
        def _():
            for hook, turn in sorted(self.turns.items()):
                if hook >= self.steps * self.per_step:
                    run(turn)
            self.links.drain()


def even(turns, hooks):
    placed = {}
    for t, turn in enumerate(turns):
        placed.setdefault(t * hooks // len(turns), []).extend(turn)
    return placed


def placed(schedule):
    turns = {}
    for hook, turn in schedule:
        turns.setdefault(hook, []).insert(0, turn)
    return turns


class Idle:
    def turn(self, index):
        pass

    def finish(self):
        pass


ANY = pl.BlockSpec(memory_space=pl.ANY)


def call(kernel, grid, inputs, outputs, scratch=()):
    made = pl.pallas_call(
        kernel,
        grid=grid,
        out_shape=[jax.ShapeDtypeStruct(shape, kind) for shape, kind, _ in outputs],
        in_specs=[spec for _, spec in inputs],
        out_specs=[spec for _, _, spec in outputs],
        scratch_shapes=list(scratch),
        compiler_params=pltpu.CompilerParams(has_side_effects=True, vmem_limit_bytes=VMEM_LIMIT),
    )
    return made(*[array for array, _ in inputs])


def gather_kernel(widths, *refs):
    count = len(widths)
    small, shards, refs = refs[0], refs[1 : 1 + count], refs[1 + count :]
    small_all, wholes, sems = refs[0], refs[1 : 1 + count], refs[1 + count :]
    me, links = place(), Links(*sems)
    begin, end = exchange_small(small, small_all, links, me)
    units = []
    for shard, whole, width in zip(shards, wholes, widths):
        for first in range(0, width, 1024):
            columns = pl.ds(first, 1024)
            units.append(gather_turns(links, me, shard.at[:, columns], whole.at[:, columns], 128 if len(units) % 2 else 256))
    begin()
    for turn in merged(units, GATHER_EVERY):
        run(turn)
    end()
    links.drain()


def gather_all(small, shards):
    widths = [s.shape[1] for s in shards]
    units = sum(widths) // 1024
    out = call(
        functools.partial(gather_kernel, widths),
        (),
        [(small, ANY)] + [(s, ANY) for s in shards],
        [((32,) + small.shape[1:], small.dtype, ANY)] + [((8 * s.shape[0], s.shape[1]), s.dtype, ANY) for s in shards],
        semaphores(31 + GATHER_HOPS * units, 1 + GATHER_NEAR * units),
    )
    return out[0], out[1:]


def attend_kernel(shared, q_ref, k_ref, v_ref, ql_ref, kl_ref, *refs):
    if shared:
        shards, out_ref, qa_ref, wholes, *sems = refs
        me, links = place(), Links(*sems)
        units = [
            gather_turns(links, me, shards.at[i, half], wholes.at[i], 128 if half.start else 256, half.start)
            for i in range(shared)
            for half in HALVES
        ]
        host = Host(links, even(merged(units, GATHER_EVERY), D // 32), D // 128, 4)
    else:
        (out_ref, qa_ref), host = refs, Idle()
    rows = q_ref.shape[0]
    block = min(ATTENTION_ROWS, rows)
    low = lax.broadcasted_iota(jnp.int32, (1, 128), 1) < HEAD_DIM
    lane = lax.broadcasted_iota(jnp.int32, (1, 128), 1) % HEAD_DIM
    keys, vals = [], []
    for own in (low, ~low):
        keys.append(jnp.where(own, k_ref[...], kl_ref[...]))
        vals.append(jnp.where(own, v_ref[...], jnp.bfloat16(1)))
    for at, first in enumerate(range(0, rows, block)):
        here = pl.ds(first, block)
        queries = q_ref[here, :] * jnp.bfloat16(HEAD_DIM**-0.5)
        mixed = []
        for head, own in enumerate((low, ~low)):
            host.turn(2 * at + head)
            asked = jnp.where(own, queries, ql_ref[here, :])
            scores = nt(asked, keys[head])
            top = jnp.max(scores, axis=1, keepdims=True)
            weight = jnp.exp(scores - top).astype(jnp.bfloat16)
            both = nn(weight, vals[head])
            mixed.append(both)
            log_total = -(top + jnp.log(both))
            first_part = log_total.astype(jnp.bfloat16)
            rest = log_total - first_part.astype(jnp.float32)
            second = rest.astype(jnp.bfloat16)
            third = (rest - second.astype(jnp.float32)).astype(jnp.bfloat16)
            for i, part in enumerate((first_part, second, third)):
                asked = jnp.where(~own & (lane == LSE_LANE + i), part, asked)
            qa_ref[head, here, :] = asked
        total = pltpu.roll(jnp.where(low, mixed[1], mixed[0]), HEAD_DIM, 1)
        out_ref[here, :] = (jnp.where(low, mixed[0], mixed[1]) / total).astype(jnp.bfloat16)
    host.finish()


def attend(projected, query_lanes, key_lanes, shards=None):
    rows, pairs = projected.shape[0], D // 128
    spec = lambda shift: pl.BlockSpec((rows, 128), lambda i: (0, i + shift))
    same = pl.BlockSpec((rows, 128), lambda i: (0, 0))
    inputs = [(projected, spec(0)), (projected, spec(pairs)), (projected, spec(2 * pairs)), (query_lanes, same), (key_lanes, same)]
    outputs = [((rows, D), jnp.bfloat16, spec(0)), ((HEADS, rows, 128), jnp.bfloat16, pl.BlockSpec((2, rows, 128), lambda i: (i, 0, 0)))]
    if shards is None:
        return call(functools.partial(attend_kernel, 0), (pairs,), inputs, outputs)
    units, depth, width = shards.shape
    return call(
        functools.partial(attend_kernel, units),
        (pairs,),
        inputs + [(shards, ANY)],
        outputs + [((units, 8 * depth, width), shards.dtype, ANY)],
        semaphores(2 * GATHER_HOPS * units, 2 * GATHER_NEAR * units),
    )


def attend_back_kernel(counts, k_ref, v_ref, kl_ref, qa_ref, out_ref, go_ref, *refs):
    units = sum(counts)
    if units:
        groups, refs = refs[: len(counts)], refs[len(counts) :]
        small, factors, grad_ref, results, small_all, factor_group, factor_all, kt_ref, dqt_ref, *refs = refs
        summed, lands, sems = refs[0], refs[1 : 1 + 12 * units], refs[1 + 12 * units :]
        me, links = place(), Links(*sems)
        begin, end = exchange_small(small, small_all, links, me)
        locals_ = [group.at[i] for group, count in zip(groups, counts) for i in range(count)]
        plans = [
            reduce_turns(
                links, me, locals_[i // 2], i % 2 * 64, summed.at[i // 2, HALVES[i % 2]], results.at[i // 2, HALVES[i % 2]], lands[6 * i : 6 * i + 6]
            )
            for i in range(2 * units)
        ]
        plans.append(factors_turns(links, me, factors, factor_group, factor_all))
        turns = merged(plans, REDUCE_EVERY, 2)
        turns[0].append(begin)
        turns[-1].append(end)
        host = Host(links, even(turns, D // 32), D // 128, 4)
    else:
        (grad_ref, kt_ref, dqt_ref), host = refs, Idle()
    rows = k_ref.shape[0]
    block = min(ATTENTION_ROWS, rows)
    low = lax.broadcasted_iota(jnp.int32, (1, 128), 1) < HEAD_DIM
    grads = go_ref[...]
    product = pltpu.roll(-(grads.astype(jnp.float32) * out_ref[...].astype(jnp.float32)), HEAD_DIM, 1).astype(jnp.bfloat16)
    kt_ref[...] = k_ref[...].astype(jnp.float32).T.astype(jnp.bfloat16)
    given = [jnp.where(own, grads, product) for own in (low, ~low)]
    for at, first in enumerate(range(0, rows, block)):
        here = pl.ds(first, block)
        dks, dvs = [], []
        for head, own in enumerate((low, ~low)):
            host.turn(2 * at + head)
            keys = jnp.where(own, k_ref[here, :], kl_ref[here, :])
            vals = jnp.where(own, v_ref[here, :], jnp.bfloat16(1))
            probs = jnp.exp(nt(keys, qa_ref[head]))
            slopes = nt(vals, given[head])
            moved = (probs * slopes).astype(jnp.bfloat16)
            dvs.append(nn(probs.astype(jnp.bfloat16), grads))
            dks.append(nn(moved, qa_ref[head]))
            part = nn(kt_ref[head * HEAD_DIM : (head + 1) * HEAD_DIM, here], moved)
            where = pl.ds(head * HEAD_DIM, HEAD_DIM)
            if first == 0:
                dqt_ref[where, :] = part
            else:
                dqt_ref[where, :] += part
        grad_ref[1, here, :] = jnp.where(low, dks[0], dks[1]).astype(jnp.bfloat16)
        grad_ref[2, here, :] = jnp.where(low, dvs[0], dvs[1]).astype(jnp.bfloat16)
    grad_ref[0] = (dqt_ref[...].T * HEAD_DIM**-0.5).astype(jnp.bfloat16)
    host.finish()


VMEM = pl.BlockSpec(memory_space=pltpu.VMEM)


def attend_back(projected, key_lanes, asked, attn_out, grad_attn, groups=(), small=None, factors=None):
    rows, pairs = projected.shape[0], D // 128
    spec = lambda shift: pl.BlockSpec((rows, 128), lambda i: (0, i + shift))
    same = pl.BlockSpec((rows, 128), lambda i: (0, 0))
    two = pl.BlockSpec((2, rows, 128), lambda i: (i, 0, 0))
    inputs = [(projected, spec(pairs)), (projected, spec(2 * pairs)), (key_lanes, same), (asked, two), (attn_out, spec(0)), (grad_attn, spec(0))]
    outputs = [((3, rows, D), jnp.bfloat16, pl.BlockSpec((3, rows, 128), lambda i: (0, 0, i)))]
    scratch = [pltpu.VMEM((128, rows), jnp.bfloat16), pltpu.VMEM((128, rows), jnp.float32)]
    counts = [g.shape[0] for g in groups]
    units = sum(counts)
    if units:
        inputs += [(g, ANY) for g in groups] + [(small, ANY), (factors, ANY)]
        slots, width = factors.shape
        outputs += [((units, 128, D), jnp.bfloat16, ANY), ((32,) + small.shape[1:], small.dtype, ANY)]
        outputs += [((4 * slots, width), factors.dtype, ANY), ((32 * slots, width), factors.dtype, ANY)]
        scratch += [pltpu.VMEM((units, 128, D), jnp.bfloat16)] + [land for _ in range(2 * units) for land in reduce_lands(64)]
        scratch += semaphores(31 + FACTOR_HOPS + 2 * REDUCE_HOPS * units, 1 + FACTOR_NEAR + 2 * REDUCE_NEAR * units)
    return call(functools.partial(attend_back_kernel, counts), (pairs,), inputs, outputs, scratch)


def before_kernel(attn_ref, tok_ref, cot_ref, wout_ref, bout_ref, scale_ref, shift_ref, live_ref, middle_ref, hidden_ref, two_ref, gbdown_ref):
    r = pl.program_id(0)
    rows = tok_ref.shape[0]
    units = rows // UNIT

    @pl.when(r == 0)
    def _():
        gbdown_ref[...] = jnp.zeros_like(gbdown_ref)

    middle_ref[...] = nn(attn_ref[...], wout_ref[0]) + bout_ref[...].astype(jnp.float32)
    for i in range(units):
        u = r * units + i
        at = pl.ds(i * UNIT, UNIT)
        live = live_ref[pl.ds(u, 1), :]
        value = tok_ref[at, :].astype(jnp.float32) + live * middle_ref[at, :]
        middle_ref[at, :] = value
        normed, _ = normalize(value)
        hidden_ref[at, :] = (normed * (1.0 + scale_ref[pl.ds(u, 1), :]) + shift_ref[pl.ds(u, 1), :]).astype(jnp.bfloat16)
        grad = (live * cot_ref[at, :].astype(jnp.float32)).astype(jnp.bfloat16)
        two_ref[at, :] = grad
        gbdown_ref[...] += jnp.sum(grad.astype(jnp.float32), axis=0, keepdims=True)


def before_mlp(attn_out, tokens, cotangent, weights, b_out, scale, shift, live):
    rows = tokens.shape[0]
    block = pl.BlockSpec((256, D), lambda r: (r, 0))
    once = lambda shape: pl.BlockSpec(shape, lambda r: (0,) * len(shape))
    units = once((rows // UNIT, D))
    return call(
        before_kernel,
        (rows // 256,),
        [(attn_out, block), (tokens, block), (cotangent, block), (weights, once((1, D, D))), (b_out, once((1, D))), (scale, units), (shift, units), (live, units)],
        [((rows, D), jnp.float32, block), ((rows, D), jnp.bfloat16, block), ((rows, D), jnp.bfloat16, block), ((1, D), jnp.float32, once((1, D)))],
    )


def mlp_kernel(early, hidden, two, bup_ref, weights, *refs):
    j = pl.program_id(0)
    rows = hidden.shape[0]
    late = FF_BLOCKS - early
    if late:
        shards, acc, back, gbup_ref, grads_ref, results, act, pre, held, made, summed, *refs = refs
        lands, sems = refs[: 20 * early], refs[20 * early :]
    else:
        acc, back, gbup_ref, grads_ref, act, pre, held, made, *sems = refs
    slots = made.shape[0]
    me, links = place(), Links(*sems)
    fetch = [[Near(links, lambda b=b, w=w: weights.at[1 + 2 * b + w], lambda b=b, w=w: held.at[b, w]) for w in (0, 1)] for b in range(early)]
    store = [Near(links, lambda b=b: made.at[b % slots], lambda b=b: grads_ref.at[b - FF_BLOCKS + grads_ref.shape[0]]) for b in range(FF_BLOCKS)]
    kept_blocks = range(FF_BLOCKS - grads_ref.shape[0], FF_BLOCKS)
    if late:
        schedule = []
        for i in range(4 * late):
            b, w, half = early + i // 4, i // 2 % 2, HALVES[i % 2]
            unit = gather_turns(links, me, shards.at[i // 2, half], held.at[b, w], 128 if i % 2 else 256, half.start)
            schedule += [(GATHER_START * i + at, turn) for at, turn in zip(GATHER_LAGS, unit)]
        for i in range(4 * early):
            b, w, half = i // 4, i // 2 % 2, HALVES[i % 2]
            unit = reduce_turns(
                links, me, made.at[b % slots, w], half.start, summed.at[2 * b + w, half], results.at[2 * b + w, half], lands[5 * i : 5 * i + 5]
            )
            schedule += [(16 * (b + 1) + REDUCE_START * (i % 4) + at, turn) for at, turn in zip(REDUCE_LAGS, unit)]
        host = Host(links, placed(schedule), FF_BLOCKS, 16)
    else:
        host = Idle()

    @pl.when(j == 0)
    def _():
        for pair in fetch:
            for near in pair:
                near.start()

    host.turn(0)
    for b in range(early):

        @pl.when(j == b)
        def _():
            for near in fetch[b]:
                near.arrived()

    gbup_ref[...] = jnp.zeros_like(gbup_ref)
    up, down = held.at[j, 0], held.at[j, 1]
    block = rows // 4
    for r in range(4):
        if r:
            host.turn(2 * r)
        here = pl.ds(r * block, block)
        value, slope = gelu_both(nn(hidden[here, :], up[...]) + bup_ref[0].astype(jnp.float32))
        value = value.astype(jnp.bfloat16)
        grad = (nt(two[here, :], down[...]) * slope).astype(jnp.bfloat16)
        act[here, :] = value
        pre[here, :] = grad
        gbup_ref[0] += jnp.sum(grad.astype(jnp.float32), axis=0, keepdims=True)
        host.turn(2 * r + 1)
        forward, backward = nn(value, down[...]), nt(grad, up[...])

        @pl.when(j == 0)
        def _():
            acc[here, :] = forward
            back[here, :] = backward

        @pl.when(j > 0)
        def _():
            acc[here, :] += forward
            back[here, :] += backward

    slot = lax.rem(j, slots)
    for r in range(4):
        here = pl.ds(r * 256, 256)
        for w, (left, right) in enumerate(((hidden, pre), (act, two))):
            host.turn(8 + 2 * r + w)
            value = tn(left[:, here], right[...]).astype(jnp.bfloat16)
            for half in (0, 1):
                made[slot, w, 2 * r + half] = value[half * 128 : half * 128 + 128]
    for b in kept_blocks:
        pl.when(j == b)(store[b].start)

    @pl.when(j == FF_BLOCKS - 1)
    def _():
        for b in kept_blocks:
            store[b].arrived()

    host.finish()


def feed_forward(hidden, two, weights, b_up, shards=None):
    rows = hidden.shape[0]
    once = lambda shape: pl.BlockSpec(shape, lambda j: (0, 0), pipeline_mode=pl.Buffered(1))
    whole = once((rows, D))
    row = pl.BlockSpec((1, 1, D), lambda j: (j, 0, 0))
    f32, b16 = jnp.float32, jnp.bfloat16
    early = FF_BLOCKS if shards is None else EARLY
    late = FF_BLOCKS - early
    kept = late or FF_BLOCKS
    inputs = [(hidden, whole), (two, whole), (b_up, row), (weights, ANY)]
    outputs = [((rows, D), f32, whole), ((rows, D), f32, whole), ((FF_BLOCKS, 1, D), f32, row), ((kept, 2, 8, 128, D), b16, ANY)]
    slots = 2 if late else FF_BLOCKS
    scratch = [
        pltpu.VMEM((rows, D), b16), pltpu.VMEM((rows, D), b16), pltpu.VMEM((FF_BLOCKS, 2, D, D), b16), pltpu.VMEM((slots, 2, 8, 128, D), b16),
    ]
    hops, near = 1, 2 * early + FF_BLOCKS
    if late:
        inputs += [(shards, ANY)]
        outputs += [((2 * early, 128, D), b16, ANY)]
        scratch += [pltpu.VMEM((2 * early, 128, D), b16)] + [land for _ in range(4 * early) for land in reduce_lands(64, far=False)]
        hops = 4 * late * GATHER_HOPS + 4 * early * REDUCE_HOPS
        near += 4 * late * GATHER_NEAR + 4 * early * REDUCE_NEAR
    return call(functools.partial(mlp_kernel, early), (FF_BLOCKS,), inputs, outputs, scratch + semaphores(hops, near))


def after_kernel(
    middle_ref, acc_ref, back_ref, cot_ref, attn_ref, wout_ref, bdown_ref, scale_ref, live_ref,
    out_ref, mid_grad_ref, attn_grad_ref, gout_ref, gbout_ref, gscale_ref, gshift_ref, one_ref, total_ref,
):
    r = pl.program_id(0)
    rows = cot_ref.shape[0]
    units = rows // UNIT

    @pl.when(r == 0)
    def _():
        gbout_ref[...] = jnp.zeros_like(gbout_ref)
        total_ref[...] = jnp.zeros_like(total_ref)

    for i in range(units):
        u = r * units + i
        at = pl.ds(i * UNIT, UNIT)
        live = live_ref[pl.ds(u, 1), :]
        value = middle_ref[at, :]
        out_ref[at, :] = (value + live * (acc_ref[at, :] + bdown_ref[...].astype(jnp.float32))).astype(jnp.bfloat16)
        normed, inverse = normalize(value)
        grad = back_ref[at, :]
        gshift_ref[pl.ds(u, 1), :] = jnp.sum(grad, axis=0, keepdims=True)
        gscale_ref[pl.ds(u, 1), :] = jnp.sum(grad * normed, axis=0, keepdims=True)
        passed = cot_ref[at, :].astype(jnp.float32) + norm_back(grad * (1.0 + scale_ref[pl.ds(u, 1), :]), normed, inverse)
        mid_grad_ref[at, :] = passed
        one = (live * passed).astype(jnp.bfloat16)
        one_ref[at, :] = one
        gbout_ref[...] += jnp.sum(one.astype(jnp.float32), axis=0, keepdims=True)
    attn_grad_ref[...] = nt(one_ref[...], wout_ref[0]).astype(jnp.bfloat16)
    total_ref[...] += tn(attn_ref[...], one_ref[...])

    @pl.when(r == pl.num_programs(0) - 1)
    def _():
        for i in range(8):
            gout_ref[0, i] = total_ref[i * 128 : i * 128 + 128, :].astype(jnp.bfloat16)


def after_mlp(middle, acc, back, cotangent, attn_out, weights, b_down, scale, live):
    rows = middle.shape[0]
    block = pl.BlockSpec((256, D), lambda r: (r, 0))
    once = lambda shape: pl.BlockSpec(shape, lambda r: (0,) * len(shape))
    units, row = once((rows // UNIT, D)), once((1, D))
    f32, b16 = jnp.float32, jnp.bfloat16
    return call(
        after_kernel,
        (rows // 256,),
        [
            (middle, block), (acc, block), (back, block), (cotangent, block), (attn_out, block), (weights, once((1, D, D))),
            (b_down, row), (scale, units), (live, units),
        ],
        [
            ((rows, D), b16, block), ((rows, D), f32, block), ((rows, D), b16, block), ((1, 8, 128, D), b16, once((1, 8, 128, D))), ((1, D), f32, row),
            ((rows // UNIT, D), f32, units), ((rows // UNIT, D), f32, units),
        ],
        [pltpu.VMEM((256, D), b16), pltpu.VMEM((D, D), f32)],
    )


def head_kernel(tok_ref, scale_ref, shift_ref, w_ref, hidden_ref, out_ref):
    rows = tok_ref.shape[0]

    @pl.when(pl.program_id(0) == 0)
    def _():
        def unit(u):
            at = pl.ds(pl.multiple_of(u * UNIT, UNIT), UNIT)
            normed, _ = normalize(tok_ref[at, :].astype(jnp.float32))
            hidden_ref[at, :] = (normed * (1.0 + scale_ref[pl.ds(u, 1), :]) + shift_ref[pl.ds(u, 1), :]).astype(jnp.bfloat16)

        loop(rows // UNIT, unit)

    def block(r):
        here = pl.ds(pl.multiple_of(r * ROWS, ROWS), ROWS)
        out_ref[here, :] = nn(hidden_ref[here, :], w_ref[...]).astype(jnp.bfloat16)

    loop(rows // ROWS, block)


def project_in(tokens, scale, shift, w_qkv):
    rows = tokens.shape[0]
    whole = lambda shape: pl.BlockSpec(shape, lambda j: (0, 0))
    return pl.pallas_call(
        head_kernel,
        grid=(3,),
        out_shape=[jax.ShapeDtypeStruct((rows, D), jnp.bfloat16), jax.ShapeDtypeStruct((rows, 3 * D), jnp.bfloat16)],
        in_specs=[whole((rows, D)), whole((rows // UNIT, D)), whole((rows // UNIT, D)), pl.BlockSpec((D, D), lambda j: (0, j))],
        out_specs=[whole((rows, D)), pl.BlockSpec((rows, D), lambda j: (0, j))],
        compiler_params=pltpu.CompilerParams(vmem_limit_bytes=VMEM_LIMIT),
    )(tokens, scale, shift, w_qkv)


def tail_kernel(shared, grad_ref, hidden_ref, w_ref, tok_ref, mid_ref, scale_ref, *refs):
    p = pl.program_id(0)
    rows = tok_ref.shape[0]
    if shared:
        table_ref, results, gtok_ref, gscale_ref, gshift_ref, factor_group, factor_all, back, gw, summed, factors, *refs = refs
        lands, sems = refs[:30], refs[30:]
        me, links = place(), Links(*sems)
        schedule = []
        for i in range(6):
            half = HALVES[i % 2]
            unit = reduce_turns(
                links, me, gw.at[i // 2], half.start, summed.at[i // 2, half], results.at[i // 2, half], lands[5 * i : 5 * i + 5]
            )
            schedule += [(2 * (i // 2) + 1 + i % 2 + k, turn) for k, turn in enumerate(unit)]
        turns = placed(schedule)
        host = Host(links, {h: t for h, t in turns.items() if h < 12}, 6, 2)
        rest = [turns[h] for h in sorted(turns) if h >= 12]
        spread = factors_turns(links, me, factors, factor_group, factor_all)
    else:
        gw, gtok_ref, gscale_ref, gshift_ref, back = refs
        host = Idle()

    host.turn(0)

    @pl.when(p < 3)
    def _():
        for r in range(D // 256):
            value = tn(hidden_ref[:, r * 256 : r * 256 + 256], grad_ref[0]).astype(jnp.bfloat16)
            for half in (0, 1):
                gw[p if shared else 0, 2 * r + half] = value[half * 128 : half * 128 + 128]

    def way_back(first):
        for r in range(2):
            here = pl.ds(first + r * (rows // 4), rows // 4)
            part = nt(grad_ref[0, here, :], w_ref[...])

            @pl.when(p == 3)
            def _():
                back[here, :] = part

            @pl.when(p > 3)
            def _():
                back[here, :] += part

    pl.when(p >= 3)(functools.partial(way_back, 0))
    host.turn(1)
    pl.when(p >= 3)(functools.partial(way_back, rows // 2))

    @pl.when(p == pl.num_programs(0) - 1)
    def _():
        def unit(u):
            at = pl.ds(pl.multiple_of(u * UNIT, UNIT), UNIT)
            normed, inverse = normalize(tok_ref[at, :].astype(jnp.float32))
            grad = back[at, :]
            gshift_ref[pl.ds(u, 1), :] = jnp.sum(grad, axis=0, keepdims=True)
            gscale_ref[pl.ds(u, 1), :] = jnp.sum(grad * normed, axis=0, keepdims=True)
            gtok_ref[at, :] = mid_ref[at, :] + norm_back(grad * (1.0 + scale_ref[pl.ds(u, 1), :]), normed, inverse)

        loop(rows // UNIT, unit)
        if shared:
            table = table_ref[...].astype(jnp.bfloat16)
            for i, ref in enumerate((gscale_ref, gshift_ref)):
                whole, sums = ref[...], None
                for _ in range(3):
                    part = whole.astype(jnp.bfloat16)
                    whole = whole - part.astype(jnp.float32)
                    sums = nn(table, part) if sums is None else sums + nn(table, part)
                factors[:, i * D : (i + 1) * D] = sums.astype(jnp.bfloat16)
            for i in range(max(len(rest), len(spread))):
                if i < len(spread):
                    spread[i]()
                if i < len(rest):
                    run(rest[i])

    host.finish()


def project_back(grad_proj, hidden, w_qkv, tokens, grad_mid, scale, table=None):
    rows = tokens.shape[0]
    once = lambda shape: pl.BlockSpec(shape, lambda p: (0, 0), pipeline_mode=pl.Buffered(1))
    units, whole = once((rows // UNIT, D)), once((rows, D))
    f32, b16 = jnp.float32, jnp.bfloat16
    block = pl.BlockSpec((1, rows, D), lambda p: (lax.rem(p, 3), 0, 0))
    inputs = [
        (grad_proj, block), (hidden, whole), (w_qkv, pl.BlockSpec((D, D), lambda p: (0, jnp.maximum(p - 3, 0)))), (tokens, whole), (grad_mid, whole), (scale, units),
    ]
    outputs = [((rows, D), f32, whole), ((rows // UNIT, D), f32, units), ((rows // UNIT, D), f32, units)]
    scratch = [pltpu.VMEM((rows, D), f32)]
    shared = table is not None
    if shared:
        slots = table.shape[0]
        inputs += [(table, once(table.shape))]
        outputs = [((3, 128, D), b16, ANY)] + outputs
        outputs += [((4 * slots, 2 * D), b16, ANY), ((32 * slots, 2 * D), b16, ANY)]
        scratch += [pltpu.VMEM((3, 8, 128, D), b16), pltpu.VMEM((3, 128, D), b16), pltpu.VMEM((slots, 2 * D), b16)] + [land for _ in range(6) for land in reduce_lands(64, far=False)]
        scratch += semaphores(6 * REDUCE_HOPS + FACTOR_HOPS, 6 * REDUCE_NEAR + FACTOR_NEAR)
    else:
        outputs = [((3, 8, 128, D), b16, pl.BlockSpec((1, 8, 128, D), lambda p: (jnp.minimum(p, 2), 0, 0, 0)))] + outputs
    return call(functools.partial(tail_kernel, shared), (6,), inputs, outputs, scratch)


def tuned(sizes):
    return sizes == (4, 8)


def blocks_of(columns):
    return columns.reshape(columns.shape[0], FF_BLOCKS, -1).transpose(1, 0, 2)


def local(
    sizes, tokens, lengths, buckets, w_mod, b_mod, w_qkv, w_out, b_out, w_up, b_up, w_down, b_down, cotangent,
):
    rows, slots, n = tokens.shape[0], lengths.shape[1], sizes[1]
    own = tuned(sizes)
    segment, live, unit_table = layout(lengths[0], rows)
    feats = time_features(buckets[0]).astype(jnp.bfloat16)
    whole = lambda array: lax.all_gather(array, "fsdp", axis=0, tiled=True)
    if own:
        packed = jnp.concatenate([b_mod, b_out, b_up, b_down]).reshape(-1, 128)
        packed = jnp.pad(packed, ((0, 16 - packed.shape[0]), (0, 0)))
        by_owner = feats.reshape(slots, n, 128).transpose(1, 0, 2)
        small = jnp.concatenate([jnp.broadcast_to(packed, (n, 16, 128)), by_owner], axis=1)
        small_all, (full_mod, full_qkv) = gather_all(small, (w_mod, w_qkv))
        of_group = lax.dynamic_slice(small_all, (lax.axis_index("dp") * n, 0, 0), (n, 16, 128))
        full_bmod, full_bout, full_bdown = of_group[:, :4].reshape(-1), of_group[:, 4].reshape(1, -1), of_group[:, 9].reshape(1, -1)
        full_bup = of_group[:, 5:9].transpose(1, 0, 2).reshape(FF_BLOCKS, 1, -1)
        every_feats = small_all[:, 16:].reshape(sizes[0], n, slots, 128).transpose(1, 0, 2, 3).reshape(-1, 128)
    else:
        full_mod, full_qkv, full_bmod, full_bout, full_bup, full_bdown = [whole(a) for a in (w_mod, w_qkv, b_mod, b_out, b_up, b_down)]
        full_bout, full_bdown, full_bup = full_bout[None], full_bdown[None], full_bup.reshape(FF_BLOCKS, 1, -1)
        every_feats = lax.all_gather(feats, ("dp", "fsdp"), axis=0, tiled=True)
        every_feats = lax.dynamic_slice(every_feats, (0, lax.axis_index("fsdp") * (D // n)), (every_feats.shape[0], D // n))
    modulation = jnp.dot(feats, full_mod, preferred_element_type=jnp.float32) + full_bmod
    per_unit = jnp.dot(unit_table, modulation, precision=HIGHEST)
    scale_one, shift_one, scale_two, shift_two = [per_unit[:, i * D : (i + 1) * D] for i in range(4)]
    live_units = jnp.broadcast_to(live[:, None], (rows // UNIT, D))
    hidden_attn, projected = project_in(tokens, scale_one, shift_one, full_qkv)
    query_lanes, key_lanes = attention_lanes(jnp.repeat(segment, UNIT), slots)
    if own:
        ups = w_up.reshape(-1, n, FF_BLOCKS, 128).transpose(2, 0, 1, 3).reshape(FF_BLOCKS, 1, -1, D)
        downs = w_down.reshape(FF_BLOCKS, 1, -1, D)
        pairs = jnp.concatenate([ups, downs], axis=1).reshape(2 * FF_BLOCKS, -1, D)
        attn_out, asked, weights = attend(projected, query_lanes, key_lanes, jnp.concatenate([w_out[None], pairs[: 2 * EARLY]]))
        late = pairs[2 * EARLY :]
    else:
        attn_out, asked = attend(projected, query_lanes, key_lanes)
        pairs = jnp.stack([blocks_of(whole(w_up)), whole(w_down).reshape(FF_BLOCKS, D, D)], axis=1)
        weights, late = jnp.concatenate([whole(w_out)[None], pairs.reshape(2 * FF_BLOCKS, D, D)]), None
    middle, hidden_mlp, grad_two, grad_b_down = before_mlp(
        attn_out, tokens, cotangent, weights, full_bout, scale_two, shift_two, live_units
    )
    forward, backward, grad_b_up, grad_pairs, *totals_early = feed_forward(hidden_mlp, grad_two, weights, full_bup, late)
    output, grad_mid, grad_attn, grad_w_out, grad_b_out, grad_scale_two, grad_shift_two = after_mlp(
        middle, forward, backward, cotangent, attn_out, weights, full_bdown, scale_two, live_units
    )

    def factors_of(first, second):
        return jnp.dot(unit_table.T, jnp.concatenate([first, second], axis=1), precision=HIGHEST).astype(jnp.bfloat16)

    mod_two = factors_of(grad_scale_two, grad_shift_two)
    if own:
        sums = [grad_b_out.reshape(n, 1, 128), grad_b_up.reshape(FF_BLOCKS, n, 128).transpose(1, 0, 2), grad_b_down.reshape(n, 1, 128)]
        small = jnp.pad(jnp.concatenate(sums, axis=1), ((0, 0), (0, 2), (0, 0)))
        grad_proj, totals, small_all, _, mod_two = attend_back(
            projected, key_lanes, asked, attn_out, grad_attn, (grad_pairs.reshape(-1, 8, 128, D), grad_w_out), small, mod_two
        )
        total = jnp.sum(small_all, axis=0)
        sum_bout, sum_bup, sum_bdown = total[0], total[1:5].reshape(-1), total[5]
    else:
        grad_proj = attend_back(projected, key_lanes, asked, attn_out, grad_attn)[0]
    qkv_grads, grad_tokens, grad_scale_one, grad_shift_one, *factors = project_back(
        grad_proj, hidden_attn, full_qkv, tokens, grad_mid, scale_one, unit_table.T if own else None
    )
    if own:
        mod_one = factors[1]
    else:
        mod_one = factors_of(grad_scale_one, grad_shift_one)
        mod_one, mod_two = [lax.all_gather(m, ("dp", "fsdp"), axis=0, tiled=True) for m in (mod_one, mod_two)]
    sum_mod = jnp.concatenate(
        [jnp.einsum("sd,sc->dc", every_feats, m, preferred_element_type=jnp.float32) for m in (mod_one, mod_two)], axis=1
    )
    position, share = lax.axis_index("fsdp"), 4 * D // n
    chosen = jnp.where(position < n // 2, mod_one, mod_two)
    sum_bmod = jnp.sum(
        lax.dynamic_slice(chosen, (0, position % (n // 2) * share), (chosen.shape[0], share)), axis=0, dtype=jnp.float32
    )
    if own:
        totals, qkv_grads = totals.astype(jnp.float32), qkv_grads.astype(jnp.float32)
        pairs = jnp.concatenate([totals_early[0].astype(jnp.float32), totals[:-1]]).reshape(FF_BLOCKS, 2, 128, D)
        sum_up = pairs[:, 0].reshape(FF_BLOCKS, -1, n, 128).transpose(1, 2, 0, 3).reshape(w_up.shape)
        sum_down = pairs[:, 1].reshape(w_down.shape)
        sum_out = totals[-1]
        sum_qkv = qkv_grads.transpose(1, 0, 2).reshape(w_qkv.shape)
    else:
        summed = lambda a: lax.psum(lax.psum_scatter(a, "fsdp", scatter_dimension=0, tiled=True), "dp").astype(jnp.float32)
        sum_up = summed(grad_pairs[:, 0].reshape(FF_BLOCKS, D, D).transpose(1, 0, 2).reshape(D, -1))
        sum_down = summed(grad_pairs[:, 1].reshape(-1, D))
        sum_out, sum_qkv = summed(grad_w_out.reshape(D, D)), summed(qkv_grads.reshape(3, D, D).transpose(1, 0, 2).reshape(D, -1))
        sum_bout, sum_bup, sum_bdown = [summed(a.reshape(-1)) for a in (grad_b_out, grad_b_up, grad_b_down)]
    return output, grad_tokens, sum_mod, sum_bmod, sum_qkv, sum_out, sum_bout, sum_up, sum_bup, sum_down, sum_bdown


def solution(mesh):
    sizes = (mesh.shape["dp"], mesh.shape["fsdp"])
    rows, cut_rows, vector = P(("dp", "fsdp"), None), P("fsdp", None), P("fsdp")
    return jax.shard_map(
        functools.partial(local, sizes),
        mesh=mesh,
        in_specs=(rows, rows, rows, cut_rows, vector, cut_rows, cut_rows, vector, cut_rows, vector, cut_rows, vector, rows),
        out_specs=(rows, rows, cut_rows, vector, cut_rows, cut_rows, vector, cut_rows, vector, cut_rows, vector),
        check_vma=False,
    )
```

```python
import functools
import math

import jax
import jax.numpy as jnp
from jax import lax
from jax.experimental import pallas as pl
from jax.experimental.pallas import tpu as pltpu
from jax.sharding import PartitionSpec as P

D = 1024
HEADS = 16
HEAD_DIM = 64
EPSILON = 1e-05
UNIT = 64
ROWS = 512
ATTENTION_ROWS = 512
FF_BLOCKS = 4
EARLY = 2
LSE_LANE = 24
ATTEND_GATHER = (3, (0, 4, 8, 12, 15))
MLP_GATHER = (3, (0, 5, 10, 15, 18))
MLP_REDUCE = (20, 4, (0, 2, 6, 11, 16, 19, 21))
BACK_REDUCE = (2.6, (0, 2, 5, 8, 11, 13, 15))
BACK_FACTORS = (1, 4, 8, 12, 16, 19)
TAIL_REDUCE = (0, 2, 5, 9, 13, 16, 18)
VMEM_LIMIT = 62 * 2**20
HIGHEST = lax.Precision.HIGHEST
MESH = pl.DeviceIdType.MESH


def layout(lengths, tok_rows):
    slots = lengths.shape[0]
    upto = jnp.arange(slots)[:, None] <= jnp.arange(slots)[None, :]
    seq_ends = jnp.sum(jnp.where(upto, lengths[:, None], 0), axis=0, dtype=jnp.int32)
    position = jnp.arange(0, tok_rows, UNIT, dtype=jnp.int32)
    segment = jnp.sum((position[:, None] >= seq_ends[None, :]).astype(jnp.int32), axis=1, dtype=jnp.int32)
    unit_table = (segment[:, None] == jnp.arange(slots, dtype=jnp.int32)[None, :]).astype(jnp.float32)
    return segment, (segment < slots).astype(jnp.float32), unit_table


def time_features(buckets):
    half_width = D // 2
    frequency = jnp.exp(-math.log(10000.0) * jnp.arange(half_width, dtype=jnp.float32) / half_width)
    angles = buckets.astype(jnp.float32)[:, None] * frequency[None, :]
    return jnp.concatenate([jnp.sin(angles), jnp.cos(angles)], axis=1)


def place():
    dp, fsdp = lax.axis_index("dp"), lax.axis_index("fsdp")
    return dp // 2, dp % 2, fsdp // 2, fsdp % 2


def device(x, core, z, y):
    return (x * 2 + core, z * 2 + y)


class Hop:
    def __init__(self, links, src, dst, target):
        self.links, self.src, self.dst, self.target, self.gone = links, src, dst, target, False
        self.slot = links.used
        links.used += 1
        links.hops.append(self)

    def made(self):
        return pltpu.make_async_remote_copy(
            src_ref=self.src(),
            dst_ref=self.dst(),
            send_sem=self.links.send_sems.at[self.slot],
            recv_sem=self.links.recv_sems.at[self.slot],
            device_id=self.target(),
            device_id_type=MESH,
        )

    def start(self):
        self.made().start()

    def arrived(self):
        self.made().wait_recv()

    def left(self):
        self.gone = True
        self.made().wait_send()


class Near:
    def __init__(self, links, src, dst):
        self.links, self.src, self.dst = links, src, dst
        self.slot = links.used_near
        links.used_near += 1

    def made(self):
        return pltpu.make_async_copy(self.src(), self.dst(), self.links.near_sems.at[self.slot])

    def start(self):
        self.made().start()

    def arrived(self):
        self.made().wait()


class Links:
    def __init__(self, send_sems, recv_sems, near_sems):
        self.send_sems, self.recv_sems, self.near_sems = send_sems, recv_sems, near_sems
        self.used, self.used_near, self.hops, self.ends = 0, 0, [], []

    def drain(self):
        for hop in self.hops:
            if not hop.gone:
                hop.left()
        for end in self.ends:
            end()


def lanes(at, size):
    return pl.ds(pl.multiple_of(at, 128), size)


def lines(at, size):
    return pl.ds(pl.multiple_of(at, 16), size)


HALVES = (pl.ds(0, 64), pl.ds(64, 64))


def gather_turns(links, me, shard, whole, outer, at=None):
    x, core, z, y = me
    rows, width = shard.shape
    half = width // 2
    inner = half - 2 * outer
    own = lanes(core * half + x * outer, outer + inner)
    crossing = lanes(core * half + x * (outer + inner), outer)
    full = lanes(core * half, half)

    def place_of(index):
        return lines(index * rows, rows) if at is None else lines(index * 128 + at, rows)

    mine = place_of(z * 2 + y)
    blocks = {}
    for k in range(4):
        source = ((z - k + 4) % 4) * 2
        blocks["z", k], blocks["y", k] = place_of(source + y), place_of(source + 1 - y)
    to_z = {k: device(x, core, (z + k) % 4, y) for k in (1, 2, 3)}
    to_y, to_x, to_core = device(x, core, z, 1 - y), device(1 - x, core, z, y), device(x, 1 - core, z, y)

    def from_shard(target):
        return Hop(links, lambda: shard.at[:, own], lambda: whole.at[mine, own], lambda: target)

    def pass_on(way, k, columns, target):
        def ref():
            return whole.at[blocks[way, k], columns]

        return Hop(links, ref, ref, lambda: target)

    keep = Near(links, lambda: shard, lambda: whole.at[mine, :])
    along_z = {k: from_shard(to_z[k]) for k in (1, 2, 3)}
    along_y = {0: from_shard(to_y)}
    for k in (1, 2, 3):
        along_y[k] = pass_on("z", k, own, to_y)
    order = [("z", 1), ("y", 0), ("z", 2), ("y", 1), ("z", 3), ("y", 2), ("y", 3)]
    crossed = [pass_on(way, k, crossing, to_x) for way, k in order] if outer else None
    handed = [pass_on(way, k, full, to_core) for way, k in order]

    def first():
        for k in (1, 2, 3):
            along_z[k].start()
        along_y[0].start()
        keep.start()

    def arrive(j):
        way, k = order[j]
        (along_z if way == "z" else along_y)[k].arrived()
        if way == "z":
            along_y[k].start()
        (crossed if outer else handed)[j].start()

    def hand_on(j):
        if outer:
            crossed[j].arrived()
            handed[j].start()

    def last():
        for hop in handed:
            hop.arrived()
        keep.arrived()

    return [
        first,
        lambda: [arrive(j) for j in (1, 0, 2, 4)],
        lambda: [arrive(j) for j in (3, 5, 6)] + [hand_on(j) for j in (1, 0, 2, 4)],
        lambda: [hand_on(j) for j in (3, 5, 6)],
        last,
    ]


GATHER_HOPS, GATHER_NEAR = 3 + 4 + 7 + 7, 1


def reduce_lands(rows, width=1024, far=True):
    half = width // 2
    outer = half // 4
    shapes = [
        (4, 2, rows, half), (4, 2, rows, outer), (4, rows, half - outer), (3, rows, half - outer), (rows, half - outer),
    ]
    if far:
        shapes.append((4, 2, rows, half))
    return [pltpu.VMEM(s, jnp.bfloat16) for s in shapes]


def reduce_turns(links, me, local, at, result, out, lands):
    x, core, z, y = me
    total, from_x, from_y, from_z, from_last = lands[:5]
    far = lands[5] if len(lands) > 5 else None
    rows, width = result.shape
    half = width // 2
    outer = half // 4
    wide = half - outer

    own, kept, given = lanes(x * outer, wide), lanes(x * wide, outer), lanes((1 - x) * wide, outer)
    sides, here = {True: lanes(core * half, half), False: lanes((1 - core) * half, half)}, pl.ds(at, rows)
    owners_of = [pl.ds(((z + t + 1) % 4) * 2, 2) for t in range(4)]
    other = 1 - y
    at_core, at_x, at_y = device(x, 1 - core, z, y), device(1 - x, core, z, y), device(x, core, z, other)
    at_z = [device(x, core, (z + t + 1) % 4, y) for t in range(3)]

    def owners(t, ours):
        return local.at[owners_of[t], here, sides[ours]]

    turns4 = range(4)
    load = [Near(links, lambda t=t: owners(t, True), lambda t=t: far.at[t]) for t in turns4] if far is not None else []
    to_core = [Hop(links, lambda t=t: owners(t, False), lambda t=t: total.at[t], lambda: at_core) for t in turns4]
    to_x = [Hop(links, lambda t=t: total.at[t, :, :, given], lambda t=t: from_x.at[t], lambda: at_x) for t in turns4]
    to_y = [Hop(links, lambda t=t: total.at[t, other, :, own], lambda t=t: from_y.at[t], lambda: at_y) for t in turns4]
    to_z = [Hop(links, lambda t=t: total.at[t, y, :, own], lambda t=t: from_z.at[t], lambda t=t: at_z[t]) for t in range(3)]
    to_last = Hop(links, lambda: total.at[3, y, :, own], lambda: from_last, lambda: at_x)
    mine = lambda: result.at[:, sides[True]]
    to_final = Hop(links, mine, mine, lambda: at_core)
    store = Near(links, lambda: result, lambda: out)
    links.ends.append(store.arrived)

    def add(index, landed):
        total[index] = (total[index].astype(jnp.float32) + landed.astype(jnp.float32)).astype(total.dtype)

    def first():
        for t in turns4:
            to_core[t].start()
        for near in load:
            near.start()

    def core_turn():
        for t in turns4:
            to_core[t].arrived()
            if far is None:
                to_core[t].left()
                add(t, owners(t, True)[...])
            else:
                load[t].arrived()
                add(t, far[t])
            to_x[t].start()

    def x_turn():
        for t in turns4:
            to_x[t].arrived()
            add((t, slice(None), slice(None), kept), from_x[t])
            to_y[t].start()

    def y_turn():
        for t in range(3):
            to_y[t].arrived()
            add((t, y, slice(None), own), from_y[t])
            to_z[t].start()

    def z_turn():
        to_y[3].arrived()
        everything = total[3, y, :, own].astype(jnp.float32) + from_y[3].astype(jnp.float32)
        for t in range(3):
            to_z[t].arrived()
            everything = everything + from_z[t].astype(jnp.float32)
        total[3, y, :, own] = everything.astype(total.dtype)
        to_last.start()

    def last_turn():
        to_last.arrived()
        middle = half - 2 * outer
        shared = total[3, y, :, lanes(outer, middle)].astype(jnp.float32) + from_last[:, lanes(x * outer, middle)].astype(jnp.float32)
        result[:, lanes(core * half + outer, middle)] = shared.astype(result.dtype)
        result[:, lanes(core * half + x * wide, outer)] = total[3, y, :, kept]
        result[:, lanes(core * half + (1 - x) * wide, outer)] = from_last[:, lanes((1 - x) * middle, outer)]
        to_final.start()

    def end():
        to_final.arrived()
        store.start()

    return [first, core_turn, x_turn, y_turn, z_turn, last_turn, end]


REDUCE_HOPS, REDUCE_NEAR = 4 + 4 + 4 + 3 + 2, 5


def merged(units, every, lag=1):
    turns = []
    for i, unit in enumerate(units):
        for k, turn in enumerate(unit):
            at = i * every + k * lag
            turns += [[] for _ in range(at + 1 - len(turns))]
            turns[at].insert(0, turn)
    return turns


def run(turn):
    for action in turn:
        action()


def semaphores(hops, near):
    return [pltpu.SemaphoreType.DMA((hops,)), pltpu.SemaphoreType.DMA((hops,)), pltpu.SemaphoreType.DMA((max(near, 1),))]


def exchange_small(small, small_all, links, me):
    x, core, z, y = me
    number = (x * 2 + core) * 8 + z * 2 + y
    keep = Near(links, lambda: small.at[z * 2 + y], lambda: small_all.at[number])
    few = [
        Hop(
            links,
            lambda k=k: small.at[(number + k) % 8],
            lambda: small_all.at[number],
            lambda k=k: (((number + k) % 32) // 8, (number + k) % 8),
        )
        for k in range(1, 32)
    ]

    def begin():
        keep.start()
        for hop in few:
            hop.start()

    def end():
        keep.arrived()
        for hop in few:
            hop.arrived()

    return begin, end


def factors_turns(links, me, factors, group, whole):
    x, core, z, y = me
    slots = factors.shape[0]
    mine = lambda: group.at[lines((x * 2 + core) * slots, slots), :]
    keep = Near(links, lambda: factors, mine)
    peers = [
        Hop(links, lambda: factors, mine, lambda i=i, j=j: device((x + i) % 2, (core + j) % 2, z, y)) for i, j in ((0, 1), (1, 0), (1, 1))
    ]

    def first():
        keep.start()
        for hop in peers:
            hop.start()

    def second():
        keep.arrived()
        for hop in peers:
            hop.arrived()

    turns = gather_turns(links, me, group, whole, 256)
    return [first, lambda: (second(), turns[0]())] + turns[1:]


FACTOR_HOPS, FACTOR_NEAR = 3 + GATHER_HOPS, 1 + GATHER_NEAR


def nt(a, b):
    return lax.dot_general(a, b, (((1,), (1,)), ((), ())), preferred_element_type=jnp.float32)


def tn(a, b):
    return lax.dot_general(a, b, (((0,), (0,)), ((), ())), preferred_element_type=jnp.float32)


def nn(a, b):
    return jnp.dot(a, b, preferred_element_type=jnp.float32)


def normalize(values):
    centred = values - jnp.mean(values, axis=1, keepdims=True)
    inverse = lax.rsqrt(jnp.mean(centred * centred, axis=1, keepdims=True) + EPSILON)
    return (centred * inverse, inverse)


def norm_back(grad_normed, normed, inverse):
    first_mean = jnp.mean(grad_normed, axis=1, keepdims=True)
    second_mean = jnp.mean(grad_normed * normed, axis=1, keepdims=True)
    return inverse * (grad_normed - first_mean - normed * second_mean)


def gelu_both(u):
    c = math.sqrt(2 / math.pi)
    square = u * u
    t = jnp.tanh(u * (c + (c * 0.044715) * square))
    half = 0.5 + 0.5 * t
    value = u * half
    return value, half + value * (1.0 - t) * (c + (3 * c * 0.044715) * square)


def loop(count, body):
    def step(i, carry):
        body(i)
        return carry

    lax.fori_loop(0, count, step, 0)


def attention_lanes(segment, slots):
    lane = jnp.arange(128) % 64
    hot = segment[:, None] == lane[None, :]
    listed = lane[None, :] <= slots
    query_lanes = (hot & listed).astype(jnp.bfloat16)
    ones = (lane >= LSE_LANE) & (lane < LSE_LANE + 3)
    key_lanes = jnp.where(listed & ~hot, -1e30, jnp.where(ones[None, :], 1.0, 0.0)).astype(jnp.bfloat16)
    return query_lanes, key_lanes


class Host:
    def __init__(self, links, turns, steps, per_step):
        self.links, self.turns, self.steps, self.per_step = links, turns, steps, per_step
        self.step = pl.program_id(0)

    def turn(self, index):
        for hook, turn in sorted(self.turns.items()):
            if hook < self.steps * self.per_step and hook % self.per_step == index:
                pl.when(self.step == hook // self.per_step)(functools.partial(run, turn))

    def finish(self):
        @pl.when(self.step == self.steps - 1)
        def _():
            for hook, turn in sorted(self.turns.items()):
                if hook >= self.steps * self.per_step:
                    run(turn)
            self.links.drain()


def timed(units, every, lags, first=0):
    return [(int(first + every * i) + lag, turn) for i, unit in enumerate(units) for lag, turn in zip(lags, unit)]


def placed(schedule):
    turns = {}
    for hook, turn in schedule:
        turns.setdefault(hook, []).insert(0, turn)
    return turns


class Idle:
    def turn(self, index):
        pass

    def finish(self):
        pass


ANY = pl.BlockSpec(memory_space=pl.ANY)
VMEM = pl.BlockSpec(memory_space=pltpu.VMEM)


def call(kernel, grid, inputs, outputs, scratch=()):
    made = pl.pallas_call(
        kernel,
        grid=grid,
        out_shape=[jax.ShapeDtypeStruct(shape, kind) for shape, kind, _ in outputs],
        in_specs=[spec for _, spec in inputs],
        out_specs=[spec for _, _, spec in outputs],
        scratch_shapes=list(scratch),
        compiler_params=pltpu.CompilerParams(has_side_effects=True, vmem_limit_bytes=VMEM_LIMIT),
    )
    return made(*[array for array, _ in inputs])


def exact(table, values):
    sums = None
    for _ in range(3):
        part = values.astype(jnp.bfloat16)
        values = values - part.astype(jnp.float32)
        sums = nn(table, part) if sums is None else sums + nn(table, part)
    return sums


def modulation_turns(links, me, parts, from_y, from_z, columns):
    x, core, z, y = me
    block = lambda t, side: parts.at[((z + t + 1) % 4) * 2 + side, :, columns]
    to_y = [Hop(links, lambda t=t: block(t, 1 - y), lambda t=t: from_y.at[t, :, columns], lambda: device(x, core, z, 1 - y)) for t in range(4)]
    to_z = [
        Hop(links, lambda t=t: block(t, y), lambda t=t: from_z.at[t, :, columns], lambda t=t: device(x, core, (z + t + 1) % 4, y))
        for t in range(3)
    ]

    def begin():
        for hop in to_y:
            hop.start()

    def middle():
        for t in range(3):
            to_y[t].arrived()
            block(t, y)[...] = (block(t, y)[...].astype(jnp.float32) + from_y[t, :, columns].astype(jnp.float32)).astype(parts.dtype)
            to_z[t].start()

    def end():
        to_y[3].arrived()
        total = block(3, y)[...].astype(jnp.float32) + from_y[3, :, columns].astype(jnp.float32)
        for t in range(3):
            to_z[t].arrived()
            total = total + from_z[t, :, columns].astype(jnp.float32)
        return total

    return begin, middle, end


def first_kernel(small, wmod_ref, wqkv, tok_ref, table_ref, small_all, wholes, hidden_ref, out_ref, unit_ref, landed, held, normed, *refs):
    parts, from_y, from_z, sems = refs[:2], refs[2:4], refs[4:6], refs[6:]
    me, links = place(), Links(*sems)
    x, core, z, y = me
    group = (x * 2 + core) * 8
    rows = tok_ref.shape[0]
    begin, end = exchange_small(small, landed, links, me)
    units = [
        gather_turns(links, me, wqkv.at[half, pl.ds(i * D, D)], held.at[i], 128 if half.start else 256, half.start)
        for i in range(3)
        for half in HALVES
    ]
    gather = merged(units, 1)
    halves = [modulation_turns(links, me, parts[i], from_y[i], from_z[i], pl.ds(0, 2 * D)) for i in (0, 1)]
    keep = [Near(links, lambda i=i: held.at[i], lambda i=i: wholes.at[i]) for i in range(3)]
    save = Near(links, lambda: landed, lambda: small_all)
    links.ends += [near.arrived for near in keep + [save]]

    def norm(first):
        def unit(u):
            at = pl.ds(pl.multiple_of(u * UNIT, UNIT), UNIT)
            normed[at, :] = normalize(tok_ref[at, :].astype(jnp.float32))[0]

        loop(rows // UNIT // 2, lambda i: unit(first + i))

    def settle(half):
        total = halves[half][2]()
        table = table_ref[...].astype(jnp.bfloat16)
        for f in range(4):
            bias = landed[group + 4 * half + f, :16, :].astype(jnp.float32)
            for i in range(4):
                at = (4 * f + i) * 128
                value = total[:, at : at + 128] + bias[i : i + 1, :]
                unit_ref[:, 2 * half * D + at : 2 * half * D + at + 128] = exact(table, value)

    def project(i):
        def block(r):
            here = pl.ds(pl.multiple_of(r * 256, 256), 256)
            out_ref[here, i * D : (i + 1) * D] = nn(hidden_ref[here, :], held[i]).astype(jnp.bfloat16)

        loop(rows // 256, block)

    begin()
    run(gather[0])
    norm(0)
    run(gather[1])
    norm(rows // UNIT // 2)
    end()
    save.start()
    for f in range(8):
        part = nn(landed[group + f, 16:, :], wmod_ref[...])
        for half in (0, 1):
            parts[half][f] = part[:, half * 2 * D : (half + 1) * 2 * D].astype(parts[half].dtype)
    halves[0][0]()
    run(gather[2])
    halves[0][1]()
    halves[1][0]()
    run(gather[3])
    settle(0)
    halves[1][1]()

    def shape(u):
        at = pl.ds(pl.multiple_of(u * UNIT, UNIT), UNIT)
        hidden_ref[at, :] = (normed[at, :] * (1.0 + unit_ref[pl.ds(u, 1), :D]) + unit_ref[pl.ds(u, 1), D : 2 * D]).astype(jnp.bfloat16)

    run(gather[4])
    loop(rows // UNIT, shape)
    run(gather[5])
    keep[0].start()
    project(0)
    run(gather[6])
    settle(1)
    run(gather[7])
    keep[1].start()
    project(1)
    run(gather[8])
    run(gather[9])
    keep[2].start()
    project(2)
    links.drain()


def first_all(small, w_mod, w_qkv, tokens, table):
    rows, (units, slots) = tokens.shape[0], table.shape
    b16, f32 = jnp.bfloat16, jnp.float32
    hops = 31 + 6 * GATHER_HOPS + 14
    return call(
        first_kernel,
        (),
        [(small, ANY), (w_mod, VMEM), (w_qkv, ANY), (tokens, VMEM), (table, VMEM)],
        [
            ((32,) + small.shape[1:], b16, ANY), ((3, D, D), b16, ANY), ((rows, D), b16, VMEM), ((rows, 3 * D), b16, VMEM),
            ((units, 4 * D), f32, VMEM),
        ],
        [
            pltpu.VMEM((32,) + small.shape[1:], b16), pltpu.VMEM((3, D, D), b16), pltpu.VMEM((rows, D), f32),
        ]
        + [pltpu.VMEM((count, slots, 2 * D), kind) for count in (8, 4, 3) for kind in (f32, b16)]
        + semaphores(hops, 1 + 6 * GATHER_NEAR + 4),
    )


def attend_kernel(shared, q_ref, k_ref, v_ref, ql_ref, kl_ref, *refs):
    if shared:
        shards, out_ref, qa_ref, wholes, *sems = refs
        me, links = place(), Links(*sems)
        units = [
            gather_turns(links, me, shards.at[i, half], wholes.at[i], 128 if half.start else 256, half.start)
            for i in range(shared)
            for half in HALVES
        ]
        host = Host(links, placed(timed(units, *ATTEND_GATHER)), D // 128, 4)
    else:
        (out_ref, qa_ref), host = refs, Idle()
    rows = q_ref.shape[0]
    block = min(ATTENTION_ROWS, rows)
    low = lax.broadcasted_iota(jnp.int32, (1, 128), 1) < HEAD_DIM
    lane = lax.broadcasted_iota(jnp.int32, (1, 128), 1) % HEAD_DIM
    keys, vals = [], []
    for own in (low, ~low):
        keys.append(jnp.where(own, k_ref[...], kl_ref[...]))
        vals.append(jnp.where(own, v_ref[...], jnp.bfloat16(1)))
    for at, first in enumerate(range(0, rows, block)):
        here = pl.ds(first, block)
        queries = q_ref[here, :] * jnp.bfloat16(HEAD_DIM**-0.5)
        mixed = []
        for head, own in enumerate((low, ~low)):
            host.turn(2 * at + head)
            asked = jnp.where(own, queries, ql_ref[here, :])
            scores = nt(asked, keys[head])
            top = jnp.max(scores, axis=1, keepdims=True)
            weight = jnp.exp(scores - top).astype(jnp.bfloat16)
            both = nn(weight, vals[head])
            mixed.append(both)
            log_total = -(top + jnp.log(both))
            first_part = log_total.astype(jnp.bfloat16)
            rest = log_total - first_part.astype(jnp.float32)
            second = rest.astype(jnp.bfloat16)
            third = (rest - second.astype(jnp.float32)).astype(jnp.bfloat16)
            for i, part in enumerate((first_part, second, third)):
                asked = jnp.where(~own & (lane == LSE_LANE + i), part, asked)
            qa_ref[head, here, :] = asked
        total = pltpu.roll(jnp.where(low, mixed[1], mixed[0]), HEAD_DIM, 1)
        out_ref[here, :] = (jnp.where(low, mixed[0], mixed[1]) / total).astype(jnp.bfloat16)
    host.finish()


def attend(projected, query_lanes, key_lanes, shards=None):
    rows, pairs = projected.shape[0], D // 128
    spec = lambda shift: pl.BlockSpec((rows, 128), lambda i: (0, i + shift))
    same = pl.BlockSpec((rows, 128), lambda i: (0, 0))
    inputs = [(projected, spec(0)), (projected, spec(pairs)), (projected, spec(2 * pairs)), (query_lanes, same), (key_lanes, same)]
    outputs = [((rows, D), jnp.bfloat16, spec(0)), ((HEADS, rows, 128), jnp.bfloat16, pl.BlockSpec((2, rows, 128), lambda i: (i, 0, 0)))]
    if shards is None:
        return call(functools.partial(attend_kernel, 0), (pairs,), inputs, outputs)
    units, depth, width = shards.shape
    return call(
        functools.partial(attend_kernel, units),
        (pairs,),
        inputs + [(shards, ANY)],
        outputs + [((units, 8 * depth, width), shards.dtype, ANY)],
        semaphores(2 * GATHER_HOPS * units, 2 * GATHER_NEAR * units),
    )


def attend_back_kernel(counts, k_ref, v_ref, kl_ref, qa_ref, out_ref, go_ref, *refs):
    units = sum(counts)
    if units:
        groups, refs = refs[: len(counts)], refs[len(counts) :]
        small, factors, grad_ref, results, small_all, factor_group, factor_all, kt_ref, dqt_ref, *refs = refs
        summed, lands, sems = refs[0], refs[1 : 1 + 12 * units], refs[1 + 12 * units :]
        me, links = place(), Links(*sems)
        begin, end = exchange_small(small, small_all, links, me)
        locals_ = [group.at[i] for group, count in zip(groups, counts) for i in range(count)]
        plans = [
            reduce_turns(
                links, me, locals_[i // 2], i % 2 * 64, summed.at[i // 2, HALVES[i % 2]], results.at[i // 2, HALVES[i % 2]], lands[6 * i : 6 * i + 6]
            )
            for i in range(2 * units)
        ]
        schedule = list(zip(BACK_FACTORS, factors_turns(links, me, factors, factor_group, factor_all)))
        schedule = [(0, begin)] + schedule + timed(plans, *BACK_REDUCE)
        links.ends += [end]
        host = Host(links, placed(schedule), D // 128, 4)
    else:
        (grad_ref, kt_ref, dqt_ref), host = refs, Idle()
    rows = k_ref.shape[0]
    block = min(ATTENTION_ROWS, rows)
    low = lax.broadcasted_iota(jnp.int32, (1, 128), 1) < HEAD_DIM
    grads = go_ref[...]
    product = pltpu.roll(-(grads.astype(jnp.float32) * out_ref[...].astype(jnp.float32)), HEAD_DIM, 1).astype(jnp.bfloat16)
    kt_ref[...] = k_ref[...].astype(jnp.float32).T.astype(jnp.bfloat16)
    given = [jnp.where(own, grads, product) for own in (low, ~low)]
    for at, first in enumerate(range(0, rows, block)):
        here = pl.ds(first, block)
        dks, dvs = [], []
        for head, own in enumerate((low, ~low)):
            host.turn(2 * at + head)
            keys = jnp.where(own, k_ref[here, :], kl_ref[here, :])
            vals = jnp.where(own, v_ref[here, :], jnp.bfloat16(1))
            probs = jnp.exp(nt(keys, qa_ref[head]))
            slopes = nt(vals, given[head])
            moved = (probs * slopes).astype(jnp.bfloat16)
            dvs.append(nn(probs.astype(jnp.bfloat16), grads))
            dks.append(nn(moved, qa_ref[head]))
            part = nn(kt_ref[head * HEAD_DIM : (head + 1) * HEAD_DIM, here], moved)
            where = pl.ds(head * HEAD_DIM, HEAD_DIM)
            if first == 0:
                dqt_ref[where, :] = part
            else:
                dqt_ref[where, :] += part
        grad_ref[1, here, :] = jnp.where(low, dks[0], dks[1]).astype(jnp.bfloat16)
        grad_ref[2, here, :] = jnp.where(low, dvs[0], dvs[1]).astype(jnp.bfloat16)
    grad_ref[0] = (dqt_ref[...].T * HEAD_DIM**-0.5).astype(jnp.bfloat16)
    host.finish()


def attend_back(projected, key_lanes, asked, attn_out, grad_attn, groups=(), small=None, factors=None):
    rows, pairs = projected.shape[0], D // 128
    spec = lambda shift: pl.BlockSpec((rows, 128), lambda i: (0, i + shift))
    same = pl.BlockSpec((rows, 128), lambda i: (0, 0))
    two = pl.BlockSpec((2, rows, 128), lambda i: (i, 0, 0))
    inputs = [(projected, spec(pairs)), (projected, spec(2 * pairs)), (key_lanes, same), (asked, two), (attn_out, spec(0)), (grad_attn, spec(0))]
    outputs = [((3, rows, D), jnp.bfloat16, pl.BlockSpec((3, rows, 128), lambda i: (0, 0, i)))]
    scratch = [pltpu.VMEM((128, rows), jnp.bfloat16), pltpu.VMEM((128, rows), jnp.float32)]
    counts = [g.shape[0] for g in groups]
    units = sum(counts)
    if units:
        inputs += [(g, ANY) for g in groups] + [(small, ANY), (factors, ANY)]
        slots, width = factors.shape
        outputs += [((units, 128, D), jnp.bfloat16, ANY), ((32,) + small.shape[1:], small.dtype, ANY)]
        outputs += [((4 * slots, width), factors.dtype, ANY), ((32 * slots, width), factors.dtype, ANY)]
        scratch += [pltpu.VMEM((units, 128, D), jnp.bfloat16)] + [land for _ in range(2 * units) for land in reduce_lands(64)]
        scratch += semaphores(31 + FACTOR_HOPS + 2 * REDUCE_HOPS * units, 1 + FACTOR_NEAR + 2 * REDUCE_NEAR * units)
    return call(functools.partial(attend_back_kernel, counts), (pairs,), inputs, outputs, scratch)


def before_kernel(attn_ref, tok_ref, cot_ref, wout_ref, bout_ref, scale_ref, shift_ref, live_ref, middle_ref, hidden_ref, two_ref, gbdown_ref):
    r = pl.program_id(0)
    rows = tok_ref.shape[0]
    units = rows // UNIT

    @pl.when(r == 0)
    def _():
        gbdown_ref[...] = jnp.zeros_like(gbdown_ref)

    middle_ref[...] = nn(attn_ref[...], wout_ref[0]) + bout_ref[...].astype(jnp.float32)
    for i in range(units):
        u = r * units + i
        at = pl.ds(i * UNIT, UNIT)
        live = live_ref[pl.ds(u, 1), :]
        value = tok_ref[at, :].astype(jnp.float32) + live * middle_ref[at, :]
        middle_ref[at, :] = value
        normed, _ = normalize(value)
        hidden_ref[at, :] = (normed * (1.0 + scale_ref[pl.ds(u, 1), :]) + shift_ref[pl.ds(u, 1), :]).astype(jnp.bfloat16)
        grad = (live * cot_ref[at, :].astype(jnp.float32)).astype(jnp.bfloat16)
        two_ref[at, :] = grad
        gbdown_ref[...] += jnp.sum(grad.astype(jnp.float32), axis=0, keepdims=True)


def before_mlp(attn_out, tokens, cotangent, weights, b_out, scale, shift, live):
    rows = tokens.shape[0]
    block = pl.BlockSpec((256, D), lambda r: (r, 0))
    once = lambda shape: pl.BlockSpec(shape, lambda r: (0,) * len(shape))
    units = once((rows // UNIT, D))
    return call(
        before_kernel,
        (rows // 256,),
        [(attn_out, block), (tokens, block), (cotangent, block), (weights, once((1, D, D))), (b_out, once((1, D))), (scale, units), (shift, units), (live, units)],
        [((rows, D), jnp.float32, block), ((rows, D), jnp.bfloat16, block), ((rows, D), jnp.bfloat16, block), ((1, D), jnp.float32, once((1, D)))],
    )


def mlp_kernel(early, hidden, two, bup_ref, weights, *refs):
    j = pl.program_id(0)
    rows = hidden.shape[0]
    late = FF_BLOCKS - early
    if late:
        shards, acc, back, gbup_ref, grads_ref, results, act, pre, held, made, summed, *refs = refs
        lands, sems = refs[: 20 * early], refs[20 * early :]
    else:
        acc, back, gbup_ref, grads_ref, act, pre, held, made, *sems = refs
    slots = made.shape[0]
    me, links = place(), Links(*sems)
    fetch = [[Near(links, lambda b=b, w=w: weights.at[1 + 2 * b + w], lambda b=b, w=w: held.at[b, w]) for w in (0, 1)] for b in range(early)]
    store = [Near(links, lambda b=b: made.at[b % slots], lambda b=b: grads_ref.at[b - FF_BLOCKS + grads_ref.shape[0]]) for b in range(FF_BLOCKS)]
    kept_blocks = range(FF_BLOCKS - grads_ref.shape[0], FF_BLOCKS)
    if late:
        gathers, reduces = [], []
        for i in range(4 * late):
            b, w, half = early + i // 4, i // 2 % 2, HALVES[i % 2]
            gathers.append(gather_turns(links, me, shards.at[i // 2, half], held.at[b, w], 128 if i % 2 else 256, half.start))
        for i in range(4 * early):
            b, w, half = i // 4, i // 2 % 2, HALVES[i % 2]
            reduces.append(
                reduce_turns(
                    links, me, made.at[b % slots, w], half.start, summed.at[2 * b + w, half], results.at[2 * b + w, half], lands[5 * i : 5 * i + 5]
                )
            )
        first, every, lags = MLP_REDUCE
        schedule = timed(gathers, *MLP_GATHER) + timed(reduces, every, lags, first)
        host = Host(links, placed(schedule), FF_BLOCKS, 16)
    else:
        host = Idle()

    @pl.when(j == 0)
    def _():
        for pair in fetch:
            for near in pair:
                near.start()

    host.turn(0)
    for b in range(early):

        @pl.when(j == b)
        def _():
            for near in fetch[b]:
                near.arrived()

    gbup_ref[...] = jnp.zeros_like(gbup_ref)
    up, down = held.at[j, 0], held.at[j, 1]
    block = rows // 4
    for r in range(4):
        if r:
            host.turn(2 * r)
        here = pl.ds(r * block, block)
        value, slope = gelu_both(nn(hidden[here, :], up[...]) + bup_ref[0].astype(jnp.float32))
        value = value.astype(jnp.bfloat16)
        grad = (nt(two[here, :], down[...]) * slope).astype(jnp.bfloat16)
        act[here, :] = value
        pre[here, :] = grad
        gbup_ref[0] += jnp.sum(grad.astype(jnp.float32), axis=0, keepdims=True)
        host.turn(2 * r + 1)
        forward, backward = nn(value, down[...]), nt(grad, up[...])

        @pl.when(j == 0)
        def _():
            acc[here, :] = forward
            back[here, :] = backward

        @pl.when(j > 0)
        def _():
            acc[here, :] += forward
            back[here, :] += backward

    slot = lax.rem(j, slots)
    for r in range(4):
        here = pl.ds(r * 256, 256)
        for w, (left, right) in enumerate(((hidden, pre), (act, two))):
            host.turn(8 + 2 * r + w)
            value = tn(left[:, here], right[...]).astype(jnp.bfloat16)
            for half in (0, 1):
                made[slot, w, 2 * r + half] = value[half * 128 : half * 128 + 128]
    for b in kept_blocks:
        pl.when(j == b)(store[b].start)

    @pl.when(j == FF_BLOCKS - 1)
    def _():
        for b in kept_blocks:
            store[b].arrived()

    host.finish()


def feed_forward(hidden, two, weights, b_up, shards=None):
    rows = hidden.shape[0]
    once = lambda shape: pl.BlockSpec(shape, lambda j: (0, 0), pipeline_mode=pl.Buffered(1))
    whole = once((rows, D))
    row = pl.BlockSpec((1, 1, D), lambda j: (j, 0, 0))
    f32, b16 = jnp.float32, jnp.bfloat16
    early = FF_BLOCKS if shards is None else EARLY
    late = FF_BLOCKS - early
    kept = late or FF_BLOCKS
    inputs = [(hidden, whole), (two, whole), (b_up, row), (weights, ANY)]
    outputs = [((rows, D), f32, whole), ((rows, D), f32, whole), ((FF_BLOCKS, 1, D), f32, row), ((kept, 2, 8, 128, D), b16, ANY)]
    slots = 2 if late else FF_BLOCKS
    scratch = [
        pltpu.VMEM((rows, D), b16), pltpu.VMEM((rows, D), b16), pltpu.VMEM((FF_BLOCKS, 2, D, D), b16), pltpu.VMEM((slots, 2, 8, 128, D), b16),
    ]
    hops, near = 1, 2 * early + FF_BLOCKS
    if late:
        inputs += [(shards, ANY)]
        outputs += [((2 * early, 128, D), b16, ANY)]
        scratch += [pltpu.VMEM((2 * early, 128, D), b16)] + [land for _ in range(4 * early) for land in reduce_lands(64, far=False)]
        hops = 4 * late * GATHER_HOPS + 4 * early * REDUCE_HOPS
        near += 4 * late * GATHER_NEAR + 4 * early * REDUCE_NEAR
    return call(functools.partial(mlp_kernel, early), (FF_BLOCKS,), inputs, outputs, scratch + semaphores(hops, near))


def after_kernel(
    middle_ref, acc_ref, back_ref, cot_ref, attn_ref, wout_ref, bdown_ref, scale_ref, live_ref,
    out_ref, mid_grad_ref, attn_grad_ref, gout_ref, gbout_ref, gscale_ref, gshift_ref, one_ref, total_ref,
):
    r = pl.program_id(0)
    rows = cot_ref.shape[0]
    units = rows // UNIT

    @pl.when(r == 0)
    def _():
        gbout_ref[...] = jnp.zeros_like(gbout_ref)
        total_ref[...] = jnp.zeros_like(total_ref)

    for i in range(units):
        u = r * units + i
        at = pl.ds(i * UNIT, UNIT)
        live = live_ref[pl.ds(u, 1), :]
        value = middle_ref[at, :]
        out_ref[at, :] = (value + live * (acc_ref[at, :] + bdown_ref[...].astype(jnp.float32))).astype(jnp.bfloat16)
        normed, inverse = normalize(value)
        grad = back_ref[at, :]
        gshift_ref[pl.ds(u, 1), :] = jnp.sum(grad, axis=0, keepdims=True)
        gscale_ref[pl.ds(u, 1), :] = jnp.sum(grad * normed, axis=0, keepdims=True)
        passed = cot_ref[at, :].astype(jnp.float32) + norm_back(grad * (1.0 + scale_ref[pl.ds(u, 1), :]), normed, inverse)
        mid_grad_ref[at, :] = passed
        one = (live * passed).astype(jnp.bfloat16)
        one_ref[at, :] = one
        gbout_ref[...] += jnp.sum(one.astype(jnp.float32), axis=0, keepdims=True)
    attn_grad_ref[...] = nt(one_ref[...], wout_ref[0]).astype(jnp.bfloat16)
    total_ref[...] += tn(attn_ref[...], one_ref[...])

    @pl.when(r == pl.num_programs(0) - 1)
    def _():
        for i in range(8):
            gout_ref[0, i] = total_ref[i * 128 : i * 128 + 128, :].astype(jnp.bfloat16)


def after_mlp(middle, acc, back, cotangent, attn_out, weights, b_down, scale, live):
    rows = middle.shape[0]
    block = pl.BlockSpec((256, D), lambda r: (r, 0))
    once = lambda shape: pl.BlockSpec(shape, lambda r: (0,) * len(shape))
    units, row = once((rows // UNIT, D)), once((1, D))
    f32, b16 = jnp.float32, jnp.bfloat16
    return call(
        after_kernel,
        (rows // 256,),
        [
            (middle, block), (acc, block), (back, block), (cotangent, block), (attn_out, block), (weights, once((1, D, D))),
            (b_down, row), (scale, units), (live, units),
        ],
        [
            ((rows, D), b16, block), ((rows, D), f32, block), ((rows, D), b16, block), ((1, 8, 128, D), b16, once((1, 8, 128, D))), ((1, D), f32, row),
            ((rows // UNIT, D), f32, units), ((rows // UNIT, D), f32, units),
        ],
        [pltpu.VMEM((256, D), b16), pltpu.VMEM((D, D), f32)],
    )


def head_kernel(tok_ref, scale_ref, shift_ref, w_ref, hidden_ref, out_ref):
    rows = tok_ref.shape[0]

    @pl.when(pl.program_id(0) == 0)
    def _():
        def unit(u):
            at = pl.ds(pl.multiple_of(u * UNIT, UNIT), UNIT)
            normed, _ = normalize(tok_ref[at, :].astype(jnp.float32))
            hidden_ref[at, :] = (normed * (1.0 + scale_ref[pl.ds(u, 1), :]) + shift_ref[pl.ds(u, 1), :]).astype(jnp.bfloat16)

        loop(rows // UNIT, unit)

    def block(r):
        here = pl.ds(pl.multiple_of(r * ROWS, ROWS), ROWS)
        out_ref[here, :] = nn(hidden_ref[here, :], w_ref[0]).astype(jnp.bfloat16)

    loop(rows // ROWS, block)


def project_in(tokens, scale, shift, w_qkv):
    rows = tokens.shape[0]
    whole = lambda shape: pl.BlockSpec(shape, lambda j: (0, 0))
    return pl.pallas_call(
        head_kernel,
        grid=(3,),
        out_shape=[jax.ShapeDtypeStruct((rows, D), jnp.bfloat16), jax.ShapeDtypeStruct((rows, 3 * D), jnp.bfloat16)],
        in_specs=[whole((rows, D)), whole((rows // UNIT, D)), whole((rows // UNIT, D)), pl.BlockSpec((1, D, D), lambda j: (j, 0, 0))],
        out_specs=[whole((rows, D)), pl.BlockSpec((rows, D), lambda j: (0, j))],
        compiler_params=pltpu.CompilerParams(vmem_limit_bytes=VMEM_LIMIT),
    )(tokens, scale, shift, w_qkv)


def tail_kernel(shared, grad_ref, hidden_ref, w_ref, tok_ref, mid_ref, scale_ref, *refs):
    p = pl.program_id(0)
    rows = tok_ref.shape[0]
    if shared:
        table_ref, results, gtok_ref, gscale_ref, gshift_ref, factor_group, factor_all, back, gw, summed, factors, *refs = refs
        lands, sems = refs[:30], refs[30:]
        me, links = place(), Links(*sems)
        schedule = []
        for i in range(6):
            half = HALVES[i % 2]
            unit = reduce_turns(
                links, me, gw.at[i // 2], half.start, summed.at[i // 2, half], results.at[i // 2, half], lands[5 * i : 5 * i + 5]
            )
            schedule += timed([unit], 0, TAIL_REDUCE, 4 * (i // 2 + 1) + 2 * (i % 2))
        turns = placed(schedule)
        host = Host(links, {h: t for h, t in turns.items() if h < 24}, 6, 4)
        rest = [turns[h] for h in sorted(turns) if h >= 24]
        spread = factors_turns(links, me, factors, factor_group, factor_all)
    else:
        gw, gtok_ref, gscale_ref, gshift_ref, back = refs
        host, rest = Idle(), []

    def products(r):
        value = tn(hidden_ref[:, r * 256 : r * 256 + 256], grad_ref[0]).astype(jnp.bfloat16)
        for half in (0, 1):
            gw[p if shared else 0, 2 * r + half] = value[half * 128 : half * 128 + 128]

    def way_back(r):
        here = pl.ds(r * (rows // 4), rows // 4)
        part = nt(grad_ref[0, here, :], w_ref[0])

        @pl.when(p == 3)
        def _():
            back[here, :] = part

        @pl.when(p > 3)
        def _():
            back[here, :] += part

    for r in range(4):
        host.turn(r)
        pl.when(p < 3)(functools.partial(products, r))
        pl.when(p >= 3)(functools.partial(way_back, r))

    @pl.when(p == pl.num_programs(0) - 1)
    def _():
        def unit(u):
            at = pl.ds(pl.multiple_of(u * UNIT, UNIT), UNIT)
            normed, inverse = normalize(tok_ref[at, :].astype(jnp.float32))
            grad = back[at, :]
            gshift_ref[pl.ds(u, 1), :] = jnp.sum(grad, axis=0, keepdims=True)
            gscale_ref[pl.ds(u, 1), :] = jnp.sum(grad * normed, axis=0, keepdims=True)
            gtok_ref[at, :] = mid_ref[at, :] + norm_back(grad * (1.0 + scale_ref[pl.ds(u, 1), :]), normed, inverse)

        for quarter in range(4):
            if quarter < len(rest):
                run(rest[quarter])
            loop(rows // UNIT // 4, lambda i: unit(quarter * (rows // UNIT // 4) + i))
        if shared:
            table = table_ref[...].astype(jnp.bfloat16)
            for i, ref in enumerate((gscale_ref, gshift_ref)):
                factors[:, i * D : (i + 1) * D] = exact(table, ref[...]).astype(jnp.bfloat16)
            left = rest[4:]
            for i in range(max(len(left), len(spread))):
                if i < len(spread):
                    spread[i]()
                if i < len(left):
                    run(left[i])

    host.finish()


def project_back(grad_proj, hidden, w_qkv, tokens, grad_mid, scale, table=None):
    rows = tokens.shape[0]
    once = lambda shape: pl.BlockSpec(shape, lambda p: (0, 0), pipeline_mode=pl.Buffered(1))
    units, whole = once((rows // UNIT, D)), once((rows, D))
    f32, b16 = jnp.float32, jnp.bfloat16
    block = pl.BlockSpec((1, rows, D), lambda p: (lax.rem(p, 3), 0, 0))
    inputs = [
        (grad_proj, block), (hidden, whole), (w_qkv, pl.BlockSpec((1, D, D), lambda p: (jnp.maximum(p - 3, 0), 0, 0))), (tokens, whole), (grad_mid, whole), (scale, units),
    ]
    outputs = [((rows, D), f32, whole), ((rows // UNIT, D), f32, units), ((rows // UNIT, D), f32, units)]
    scratch = [pltpu.VMEM((rows, D), f32)]
    shared = table is not None
    if shared:
        slots = table.shape[0]
        inputs += [(table, once(table.shape))]
        outputs = [((3, 128, D), b16, ANY)] + outputs
        outputs += [((4 * slots, 2 * D), b16, ANY), ((32 * slots, 2 * D), b16, ANY)]
        scratch += [pltpu.VMEM((3, 8, 128, D), b16), pltpu.VMEM((3, 128, D), b16), pltpu.VMEM((slots, 2 * D), b16)] + [land for _ in range(6) for land in reduce_lands(64, far=False)]
        scratch += semaphores(6 * REDUCE_HOPS + FACTOR_HOPS, 6 * REDUCE_NEAR + FACTOR_NEAR)
    else:
        outputs = [((3, 8, 128, D), b16, pl.BlockSpec((1, 8, 128, D), lambda p: (jnp.minimum(p, 2), 0, 0, 0)))] + outputs
    return call(functools.partial(tail_kernel, shared), (6,), inputs, outputs, scratch)


def tuned(sizes):
    return sizes == (4, 8)


def blocks_of(columns):
    return columns.reshape(columns.shape[0], FF_BLOCKS, -1).transpose(1, 0, 2)


def local(
    sizes, tokens, lengths, buckets, w_mod, b_mod, w_qkv, w_out, b_out, w_up, b_up, w_down, b_down, cotangent,
):
    rows, slots, n = tokens.shape[0], lengths.shape[1], sizes[1]
    own = tuned(sizes)
    segment, live, unit_table = layout(lengths[0], rows)
    feats = time_features(buckets[0]).astype(jnp.bfloat16)
    whole = lambda array: lax.all_gather(array, "fsdp", axis=0, tiled=True)
    if own:
        packed = jnp.concatenate([b_mod, b_out, b_up, b_down]).reshape(-1, 128)
        packed = jnp.pad(packed, ((0, 16 - packed.shape[0]), (0, 0)))
        by_owner = feats.reshape(slots, n, 128).transpose(1, 0, 2)
        small = jnp.concatenate([jnp.broadcast_to(packed, (n, 16, 128)), by_owner], axis=1)
        small_all, full_qkv, hidden_attn, projected, per_unit = first_all(small, w_mod, w_qkv, tokens, unit_table)
        of_group = lax.dynamic_slice(small_all, (lax.axis_index("dp") * n, 0, 0), (n, 16, 128))
        full_bout, full_bdown = of_group[:, 4].reshape(1, -1), of_group[:, 9].reshape(1, -1)
        full_bup = of_group[:, 5:9].transpose(1, 0, 2).reshape(FF_BLOCKS, 1, -1)
        every_feats = small_all[:, 16:].reshape(sizes[0], n, slots, 128).transpose(1, 0, 2, 3).reshape(-1, 128)
    else:
        full_mod, full_qkv, full_bmod, full_bout, full_bup, full_bdown = [whole(a) for a in (w_mod, w_qkv, b_mod, b_out, b_up, b_down)]
        full_bout, full_bdown, full_bup = full_bout[None], full_bdown[None], full_bup.reshape(FF_BLOCKS, 1, -1)
        every_feats = lax.all_gather(feats, ("dp", "fsdp"), axis=0, tiled=True)
        every_feats = lax.dynamic_slice(every_feats, (0, lax.axis_index("fsdp") * (D // n)), (every_feats.shape[0], D // n))
        modulation = jnp.dot(feats, full_mod, preferred_element_type=jnp.float32) + full_bmod
        per_unit = jnp.dot(unit_table, modulation, precision=HIGHEST)
        full_qkv = full_qkv.reshape(D, 3, D).transpose(1, 0, 2)
        hidden_attn, projected = project_in(tokens, per_unit[:, :D], per_unit[:, D : 2 * D], full_qkv)
    scale_one, _, scale_two, shift_two = [per_unit[:, i * D : (i + 1) * D] for i in range(4)]
    live_units = jnp.broadcast_to(live[:, None], (rows // UNIT, D))
    query_lanes, key_lanes = attention_lanes(jnp.repeat(segment, UNIT), slots)
    if own:
        ups = w_up.reshape(-1, n, FF_BLOCKS, 128).transpose(2, 0, 1, 3).reshape(FF_BLOCKS, 1, -1, D)
        downs = w_down.reshape(FF_BLOCKS, 1, -1, D)
        pairs = jnp.concatenate([ups, downs], axis=1).reshape(2 * FF_BLOCKS, -1, D)
        attn_out, asked, weights = attend(projected, query_lanes, key_lanes, jnp.concatenate([w_out[None], pairs[: 2 * EARLY]]))
        late = pairs[2 * EARLY :]
    else:
        attn_out, asked = attend(projected, query_lanes, key_lanes)
        pairs = jnp.stack([blocks_of(whole(w_up)), whole(w_down).reshape(FF_BLOCKS, D, D)], axis=1)
        weights, late = jnp.concatenate([whole(w_out)[None], pairs.reshape(2 * FF_BLOCKS, D, D)]), None
    middle, hidden_mlp, grad_two, grad_b_down = before_mlp(
        attn_out, tokens, cotangent, weights, full_bout, scale_two, shift_two, live_units
    )
    forward, backward, grad_b_up, grad_pairs, *totals_early = feed_forward(hidden_mlp, grad_two, weights, full_bup, late)
    output, grad_mid, grad_attn, grad_w_out, grad_b_out, grad_scale_two, grad_shift_two = after_mlp(
        middle, forward, backward, cotangent, attn_out, weights, full_bdown, scale_two, live_units
    )

    def factors_of(first, second):
        return jnp.dot(unit_table.T, jnp.concatenate([first, second], axis=1), precision=HIGHEST).astype(jnp.bfloat16)

    mod_two = factors_of(grad_scale_two, grad_shift_two)
    if own:
        sums = [grad_b_out.reshape(n, 1, 128), grad_b_up.reshape(FF_BLOCKS, n, 128).transpose(1, 0, 2), grad_b_down.reshape(n, 1, 128)]
        small = jnp.pad(jnp.concatenate(sums, axis=1), ((0, 0), (0, 2), (0, 0)))
        grad_proj, totals, small_all, _, mod_two = attend_back(
            projected, key_lanes, asked, attn_out, grad_attn, (grad_pairs.reshape(-1, 8, 128, D), grad_w_out), small, mod_two
        )
        total = jnp.sum(small_all, axis=0)
        sum_bout, sum_bup, sum_bdown = total[0], total[1:5].reshape(-1), total[5]
    else:
        grad_proj = attend_back(projected, key_lanes, asked, attn_out, grad_attn)[0]
    qkv_grads, grad_tokens, grad_scale_one, grad_shift_one, *factors = project_back(
        grad_proj, hidden_attn, full_qkv, tokens, grad_mid, scale_one, unit_table.T if own else None
    )
    if own:
        mod_one = factors[1]
    else:
        mod_one = factors_of(grad_scale_one, grad_shift_one)
        mod_one, mod_two = [lax.all_gather(m, ("dp", "fsdp"), axis=0, tiled=True) for m in (mod_one, mod_two)]
    sum_mod = jnp.concatenate(
        [jnp.einsum("sd,sc->dc", every_feats, m, preferred_element_type=jnp.float32) for m in (mod_one, mod_two)], axis=1
    )
    position, share = lax.axis_index("fsdp"), 4 * D // n
    chosen = jnp.where(position < n // 2, mod_one, mod_two)
    sum_bmod = jnp.sum(
        lax.dynamic_slice(chosen, (0, position % (n // 2) * share), (chosen.shape[0], share)), axis=0, dtype=jnp.float32
    )
    if own:
        totals, qkv_grads = totals.astype(jnp.float32), qkv_grads.astype(jnp.float32)
        pairs = jnp.concatenate([totals_early[0].astype(jnp.float32), totals[:-1]]).reshape(FF_BLOCKS, 2, 128, D)
        sum_up = pairs[:, 0].reshape(FF_BLOCKS, -1, n, 128).transpose(1, 2, 0, 3).reshape(w_up.shape)
        sum_down = pairs[:, 1].reshape(w_down.shape)
        sum_out = totals[-1]
        sum_qkv = qkv_grads.transpose(1, 0, 2).reshape(w_qkv.shape)
    else:
        summed = lambda a: lax.psum(lax.psum_scatter(a, "fsdp", scatter_dimension=0, tiled=True), "dp").astype(jnp.float32)
        sum_up = summed(grad_pairs[:, 0].reshape(FF_BLOCKS, D, D).transpose(1, 0, 2).reshape(D, -1))
        sum_down = summed(grad_pairs[:, 1].reshape(-1, D))
        sum_out, sum_qkv = summed(grad_w_out.reshape(D, D)), summed(qkv_grads.reshape(3, D, D).transpose(1, 0, 2).reshape(D, -1))
        sum_bout, sum_bup, sum_bdown = [summed(a.reshape(-1)) for a in (grad_b_out, grad_b_up, grad_b_down)]
    return output, grad_tokens, sum_mod, sum_bmod, sum_qkv, sum_out, sum_bout, sum_up, sum_bup, sum_down, sum_bdown


def solution(mesh):
    sizes = (mesh.shape["dp"], mesh.shape["fsdp"])
    rows, cut_rows, vector = P(("dp", "fsdp"), None), P("fsdp", None), P("fsdp")
    return jax.shard_map(
        functools.partial(local, sizes),
        mesh=mesh,
        in_specs=(rows, rows, rows, cut_rows, vector, cut_rows, cut_rows, vector, cut_rows, vector, cut_rows, vector, rows),
        out_specs=(rows, rows, cut_rows, vector, cut_rows, cut_rows, vector, cut_rows, vector, cut_rows, vector),
        check_vma=False,
    )
```

```python
import functools
import math

import jax
import jax.numpy as jnp
from jax import lax
from jax.experimental import pallas as pl
from jax.experimental.pallas import tpu as pltpu
from jax.sharding import PartitionSpec as P

D = 1024
HEADS = 16
HEAD_DIM = 64
EPSILON = 1e-05
UNIT = 64
ROWS = 512
ATTENTION_ROWS = 512
FF_BLOCKS = 4
EARLY = 2
LSE_LANE = 24
ATTEND_GATHER = (3, (0, 4, 8, 12, 15))
MLP_GATHER = ((0, 3, 6, 9, 12, 15, 19, 23), (0, 7, 13, 19, 22))
MLP_REDUCE = ((18, 22, 26, 30, 34, 38, 42, 46), (0, 3, 8, 14, 20, 24, 26))
BACK_REDUCE = (2.6, (0, 2, 5, 8, 11, 13, 15))
BACK_FACTORS = (1, 4, 8, 12, 16, 19)
TAIL_REDUCE = (0, 2, 6, 11, 16, 19, 21)
VMEM_LIMIT = 62 * 2**20
HIGHEST = lax.Precision.HIGHEST
MESH = pl.DeviceIdType.MESH


def layout(lengths, tok_rows):
    slots = lengths.shape[0]
    upto = jnp.arange(slots)[:, None] <= jnp.arange(slots)[None, :]
    seq_ends = jnp.sum(jnp.where(upto, lengths[:, None], 0), axis=0, dtype=jnp.int32)
    position = jnp.arange(0, tok_rows, UNIT, dtype=jnp.int32)
    segment = jnp.sum((position[:, None] >= seq_ends[None, :]).astype(jnp.int32), axis=1, dtype=jnp.int32)
    unit_table = (segment[:, None] == jnp.arange(slots, dtype=jnp.int32)[None, :]).astype(jnp.float32)
    return segment, (segment < slots).astype(jnp.float32), unit_table


def time_features(buckets):
    half_width = D // 2
    frequency = jnp.exp(-math.log(10000.0) * jnp.arange(half_width, dtype=jnp.float32) / half_width)
    angles = buckets.astype(jnp.float32)[:, None] * frequency[None, :]
    return jnp.concatenate([jnp.sin(angles), jnp.cos(angles)], axis=1)


def place():
    dp, fsdp = lax.axis_index("dp"), lax.axis_index("fsdp")
    return dp // 2, dp % 2, fsdp // 2, fsdp % 2


def device(x, core, z, y):
    return (x * 2 + core, z * 2 + y)


class Hop:
    def __init__(self, links, src, dst, target):
        self.links, self.src, self.dst, self.target, self.gone = links, src, dst, target, False
        self.slot = links.used
        links.used += 1
        links.hops.append(self)

    def made(self):
        return pltpu.make_async_remote_copy(
            src_ref=self.src(),
            dst_ref=self.dst(),
            send_sem=self.links.send_sems.at[self.slot],
            recv_sem=self.links.recv_sems.at[self.slot],
            device_id=self.target(),
            device_id_type=MESH,
        )

    def start(self):
        self.made().start()

    def arrived(self):
        self.made().wait_recv()

    def left(self):
        self.gone = True
        self.made().wait_send()


class Near:
    def __init__(self, links, src, dst):
        self.links, self.src, self.dst = links, src, dst
        self.slot = links.used_near
        links.used_near += 1

    def made(self):
        return pltpu.make_async_copy(self.src(), self.dst(), self.links.near_sems.at[self.slot])

    def start(self):
        self.made().start()

    def arrived(self):
        self.made().wait()


class Links:
    def __init__(self, send_sems, recv_sems, near_sems):
        self.send_sems, self.recv_sems, self.near_sems = send_sems, recv_sems, near_sems
        self.used, self.used_near, self.hops, self.ends = 0, 0, [], []

    def drain(self):
        for hop in self.hops:
            if not hop.gone:
                hop.left()
        for end in self.ends:
            end()


def lanes(at, size):
    return pl.ds(pl.multiple_of(at, 128), size)


def lines(at, size):
    return pl.ds(pl.multiple_of(at, 16), size)


HALVES = (pl.ds(0, 64), pl.ds(64, 64))


def gather_turns(links, me, shard, whole, outer, at=None):
    x, core, z, y = me
    rows, width = shard.shape
    half = width // 2
    inner = half - 2 * outer
    own = lanes(core * half + x * outer, outer + inner)
    crossing = lanes(core * half + x * (outer + inner), outer)
    full = lanes(core * half, half)

    def place_of(index):
        return lines(index * rows, rows) if at is None else lines(index * 128 + at, rows)

    mine = place_of(z * 2 + y)
    blocks = {}
    for k in range(4):
        source = ((z - k + 4) % 4) * 2
        blocks["z", k], blocks["y", k] = place_of(source + y), place_of(source + 1 - y)
    to_z = {k: device(x, core, (z + k) % 4, y) for k in (1, 2, 3)}
    to_y, to_x, to_core = device(x, core, z, 1 - y), device(1 - x, core, z, y), device(x, 1 - core, z, y)

    def from_shard(target):
        return Hop(links, lambda: shard.at[:, own], lambda: whole.at[mine, own], lambda: target)

    def pass_on(way, k, columns, target):
        def ref():
            return whole.at[blocks[way, k], columns]

        return Hop(links, ref, ref, lambda: target)

    keep = Near(links, lambda: shard, lambda: whole.at[mine, :])
    along_z = {k: from_shard(to_z[k]) for k in (1, 2, 3)}
    along_y = {0: from_shard(to_y)}
    for k in (1, 2, 3):
        along_y[k] = pass_on("z", k, own, to_y)
    order = [("z", 1), ("y", 0), ("z", 2), ("y", 1), ("z", 3), ("y", 2), ("y", 3)]
    crossed = [pass_on(way, k, crossing, to_x) for way, k in order] if outer else None
    handed = [pass_on(way, k, full, to_core) for way, k in order]

    def first():
        for k in (1, 2, 3):
            along_z[k].start()
        along_y[0].start()
        keep.start()

    def arrive(j):
        way, k = order[j]
        (along_z if way == "z" else along_y)[k].arrived()
        if way == "z":
            along_y[k].start()
        (crossed if outer else handed)[j].start()

    def hand_on(j):
        if outer:
            crossed[j].arrived()
            handed[j].start()

    def last():
        for hop in handed:
            hop.arrived()
        keep.arrived()

    return [
        first,
        lambda: [arrive(j) for j in (1, 0, 2, 4)],
        lambda: [arrive(j) for j in (3, 5, 6)] + [hand_on(j) for j in (1, 0, 2, 4)],
        lambda: [hand_on(j) for j in (3, 5, 6)],
        last,
    ]


GATHER_HOPS, GATHER_NEAR = 3 + 4 + 7 + 7, 1


def reduce_lands(rows, width=1024, far=True):
    half = width // 2
    outer = half // 4
    shapes = [
        (4, 2, rows, half), (4, 2, rows, outer), (4, rows, half - outer), (3, rows, half - outer), (rows, half - outer),
    ]
    if far:
        shapes.append((4, 2, rows, half))
    return [pltpu.VMEM(s, jnp.bfloat16) for s in shapes]


def reduce_turns(links, me, local, at, result, out, lands):
    x, core, z, y = me
    total, from_x, from_y, from_z, from_last = lands[:5]
    far = lands[5] if len(lands) > 5 else None
    rows, width = result.shape
    half = width // 2
    outer = half // 4
    wide = half - outer

    own, kept, given = lanes(x * outer, wide), lanes(x * wide, outer), lanes((1 - x) * wide, outer)
    sides, here = {True: lanes(core * half, half), False: lanes((1 - core) * half, half)}, pl.ds(at, rows)
    owners_of = [pl.ds(((z + t + 1) % 4) * 2, 2) for t in range(4)]
    other = 1 - y
    at_core, at_x, at_y = device(x, 1 - core, z, y), device(1 - x, core, z, y), device(x, core, z, other)
    at_z = [device(x, core, (z + t + 1) % 4, y) for t in range(3)]

    def owners(t, ours):
        return local.at[owners_of[t], here, sides[ours]]

    turns4 = range(4)
    load = [Near(links, lambda t=t: owners(t, True), lambda t=t: far.at[t]) for t in turns4] if far is not None else []
    to_core = [Hop(links, lambda t=t: owners(t, False), lambda t=t: total.at[t], lambda: at_core) for t in turns4]
    to_x = [Hop(links, lambda t=t: total.at[t, :, :, given], lambda t=t: from_x.at[t], lambda: at_x) for t in turns4]
    to_y = [Hop(links, lambda t=t: total.at[t, other, :, own], lambda t=t: from_y.at[t], lambda: at_y) for t in turns4]
    to_z = [Hop(links, lambda t=t: total.at[t, y, :, own], lambda t=t: from_z.at[t], lambda t=t: at_z[t]) for t in range(3)]
    to_last = Hop(links, lambda: total.at[3, y, :, own], lambda: from_last, lambda: at_x)
    mine = lambda: result.at[:, sides[True]]
    to_final = Hop(links, mine, mine, lambda: at_core)
    store = Near(links, lambda: result, lambda: out)
    links.ends.append(store.arrived)

    def add(index, landed):
        total[index] = (total[index].astype(jnp.float32) + landed.astype(jnp.float32)).astype(total.dtype)

    def first():
        for t in turns4:
            to_core[t].start()
        for near in load:
            near.start()

    def core_turn():
        for t in turns4:
            to_core[t].arrived()
            if far is None:
                to_core[t].left()
                add(t, owners(t, True)[...])
            else:
                load[t].arrived()
                add(t, far[t])
            to_x[t].start()

    def x_turn():
        for t in turns4:
            to_x[t].arrived()
            add((t, slice(None), slice(None), kept), from_x[t])
            to_y[t].start()

    def y_turn():
        for t in range(3):
            to_y[t].arrived()
            add((t, y, slice(None), own), from_y[t])
            to_z[t].start()

    def z_turn():
        to_y[3].arrived()
        everything = total[3, y, :, own].astype(jnp.float32) + from_y[3].astype(jnp.float32)
        for t in range(3):
            to_z[t].arrived()
            everything = everything + from_z[t].astype(jnp.float32)
        total[3, y, :, own] = everything.astype(total.dtype)
        to_last.start()

    def last_turn():
        to_last.arrived()
        middle = half - 2 * outer
        shared = total[3, y, :, lanes(outer, middle)].astype(jnp.float32) + from_last[:, lanes(x * outer, middle)].astype(jnp.float32)
        result[:, lanes(core * half + outer, middle)] = shared.astype(result.dtype)
        result[:, lanes(core * half + x * wide, outer)] = total[3, y, :, kept]
        result[:, lanes(core * half + (1 - x) * wide, outer)] = from_last[:, lanes((1 - x) * middle, outer)]
        to_final.start()

    def end():
        to_final.arrived()
        store.start()

    return [first, core_turn, x_turn, y_turn, z_turn, last_turn, end]


REDUCE_HOPS, REDUCE_NEAR = 4 + 4 + 4 + 3 + 2, 5


def merged(units, every, lag=1):
    turns = []
    for i, unit in enumerate(units):
        for k, turn in enumerate(unit):
            at = i * every + k * lag
            turns += [[] for _ in range(at + 1 - len(turns))]
            turns[at].insert(0, turn)
    return turns


def run(turn):
    for action in turn:
        action()


def semaphores(hops, near):
    return [pltpu.SemaphoreType.DMA((hops,)), pltpu.SemaphoreType.DMA((hops,)), pltpu.SemaphoreType.DMA((max(near, 1),))]


def exchange_small(small, small_all, links, me):
    x, core, z, y = me
    number = (x * 2 + core) * 8 + z * 2 + y
    keep = Near(links, lambda: small.at[z * 2 + y], lambda: small_all.at[number])
    few = [
        Hop(
            links,
            lambda k=k: small.at[(number + k) % 8],
            lambda: small_all.at[number],
            lambda k=k: (((number + k) % 32) // 8, (number + k) % 8),
        )
        for k in range(1, 32)
    ]

    def begin():
        keep.start()
        for hop in few:
            hop.start()

    def end():
        keep.arrived()
        for hop in few:
            hop.arrived()

    return begin, end


def factors_turns(links, me, factors, group, whole):
    x, core, z, y = me
    slots = factors.shape[0]
    mine = lambda: group.at[lines((x * 2 + core) * slots, slots), :]
    keep = Near(links, lambda: factors, mine)
    peers = [
        Hop(links, lambda: factors, mine, lambda i=i, j=j: device((x + i) % 2, (core + j) % 2, z, y)) for i, j in ((0, 1), (1, 0), (1, 1))
    ]

    def first():
        keep.start()
        for hop in peers:
            hop.start()

    def second():
        keep.arrived()
        for hop in peers:
            hop.arrived()

    turns = gather_turns(links, me, group, whole, 256)
    return [first, lambda: (second(), turns[0]())] + turns[1:]


FACTOR_HOPS, FACTOR_NEAR = 3 + GATHER_HOPS, 1 + GATHER_NEAR


def nt(a, b):
    return lax.dot_general(a, b, (((1,), (1,)), ((), ())), preferred_element_type=jnp.float32)


def tn(a, b):
    return lax.dot_general(a, b, (((0,), (0,)), ((), ())), preferred_element_type=jnp.float32)


def nn(a, b):
    return jnp.dot(a, b, preferred_element_type=jnp.float32)


def normalize(values):
    centred = values - jnp.mean(values, axis=1, keepdims=True)
    inverse = lax.rsqrt(jnp.mean(centred * centred, axis=1, keepdims=True) + EPSILON)
    return (centred * inverse, inverse)


def norm_back(grad_normed, normed, inverse):
    first_mean = jnp.mean(grad_normed, axis=1, keepdims=True)
    second_mean = jnp.mean(grad_normed * normed, axis=1, keepdims=True)
    return inverse * (grad_normed - first_mean - normed * second_mean)


def gelu_both(u):
    c = math.sqrt(2 / math.pi)
    square = u * u
    t = jnp.tanh(u * (c + (c * 0.044715) * square))
    half = 0.5 + 0.5 * t
    value = u * half
    return value, half + value * (1.0 - t) * (c + (3 * c * 0.044715) * square)


def loop(count, body):
    def step(i, carry):
        body(i)
        return carry

    lax.fori_loop(0, count, step, 0)


def attention_lanes(segment, slots):
    lane = jnp.arange(128) % 64
    hot = segment[:, None] == lane[None, :]
    listed = lane[None, :] <= slots
    query_lanes = (hot & listed).astype(jnp.bfloat16)
    ones = (lane >= LSE_LANE) & (lane < LSE_LANE + 3)
    key_lanes = jnp.where(listed & ~hot, -1e30, jnp.where(ones[None, :], 1.0, 0.0)).astype(jnp.bfloat16)
    return query_lanes, key_lanes


class Host:
    def __init__(self, links, turns, steps, per_step):
        self.links, self.turns, self.steps, self.per_step = links, turns, steps, per_step
        self.step = pl.program_id(0)

    def turn(self, index):
        for hook, turn in sorted(self.turns.items()):
            if hook < self.steps * self.per_step and hook % self.per_step == index:
                pl.when(self.step == hook // self.per_step)(functools.partial(run, turn))

    def finish(self):
        @pl.when(self.step == self.steps - 1)
        def _():
            for hook, turn in sorted(self.turns.items()):
                if hook >= self.steps * self.per_step:
                    run(turn)
            self.links.drain()


def timed(units, every, lags, first=0):
    starts = every if isinstance(every, tuple) else [int(first + every * i) for i in range(len(units))]
    return [(start + lag, turn) for start, unit in zip(starts, units) for lag, turn in zip(lags, unit)]


def placed(schedule):
    turns = {}
    for hook, turn in schedule:
        turns.setdefault(hook, []).insert(0, turn)
    return turns


class Idle:
    def turn(self, index):
        pass

    def finish(self):
        pass


ANY = pl.BlockSpec(memory_space=pl.ANY)
VMEM = pl.BlockSpec(memory_space=pltpu.VMEM)


def call(kernel, grid, inputs, outputs, scratch=()):
    made = pl.pallas_call(
        kernel,
        grid=grid,
        out_shape=[jax.ShapeDtypeStruct(shape, kind) for shape, kind, _ in outputs],
        in_specs=[spec for _, spec in inputs],
        out_specs=[spec for _, _, spec in outputs],
        scratch_shapes=list(scratch),
        compiler_params=pltpu.CompilerParams(has_side_effects=True, vmem_limit_bytes=VMEM_LIMIT),
    )
    return made(*[array for array, _ in inputs])


def exact(table, values):
    sums = None
    for _ in range(3):
        part = values.astype(jnp.bfloat16)
        values = values - part.astype(jnp.float32)
        sums = nn(table, part) if sums is None else sums + nn(table, part)
    return sums


def modulation_turns(links, me, parts, from_y, from_z, columns):
    x, core, z, y = me
    block = lambda t, side: parts.at[((z + t + 1) % 4) * 2 + side, :, columns]
    to_y = [Hop(links, lambda t=t: block(t, 1 - y), lambda t=t: from_y.at[t, :, columns], lambda: device(x, core, z, 1 - y)) for t in range(4)]
    to_z = [
        Hop(links, lambda t=t: block(t, y), lambda t=t: from_z.at[t, :, columns], lambda t=t: device(x, core, (z + t + 1) % 4, y))
        for t in range(3)
    ]

    def begin():
        for hop in to_y:
            hop.start()

    def middle():
        for t in range(3):
            to_y[t].arrived()
            block(t, y)[...] = (block(t, y)[...].astype(jnp.float32) + from_y[t, :, columns].astype(jnp.float32)).astype(parts.dtype)
            to_z[t].start()

    def end():
        to_y[3].arrived()
        total = block(3, y)[...].astype(jnp.float32) + from_y[3, :, columns].astype(jnp.float32)
        for t in range(3):
            to_z[t].arrived()
            total = total + from_z[t, :, columns].astype(jnp.float32)
        return total

    return begin, middle, end


def first_kernel(small, wmod_ref, wqkv, tok_ref, table_ref, small_all, wholes, hidden_ref, out_ref, unit_ref, landed, held, normed, *refs):
    parts, from_y, from_z, sems = refs[:2], refs[2:4], refs[4:6], refs[6:]
    me, links = place(), Links(*sems)
    x, core, z, y = me
    group = (x * 2 + core) * 8
    rows = tok_ref.shape[0]
    begin, end = exchange_small(small, landed, links, me)
    units = [
        gather_turns(links, me, wqkv.at[half, pl.ds(i * D, D)], held.at[i], 128 if half.start else 256, half.start)
        for i in range(3)
        for half in HALVES
    ]
    gather = merged(units, 1)
    halves = [modulation_turns(links, me, parts[i], from_y[i], from_z[i], pl.ds(0, 2 * D)) for i in (0, 1)]
    keep = [Near(links, lambda i=i: held.at[i], lambda i=i: wholes.at[i]) for i in range(3)]
    save = Near(links, lambda: landed, lambda: small_all)
    links.ends += [near.arrived for near in keep + [save]]

    def norm(first):
        def unit(u):
            at = pl.ds(pl.multiple_of(u * UNIT, UNIT), UNIT)
            normed[at, :] = normalize(tok_ref[at, :].astype(jnp.float32))[0]

        loop(rows // UNIT // 2, lambda i: unit(first + i))

    def settle(half):
        total = halves[half][2]()
        table = table_ref[...].astype(jnp.bfloat16)
        for f in range(4):
            bias = landed[group + 4 * half + f, :16, :].astype(jnp.float32)
            for i in range(4):
                at = (4 * f + i) * 128
                value = total[:, at : at + 128] + bias[i : i + 1, :]
                unit_ref[:, 2 * half * D + at : 2 * half * D + at + 128] = exact(table, value)

    def project(i):
        def block(r):
            here = pl.ds(pl.multiple_of(r * 256, 256), 256)
            out_ref[here, i * D : (i + 1) * D] = nn(hidden_ref[here, :], held[i]).astype(jnp.bfloat16)

        loop(rows // 256, block)

    begin()
    run(gather[0])
    norm(0)
    run(gather[1])
    norm(rows // UNIT // 2)
    end()
    save.start()
    for f in range(8):
        part = nn(landed[group + f, 16:, :], wmod_ref[...])
        for half in (0, 1):
            parts[half][f] = part[:, half * 2 * D : (half + 1) * 2 * D].astype(parts[half].dtype)
    halves[0][0]()
    run(gather[2])
    halves[0][1]()
    halves[1][0]()
    run(gather[3])
    settle(0)
    halves[1][1]()

    def shape(u):
        at = pl.ds(pl.multiple_of(u * UNIT, UNIT), UNIT)
        hidden_ref[at, :] = (normed[at, :] * (1.0 + unit_ref[pl.ds(u, 1), :D]) + unit_ref[pl.ds(u, 1), D : 2 * D]).astype(jnp.bfloat16)

    run(gather[4])
    loop(rows // UNIT, shape)
    run(gather[5])
    keep[0].start()
    project(0)
    run(gather[6])
    settle(1)
    run(gather[7])
    keep[1].start()
    project(1)
    run(gather[8])
    run(gather[9])
    keep[2].start()
    project(2)
    links.drain()


def first_all(small, w_mod, w_qkv, tokens, table):
    rows, (units, slots) = tokens.shape[0], table.shape
    b16, f32 = jnp.bfloat16, jnp.float32
    hops = 31 + 6 * GATHER_HOPS + 14
    return call(
        first_kernel,
        (),
        [(small, ANY), (w_mod, VMEM), (w_qkv, ANY), (tokens, VMEM), (table, VMEM)],
        [
            ((32,) + small.shape[1:], b16, ANY), ((3, D, D), b16, ANY), ((rows, D), b16, VMEM), ((rows, 3 * D), b16, VMEM),
            ((units, 4 * D), f32, VMEM),
        ],
        [
            pltpu.VMEM((32,) + small.shape[1:], b16), pltpu.VMEM((3, D, D), b16), pltpu.VMEM((rows, D), f32),
        ]
        + [pltpu.VMEM((count, slots, 2 * D), kind) for count in (8, 4, 3) for kind in (f32, b16)]
        + semaphores(hops, 1 + 6 * GATHER_NEAR + 4),
    )


def attend_kernel(shared, q_ref, k_ref, v_ref, ql_ref, kl_ref, *refs):
    if shared:
        shards, out_ref, qa_ref, wholes, *sems = refs
        me, links = place(), Links(*sems)
        units = [
            gather_turns(links, me, shards.at[i, half], wholes.at[i], 128 if half.start else 256, half.start)
            for i in range(shared)
            for half in HALVES
        ]
        host = Host(links, placed(timed(units, *ATTEND_GATHER)), D // 128, 4)
    else:
        (out_ref, qa_ref), host = refs, Idle()
    rows = q_ref.shape[0]
    block = min(ATTENTION_ROWS, rows)
    low = lax.broadcasted_iota(jnp.int32, (1, 128), 1) < HEAD_DIM
    lane = lax.broadcasted_iota(jnp.int32, (1, 128), 1) % HEAD_DIM
    keys, vals = [], []
    for own in (low, ~low):
        keys.append(jnp.where(own, k_ref[...], kl_ref[...]))
        vals.append(jnp.where(own, v_ref[...], jnp.bfloat16(1)))
    for at, first in enumerate(range(0, rows, block)):
        here = pl.ds(first, block)
        queries = q_ref[here, :] * jnp.bfloat16(HEAD_DIM**-0.5)
        mixed = []
        for head, own in enumerate((low, ~low)):
            host.turn(2 * at + head)
            asked = jnp.where(own, queries, ql_ref[here, :])
            scores = nt(asked, keys[head])
            top = jnp.max(scores, axis=1, keepdims=True)
            weight = jnp.exp(scores - top).astype(jnp.bfloat16)
            both = nn(weight, vals[head])
            mixed.append(both)
            log_total = -(top + jnp.log(both))
            first_part = log_total.astype(jnp.bfloat16)
            rest = log_total - first_part.astype(jnp.float32)
            second = rest.astype(jnp.bfloat16)
            third = (rest - second.astype(jnp.float32)).astype(jnp.bfloat16)
            for i, part in enumerate((first_part, second, third)):
                asked = jnp.where(~own & (lane == LSE_LANE + i), part, asked)
            qa_ref[head, here, :] = asked
        total = pltpu.roll(jnp.where(low, mixed[1], mixed[0]), HEAD_DIM, 1)
        out_ref[here, :] = (jnp.where(low, mixed[0], mixed[1]) / total).astype(jnp.bfloat16)
    host.finish()


def attend(projected, query_lanes, key_lanes, shards=None):
    rows, pairs = projected.shape[0], D // 128
    spec = lambda shift: pl.BlockSpec((rows, 128), lambda i: (0, i + shift))
    same = pl.BlockSpec((rows, 128), lambda i: (0, 0))
    inputs = [(projected, spec(0)), (projected, spec(pairs)), (projected, spec(2 * pairs)), (query_lanes, same), (key_lanes, same)]
    outputs = [((rows, D), jnp.bfloat16, spec(0)), ((HEADS, rows, 128), jnp.bfloat16, pl.BlockSpec((2, rows, 128), lambda i: (i, 0, 0)))]
    if shards is None:
        return call(functools.partial(attend_kernel, 0), (pairs,), inputs, outputs)
    units, depth, width = shards.shape
    return call(
        functools.partial(attend_kernel, units),
        (pairs,),
        inputs + [(shards, ANY)],
        outputs + [((units, 8 * depth, width), shards.dtype, ANY)],
        semaphores(2 * GATHER_HOPS * units, 2 * GATHER_NEAR * units),
    )


def attend_back_kernel(counts, k_ref, v_ref, kl_ref, qa_ref, out_ref, go_ref, *refs):
    units = sum(counts)
    if units:
        groups, refs = refs[: len(counts)], refs[len(counts) :]
        small, factors, grad_ref, results, small_all, factor_group, factor_all, kt_ref, dqt_ref, *refs = refs
        summed, lands, sems = refs[0], refs[1 : 1 + 12 * units], refs[1 + 12 * units :]
        me, links = place(), Links(*sems)
        begin, end = exchange_small(small, small_all, links, me)
        locals_ = [group.at[i] for group, count in zip(groups, counts) for i in range(count)]
        plans = [
            reduce_turns(
                links, me, locals_[i // 2], i % 2 * 64, summed.at[i // 2, HALVES[i % 2]], results.at[i // 2, HALVES[i % 2]], lands[6 * i : 6 * i + 6]
            )
            for i in range(2 * units)
        ]
        schedule = list(zip(BACK_FACTORS, factors_turns(links, me, factors, factor_group, factor_all)))
        schedule = [(0, begin)] + schedule + timed(plans, *BACK_REDUCE)
        links.ends += [end]
        host = Host(links, placed(schedule), D // 128, 4)
    else:
        (grad_ref, kt_ref, dqt_ref), host = refs, Idle()
    rows = k_ref.shape[0]
    block = min(ATTENTION_ROWS, rows)
    low = lax.broadcasted_iota(jnp.int32, (1, 128), 1) < HEAD_DIM
    grads = go_ref[...]
    product = pltpu.roll(-(grads.astype(jnp.float32) * out_ref[...].astype(jnp.float32)), HEAD_DIM, 1).astype(jnp.bfloat16)
    kt_ref[...] = k_ref[...].astype(jnp.float32).T.astype(jnp.bfloat16)
    given = [jnp.where(own, grads, product) for own in (low, ~low)]
    for at, first in enumerate(range(0, rows, block)):
        here = pl.ds(first, block)
        dks, dvs = [], []
        for head, own in enumerate((low, ~low)):
            host.turn(2 * at + head)
            keys = jnp.where(own, k_ref[here, :], kl_ref[here, :])
            vals = jnp.where(own, v_ref[here, :], jnp.bfloat16(1))
            probs = jnp.exp(nt(keys, qa_ref[head]))
            slopes = nt(vals, given[head])
            moved = (probs * slopes).astype(jnp.bfloat16)
            dvs.append(nn(probs.astype(jnp.bfloat16), grads))
            dks.append(nn(moved, qa_ref[head]))
            part = nn(kt_ref[head * HEAD_DIM : (head + 1) * HEAD_DIM, here], moved)
            where = pl.ds(head * HEAD_DIM, HEAD_DIM)
            if first == 0:
                dqt_ref[where, :] = part
            else:
                dqt_ref[where, :] += part
        grad_ref[1, here, :] = jnp.where(low, dks[0], dks[1]).astype(jnp.bfloat16)
        grad_ref[2, here, :] = jnp.where(low, dvs[0], dvs[1]).astype(jnp.bfloat16)
    grad_ref[0] = (dqt_ref[...].T * HEAD_DIM**-0.5).astype(jnp.bfloat16)
    host.finish()


def attend_back(projected, key_lanes, asked, attn_out, grad_attn, groups=(), small=None, factors=None):
    rows, pairs = projected.shape[0], D // 128
    spec = lambda shift: pl.BlockSpec((rows, 128), lambda i: (0, i + shift))
    same = pl.BlockSpec((rows, 128), lambda i: (0, 0))
    two = pl.BlockSpec((2, rows, 128), lambda i: (i, 0, 0))
    inputs = [(projected, spec(pairs)), (projected, spec(2 * pairs)), (key_lanes, same), (asked, two), (attn_out, spec(0)), (grad_attn, spec(0))]
    outputs = [((3, rows, D), jnp.bfloat16, pl.BlockSpec((3, rows, 128), lambda i: (0, 0, i)))]
    scratch = [pltpu.VMEM((128, rows), jnp.bfloat16), pltpu.VMEM((128, rows), jnp.float32)]
    counts = [g.shape[0] for g in groups]
    units = sum(counts)
    if units:
        inputs += [(g, ANY) for g in groups] + [(small, ANY), (factors, ANY)]
        slots, width = factors.shape
        outputs += [((units, 128, D), jnp.bfloat16, ANY), ((32,) + small.shape[1:], small.dtype, ANY)]
        outputs += [((4 * slots, width), factors.dtype, ANY), ((32 * slots, width), factors.dtype, ANY)]
        scratch += [pltpu.VMEM((units, 128, D), jnp.bfloat16)] + [land for _ in range(2 * units) for land in reduce_lands(64)]
        scratch += semaphores(31 + FACTOR_HOPS + 2 * REDUCE_HOPS * units, 1 + FACTOR_NEAR + 2 * REDUCE_NEAR * units)
    return call(functools.partial(attend_back_kernel, counts), (pairs,), inputs, outputs, scratch)


def before_kernel(attn_ref, tok_ref, cot_ref, wout_ref, bout_ref, scale_ref, shift_ref, live_ref, middle_ref, hidden_ref, two_ref, gbdown_ref):
    r = pl.program_id(0)
    rows = tok_ref.shape[0]
    units = rows // UNIT

    @pl.when(r == 0)
    def _():
        gbdown_ref[...] = jnp.zeros_like(gbdown_ref)

    middle_ref[...] = nn(attn_ref[...], wout_ref[0]) + bout_ref[...].astype(jnp.float32)
    for i in range(units):
        u = r * units + i
        at = pl.ds(i * UNIT, UNIT)
        live = live_ref[pl.ds(u, 1), :]
        value = tok_ref[at, :].astype(jnp.float32) + live * middle_ref[at, :]
        middle_ref[at, :] = value
        normed, _ = normalize(value)
        hidden_ref[at, :] = (normed * (1.0 + scale_ref[pl.ds(u, 1), :]) + shift_ref[pl.ds(u, 1), :]).astype(jnp.bfloat16)
        grad = (live * cot_ref[at, :].astype(jnp.float32)).astype(jnp.bfloat16)
        two_ref[at, :] = grad
        gbdown_ref[...] += jnp.sum(grad.astype(jnp.float32), axis=0, keepdims=True)


def before_mlp(attn_out, tokens, cotangent, weights, b_out, scale, shift, live):
    rows = tokens.shape[0]
    block = pl.BlockSpec((256, D), lambda r: (r, 0))
    once = lambda shape: pl.BlockSpec(shape, lambda r: (0,) * len(shape))
    units = once((rows // UNIT, D))
    return call(
        before_kernel,
        (rows // 256,),
        [(attn_out, block), (tokens, block), (cotangent, block), (weights, once((1, D, D))), (b_out, once((1, D))), (scale, units), (shift, units), (live, units)],
        [((rows, D), jnp.float32, block), ((rows, D), jnp.bfloat16, block), ((rows, D), jnp.bfloat16, block), ((1, D), jnp.float32, once((1, D)))],
    )


def mlp_kernel(early, hidden, two, bup_ref, weights, *refs):
    j = pl.program_id(0)
    rows = hidden.shape[0]
    late = FF_BLOCKS - early
    if late:
        shards, acc, back, gbup_ref, grads_ref, results, act, pre, held, made, summed, *refs = refs
        lands, sems = refs[: 20 * early], refs[20 * early :]
    else:
        acc, back, gbup_ref, grads_ref, act, pre, held, made, *sems = refs
    slots = made.shape[0]
    me, links = place(), Links(*sems)
    fetch = [[Near(links, lambda b=b, w=w: weights.at[1 + 2 * b + w], lambda b=b, w=w: held.at[b, w]) for w in (0, 1)] for b in range(early)]
    store = [Near(links, lambda b=b: made.at[b % slots], lambda b=b: grads_ref.at[b - FF_BLOCKS + grads_ref.shape[0]]) for b in range(FF_BLOCKS)]
    kept_blocks = range(FF_BLOCKS - grads_ref.shape[0], FF_BLOCKS)
    if late:
        gathers, reduces = [], []
        for i in range(4 * late):
            b, w, half = early + i // 4, i // 2 % 2, HALVES[i % 2]
            gathers.append(gather_turns(links, me, shards.at[i // 2, half], held.at[b, w], 128 if i % 2 else 256, half.start))
        for i in range(4 * early):
            b, w, half = i // 4, i // 2 % 2, HALVES[i % 2]
            reduces.append(
                reduce_turns(
                    links, me, made.at[b % slots, w], half.start, summed.at[2 * b + w, half], results.at[2 * b + w, half], lands[5 * i : 5 * i + 5]
                )
            )
        schedule = timed(gathers, *MLP_GATHER) + timed(reduces, *MLP_REDUCE)
        host = Host(links, placed(schedule), FF_BLOCKS, 16)
    else:
        host = Idle()

    @pl.when(j == 0)
    def _():
        for pair in fetch:
            for near in pair:
                near.start()

    host.turn(0)
    for b in range(early):

        @pl.when(j == b)
        def _():
            for near in fetch[b]:
                near.arrived()

    gbup_ref[...] = jnp.zeros_like(gbup_ref)
    up, down = held.at[j, 0], held.at[j, 1]
    block = rows // 4
    for r in range(4):
        if r:
            host.turn(2 * r)
        here = pl.ds(r * block, block)
        value, slope = gelu_both(nn(hidden[here, :], up[...]) + bup_ref[0].astype(jnp.float32))
        value = value.astype(jnp.bfloat16)
        grad = (nt(two[here, :], down[...]) * slope).astype(jnp.bfloat16)
        act[here, :] = value
        pre[here, :] = grad
        gbup_ref[0] += jnp.sum(grad.astype(jnp.float32), axis=0, keepdims=True)
        host.turn(2 * r + 1)
        forward, backward = nn(value, down[...]), nt(grad, up[...])

        @pl.when(j == 0)
        def _():
            acc[here, :] = forward
            back[here, :] = backward

        @pl.when(j > 0)
        def _():
            acc[here, :] += forward
            back[here, :] += backward

    slot = lax.rem(j, slots)
    for r in range(4):
        here = pl.ds(r * 256, 256)
        for w, (left, right) in enumerate(((hidden, pre), (act, two))):
            host.turn(8 + 2 * r + w)
            value = tn(left[:, here], right[...]).astype(jnp.bfloat16)
            for half in (0, 1):
                made[slot, w, 2 * r + half] = value[half * 128 : half * 128 + 128]
    for b in kept_blocks:
        pl.when(j == b)(store[b].start)

    @pl.when(j == FF_BLOCKS - 1)
    def _():
        for b in kept_blocks:
            store[b].arrived()

    host.finish()


def feed_forward(hidden, two, weights, b_up, shards=None):
    rows = hidden.shape[0]
    once = lambda shape: pl.BlockSpec(shape, lambda j: (0, 0), pipeline_mode=pl.Buffered(1))
    whole = once((rows, D))
    row = pl.BlockSpec((1, 1, D), lambda j: (j, 0, 0))
    f32, b16 = jnp.float32, jnp.bfloat16
    early = FF_BLOCKS if shards is None else EARLY
    late = FF_BLOCKS - early
    kept = late or FF_BLOCKS
    inputs = [(hidden, whole), (two, whole), (b_up, row), (weights, ANY)]
    outputs = [((rows, D), f32, whole), ((rows, D), f32, whole), ((FF_BLOCKS, 1, D), f32, row), ((kept, 2, 8, 128, D), b16, ANY)]
    slots = 2 if late else FF_BLOCKS
    scratch = [
        pltpu.VMEM((rows, D), b16), pltpu.VMEM((rows, D), b16), pltpu.VMEM((FF_BLOCKS, 2, D, D), b16), pltpu.VMEM((slots, 2, 8, 128, D), b16),
    ]
    hops, near = 1, 2 * early + FF_BLOCKS
    if late:
        inputs += [(shards, ANY)]
        outputs += [((2 * early, 128, D), b16, ANY)]
        scratch += [pltpu.VMEM((2 * early, 128, D), b16)] + [land for _ in range(4 * early) for land in reduce_lands(64, far=False)]
        hops = 4 * late * GATHER_HOPS + 4 * early * REDUCE_HOPS
        near += 4 * late * GATHER_NEAR + 4 * early * REDUCE_NEAR
    return call(functools.partial(mlp_kernel, early), (FF_BLOCKS,), inputs, outputs, scratch + semaphores(hops, near))


def after_kernel(
    middle_ref, acc_ref, back_ref, cot_ref, attn_ref, wout_ref, bdown_ref, scale_ref, live_ref,
    out_ref, mid_grad_ref, attn_grad_ref, gout_ref, gbout_ref, gscale_ref, gshift_ref, one_ref, total_ref,
):
    r = pl.program_id(0)
    rows = cot_ref.shape[0]
    units = rows // UNIT

    @pl.when(r == 0)
    def _():
        gbout_ref[...] = jnp.zeros_like(gbout_ref)
        total_ref[...] = jnp.zeros_like(total_ref)

    for i in range(units):
        u = r * units + i
        at = pl.ds(i * UNIT, UNIT)
        live = live_ref[pl.ds(u, 1), :]
        value = middle_ref[at, :]
        out_ref[at, :] = (value + live * (acc_ref[at, :] + bdown_ref[...].astype(jnp.float32))).astype(jnp.bfloat16)
        normed, inverse = normalize(value)
        grad = back_ref[at, :]
        gshift_ref[pl.ds(u, 1), :] = jnp.sum(grad, axis=0, keepdims=True)
        gscale_ref[pl.ds(u, 1), :] = jnp.sum(grad * normed, axis=0, keepdims=True)
        passed = cot_ref[at, :].astype(jnp.float32) + norm_back(grad * (1.0 + scale_ref[pl.ds(u, 1), :]), normed, inverse)
        mid_grad_ref[at, :] = passed
        one = (live * passed).astype(jnp.bfloat16)
        one_ref[at, :] = one
        gbout_ref[...] += jnp.sum(one.astype(jnp.float32), axis=0, keepdims=True)
    attn_grad_ref[...] = nt(one_ref[...], wout_ref[0]).astype(jnp.bfloat16)
    total_ref[...] += tn(attn_ref[...], one_ref[...])

    @pl.when(r == pl.num_programs(0) - 1)
    def _():
        for i in range(8):
            gout_ref[0, i] = total_ref[i * 128 : i * 128 + 128, :].astype(jnp.bfloat16)


def after_mlp(middle, acc, back, cotangent, attn_out, weights, b_down, scale, live):
    rows = middle.shape[0]
    block = pl.BlockSpec((256, D), lambda r: (r, 0))
    once = lambda shape: pl.BlockSpec(shape, lambda r: (0,) * len(shape))
    units, row = once((rows // UNIT, D)), once((1, D))
    f32, b16 = jnp.float32, jnp.bfloat16
    return call(
        after_kernel,
        (rows // 256,),
        [
            (middle, block), (acc, block), (back, block), (cotangent, block), (attn_out, block), (weights, once((1, D, D))),
            (b_down, row), (scale, units), (live, units),
        ],
        [
            ((rows, D), b16, block), ((rows, D), f32, block), ((rows, D), b16, block), ((1, 8, 128, D), b16, once((1, 8, 128, D))), ((1, D), f32, row),
            ((rows // UNIT, D), f32, units), ((rows // UNIT, D), f32, units),
        ],
        [pltpu.VMEM((256, D), b16), pltpu.VMEM((D, D), f32)],
    )


def head_kernel(tok_ref, scale_ref, shift_ref, w_ref, hidden_ref, out_ref):
    rows = tok_ref.shape[0]

    @pl.when(pl.program_id(0) == 0)
    def _():
        def unit(u):
            at = pl.ds(pl.multiple_of(u * UNIT, UNIT), UNIT)
            normed, _ = normalize(tok_ref[at, :].astype(jnp.float32))
            hidden_ref[at, :] = (normed * (1.0 + scale_ref[pl.ds(u, 1), :]) + shift_ref[pl.ds(u, 1), :]).astype(jnp.bfloat16)

        loop(rows // UNIT, unit)

    def block(r):
        here = pl.ds(pl.multiple_of(r * ROWS, ROWS), ROWS)
        out_ref[here, :] = nn(hidden_ref[here, :], w_ref[0]).astype(jnp.bfloat16)

    loop(rows // ROWS, block)


def project_in(tokens, scale, shift, w_qkv):
    rows = tokens.shape[0]
    whole = lambda shape: pl.BlockSpec(shape, lambda j: (0, 0))
    return pl.pallas_call(
        head_kernel,
        grid=(3,),
        out_shape=[jax.ShapeDtypeStruct((rows, D), jnp.bfloat16), jax.ShapeDtypeStruct((rows, 3 * D), jnp.bfloat16)],
        in_specs=[whole((rows, D)), whole((rows // UNIT, D)), whole((rows // UNIT, D)), pl.BlockSpec((1, D, D), lambda j: (j, 0, 0))],
        out_specs=[whole((rows, D)), pl.BlockSpec((rows, D), lambda j: (0, j))],
        compiler_params=pltpu.CompilerParams(vmem_limit_bytes=VMEM_LIMIT),
    )(tokens, scale, shift, w_qkv)


def tail_kernel(shared, grad_ref, hidden_ref, w_ref, tok_ref, scale_ref, *refs):
    p = pl.program_id(0)
    rows = tok_ref.shape[0]
    if shared:
        table_ref, results, gtok_ref, gscale_ref, gshift_ref, factor_group, factor_all, back, gw, summed, factors, *refs = refs
        lands, sems = refs[:30], refs[30:]
        me, links = place(), Links(*sems)
        schedule = []
        for i in range(6):
            half = HALVES[i % 2]
            unit = reduce_turns(
                links, me, gw.at[i // 2], half.start, summed.at[i // 2, half], results.at[i // 2, half], lands[5 * i : 5 * i + 5]
            )
            schedule += timed([unit], 0, TAIL_REDUCE, 4 * (i // 2 + 1) + 2 * (i % 2))
        turns = placed(schedule)
        host = Host(links, {h: t for h, t in turns.items() if h < 24}, 6, 4)
        rest = [turns[h] for h in sorted(turns) if h >= 24]
        spread = factors_turns(links, me, factors, factor_group, factor_all)
    else:
        gw, gtok_ref, gscale_ref, gshift_ref, back = refs
        host, rest = Idle(), []

    def products(r):
        value = tn(hidden_ref[:, r * 256 : r * 256 + 256], grad_ref[0]).astype(jnp.bfloat16)
        for half in (0, 1):
            gw[p if shared else 0, 2 * r + half] = value[half * 128 : half * 128 + 128]

    def way_back(r):
        here = pl.ds(r * (rows // 4), rows // 4)
        part = nt(grad_ref[0, here, :], w_ref[0])

        @pl.when(p == 3)
        def _():
            back[here, :] = part

        @pl.when(p > 3)
        def _():
            back[here, :] += part

    for r in range(4):
        host.turn(r)
        pl.when(p < 3)(functools.partial(products, r))
        pl.when(p >= 3)(functools.partial(way_back, r))

    @pl.when(p == pl.num_programs(0) - 1)
    def _():
        def unit(u):
            at = pl.ds(pl.multiple_of(u * UNIT, UNIT), UNIT)
            normed, inverse = normalize(tok_ref[at, :].astype(jnp.float32))
            grad = back[at, :]
            gshift_ref[pl.ds(u, 1), :] = jnp.sum(grad, axis=0, keepdims=True)
            gscale_ref[pl.ds(u, 1), :] = jnp.sum(grad * normed, axis=0, keepdims=True)
            passed = norm_back(grad * (1.0 + scale_ref[pl.ds(u, 1), :]), normed, inverse)
            gtok_ref[at, :] = passed.astype(jnp.bfloat16)

        for quarter in range(4):
            if quarter < len(rest):
                run(rest[quarter])
            loop(rows // UNIT // 4, lambda i: unit(quarter * (rows // UNIT // 4) + i))
        if shared:
            table = table_ref[...].astype(jnp.bfloat16)
            for i, ref in enumerate((gscale_ref, gshift_ref)):
                factors[:, i * D : (i + 1) * D] = exact(table, ref[...]).astype(jnp.bfloat16)
            left = rest[4:]
            for i in range(max(len(left), len(spread))):
                if i < len(spread):
                    spread[i]()
                if i < len(left):
                    run(left[i])

    host.finish()


def project_back(grad_proj, hidden, w_qkv, tokens, scale, table=None):
    rows = tokens.shape[0]
    once = lambda shape: pl.BlockSpec(shape, lambda p: (0, 0), pipeline_mode=pl.Buffered(1))
    units, whole = once((rows // UNIT, D)), once((rows, D))
    f32, b16 = jnp.float32, jnp.bfloat16
    block = pl.BlockSpec((1, rows, D), lambda p: (lax.rem(p, 3), 0, 0))
    inputs = [
        (grad_proj, block), (hidden, whole), (w_qkv, pl.BlockSpec((1, D, D), lambda p: (jnp.maximum(p - 3, 0), 0, 0))), (tokens, whole), (scale, units),
    ]
    outputs = [((rows, D), b16, whole), ((rows // UNIT, D), f32, units), ((rows // UNIT, D), f32, units)]
    scratch = [pltpu.VMEM((rows, D), f32)]
    shared = table is not None
    if shared:
        slots = table.shape[0]
        inputs += [(table, once(table.shape))]
        outputs = [((3, 128, D), b16, ANY)] + outputs
        outputs += [((4 * slots, 2 * D), b16, ANY), ((32 * slots, 2 * D), b16, ANY)]
        scratch += [pltpu.VMEM((3, 8, 128, D), b16), pltpu.VMEM((3, 128, D), b16), pltpu.VMEM((slots, 2 * D), b16)] + [land for _ in range(6) for land in reduce_lands(64, far=False)]
        scratch += semaphores(6 * REDUCE_HOPS + FACTOR_HOPS, 6 * REDUCE_NEAR + FACTOR_NEAR)
    else:
        outputs = [((3, 8, 128, D), b16, pl.BlockSpec((1, 8, 128, D), lambda p: (jnp.minimum(p, 2), 0, 0, 0)))] + outputs
    return call(functools.partial(tail_kernel, shared), (6,), inputs, outputs, scratch)


def tuned(sizes):
    return sizes == (4, 8)


def blocks_of(columns):
    return columns.reshape(columns.shape[0], FF_BLOCKS, -1).transpose(1, 0, 2)


def local(
    sizes, tokens, lengths, buckets, w_mod, b_mod, w_qkv, w_out, b_out, w_up, b_up, w_down, b_down, cotangent,
):
    rows, slots, n = tokens.shape[0], lengths.shape[1], sizes[1]
    own = tuned(sizes)
    segment, live, unit_table = layout(lengths[0], rows)
    feats = time_features(buckets[0]).astype(jnp.bfloat16)
    whole = lambda array: lax.all_gather(array, "fsdp", axis=0, tiled=True)
    if own:
        packed = jnp.concatenate([b_mod, b_out, b_up, b_down]).reshape(-1, 128)
        packed = jnp.pad(packed, ((0, 16 - packed.shape[0]), (0, 0)))
        by_owner = feats.reshape(slots, n, 128).transpose(1, 0, 2)
        small = jnp.concatenate([jnp.broadcast_to(packed, (n, 16, 128)), by_owner], axis=1)
        small_all, full_qkv, hidden_attn, projected, per_unit = first_all(small, w_mod, w_qkv, tokens, unit_table)
        of_group = lax.dynamic_slice(small_all, (lax.axis_index("dp") * n, 0, 0), (n, 16, 128))
        full_bout, full_bdown = of_group[:, 4].reshape(1, -1), of_group[:, 9].reshape(1, -1)
        full_bup = of_group[:, 5:9].transpose(1, 0, 2).reshape(FF_BLOCKS, 1, -1)
        every_feats = small_all[:, 16:].reshape(sizes[0], n, slots, 128).transpose(1, 0, 2, 3).reshape(-1, 128)
    else:
        full_mod, full_qkv, full_bmod, full_bout, full_bup, full_bdown = [whole(a) for a in (w_mod, w_qkv, b_mod, b_out, b_up, b_down)]
        full_bout, full_bdown, full_bup = full_bout[None], full_bdown[None], full_bup.reshape(FF_BLOCKS, 1, -1)
        every_feats = lax.all_gather(feats, ("dp", "fsdp"), axis=0, tiled=True)
        every_feats = lax.dynamic_slice(every_feats, (0, lax.axis_index("fsdp") * (D // n)), (every_feats.shape[0], D // n))
        modulation = jnp.dot(feats, full_mod, preferred_element_type=jnp.float32) + full_bmod
        per_unit = jnp.dot(unit_table, modulation, precision=HIGHEST)
        full_qkv = full_qkv.reshape(D, 3, D).transpose(1, 0, 2)
        hidden_attn, projected = project_in(tokens, per_unit[:, :D], per_unit[:, D : 2 * D], full_qkv)
    scale_one, _, scale_two, shift_two = [per_unit[:, i * D : (i + 1) * D] for i in range(4)]
    live_units = jnp.broadcast_to(live[:, None], (rows // UNIT, D))
    query_lanes, key_lanes = attention_lanes(jnp.repeat(segment, UNIT), slots)
    if own:
        ups = w_up.reshape(-1, n, FF_BLOCKS, 128).transpose(2, 0, 1, 3).reshape(FF_BLOCKS, 1, -1, D)
        downs = w_down.reshape(FF_BLOCKS, 1, -1, D)
        pairs = jnp.concatenate([ups, downs], axis=1).reshape(2 * FF_BLOCKS, -1, D)
        attn_out, asked, weights = attend(projected, query_lanes, key_lanes, jnp.concatenate([w_out[None], pairs[: 2 * EARLY]]))
        late = pairs[2 * EARLY :]
    else:
        attn_out, asked = attend(projected, query_lanes, key_lanes)
        pairs = jnp.stack([blocks_of(whole(w_up)), whole(w_down).reshape(FF_BLOCKS, D, D)], axis=1)
        weights, late = jnp.concatenate([whole(w_out)[None], pairs.reshape(2 * FF_BLOCKS, D, D)]), None
    middle, hidden_mlp, grad_two, grad_b_down = before_mlp(
        attn_out, tokens, cotangent, weights, full_bout, scale_two, shift_two, live_units
    )
    forward, backward, grad_b_up, grad_pairs, *totals_early = feed_forward(hidden_mlp, grad_two, weights, full_bup, late)
    output, grad_mid, grad_attn, grad_w_out, grad_b_out, grad_scale_two, grad_shift_two = after_mlp(
        middle, forward, backward, cotangent, attn_out, weights, full_bdown, scale_two, live_units
    )

    def factors_of(first, second):
        return jnp.dot(unit_table.T, jnp.concatenate([first, second], axis=1), precision=HIGHEST).astype(jnp.bfloat16)

    mod_two = factors_of(grad_scale_two, grad_shift_two)
    if own:
        sums = [grad_b_out.reshape(n, 1, 128), grad_b_up.reshape(FF_BLOCKS, n, 128).transpose(1, 0, 2), grad_b_down.reshape(n, 1, 128)]
        small = jnp.pad(jnp.concatenate(sums, axis=1), ((0, 0), (0, 2), (0, 0)))
        grad_proj, totals, small_all, _, mod_two = attend_back(
            projected, key_lanes, asked, attn_out, grad_attn, (grad_pairs.reshape(-1, 8, 128, D), grad_w_out), small, mod_two
        )
        total = jnp.sum(small_all, axis=0)
        sum_bout, sum_bup, sum_bdown = total[0], total[1:5].reshape(-1), total[5]
    else:
        grad_proj = attend_back(projected, key_lanes, asked, attn_out, grad_attn)[0]
    qkv_grads, through_norm, grad_scale_one, grad_shift_one, *factors = project_back(
        grad_proj, hidden_attn, full_qkv, tokens, scale_one, unit_table.T if own else None
    )
    grad_tokens = grad_mid + through_norm.astype(jnp.float32)
    if own:
        mod_one = factors[1]
    else:
        mod_one = factors_of(grad_scale_one, grad_shift_one)
        mod_one, mod_two = [lax.all_gather(m, ("dp", "fsdp"), axis=0, tiled=True) for m in (mod_one, mod_two)]
    sum_mod = jnp.concatenate(
        [jnp.einsum("sd,sc->dc", every_feats, m, preferred_element_type=jnp.float32) for m in (mod_one, mod_two)], axis=1
    )
    position, share = lax.axis_index("fsdp"), 4 * D // n
    chosen = jnp.where(position < n // 2, mod_one, mod_two)
    sum_bmod = jnp.sum(
        lax.dynamic_slice(chosen, (0, position % (n // 2) * share), (chosen.shape[0], share)), axis=0, dtype=jnp.float32
    )
    if own:
        totals, qkv_grads = totals.astype(jnp.float32), qkv_grads.astype(jnp.float32)
        pairs = jnp.concatenate([totals_early[0].astype(jnp.float32), totals[:-1]]).reshape(FF_BLOCKS, 2, 128, D)
        sum_up = pairs[:, 0].reshape(FF_BLOCKS, -1, n, 128).transpose(1, 2, 0, 3).reshape(w_up.shape)
        sum_down = pairs[:, 1].reshape(w_down.shape)
        sum_out = totals[-1]
        sum_qkv = qkv_grads.transpose(1, 0, 2).reshape(w_qkv.shape)
    else:
        summed = lambda a: lax.psum(lax.psum_scatter(a, "fsdp", scatter_dimension=0, tiled=True), "dp").astype(jnp.float32)
        sum_up = summed(grad_pairs[:, 0].reshape(FF_BLOCKS, D, D).transpose(1, 0, 2).reshape(D, -1))
        sum_down = summed(grad_pairs[:, 1].reshape(-1, D))
        sum_out, sum_qkv = summed(grad_w_out.reshape(D, D)), summed(qkv_grads.reshape(3, D, D).transpose(1, 0, 2).reshape(D, -1))
        sum_bout, sum_bup, sum_bdown = [summed(a.reshape(-1)) for a in (grad_b_out, grad_b_up, grad_b_down)]
    return output, grad_tokens, sum_mod, sum_bmod, sum_qkv, sum_out, sum_bout, sum_up, sum_bup, sum_down, sum_bdown


def solution(mesh):
    sizes = (mesh.shape["dp"], mesh.shape["fsdp"])
    rows, cut_rows, vector = P(("dp", "fsdp"), None), P("fsdp", None), P("fsdp")
    return jax.shard_map(
        functools.partial(local, sizes),
        mesh=mesh,
        in_specs=(rows, rows, rows, cut_rows, vector, cut_rows, cut_rows, vector, cut_rows, vector, cut_rows, vector, rows),
        out_specs=(rows, rows, cut_rows, vector, cut_rows, cut_rows, vector, cut_rows, vector, cut_rows, vector),
        check_vma=False,
    )
```

```python
import functools
import math

import jax
import jax.numpy as jnp
from jax import lax
from jax.experimental import pallas as pl
from jax.experimental.pallas import tpu as pltpu
from jax.sharding import PartitionSpec as P

D = 1024
HEADS = 16
HEAD_DIM = 64
EPSILON = 1e-05
UNIT = 64
ROWS = 512
ATTENTION_ROWS = 512
FF_BLOCKS = 4
EARLY = 2
LSE_LANE = 24
ATTEND_GATHER = (2.5, (0, 4, 8, 11, 13))
MLP_GATHER = ((0, 3, 6, 9, 12, 15, 19, 23), (0, 7, 13, 19, 22))
MLP_REDUCE = ((18, 22, 26, 30, 34, 38, 42, 46), (0, 3, 8, 14, 20, 24, 26))
BACK_REDUCE = (2.6, (0, 2, 5, 8, 11, 13, 15))
BACK_FACTORS = (1, 4, 8, 12, 16, 19)
TAIL_REDUCE = (0, 2, 6, 11, 16, 19, 21)
VMEM_LIMIT = 62 * 2**20
HIGHEST = lax.Precision.HIGHEST
MESH = pl.DeviceIdType.MESH


def layout(lengths, tok_rows):
    slots = lengths.shape[0]
    upto = jnp.arange(slots)[:, None] <= jnp.arange(slots)[None, :]
    seq_ends = jnp.sum(jnp.where(upto, lengths[:, None], 0), axis=0, dtype=jnp.int32)
    position = jnp.arange(0, tok_rows, UNIT, dtype=jnp.int32)
    segment = jnp.sum((position[:, None] >= seq_ends[None, :]).astype(jnp.int32), axis=1, dtype=jnp.int32)
    unit_table = (segment[:, None] == jnp.arange(slots, dtype=jnp.int32)[None, :]).astype(jnp.float32)
    return segment, (segment < slots).astype(jnp.float32), unit_table


def time_features(buckets):
    half_width = D // 2
    frequency = jnp.exp(-math.log(10000.0) * jnp.arange(half_width, dtype=jnp.float32) / half_width)
    angles = buckets.astype(jnp.float32)[:, None] * frequency[None, :]
    return jnp.concatenate([jnp.sin(angles), jnp.cos(angles)], axis=1)


def place():
    dp, fsdp = lax.axis_index("dp"), lax.axis_index("fsdp")
    return dp // 2, dp % 2, fsdp // 2, fsdp % 2


def device(x, core, z, y):
    return (x * 2 + core, z * 2 + y)


class Hop:
    def __init__(self, links, src, dst, target):
        self.links, self.src, self.dst, self.target, self.gone = links, src, dst, target, False
        self.slot = links.used
        links.used += 1
        links.hops.append(self)

    def made(self):
        return pltpu.make_async_remote_copy(
            src_ref=self.src(),
            dst_ref=self.dst(),
            send_sem=self.links.send_sems.at[self.slot],
            recv_sem=self.links.recv_sems.at[self.slot],
            device_id=self.target(),
            device_id_type=MESH,
        )

    def start(self):
        self.made().start()

    def arrived(self):
        self.made().wait_recv()

    def left(self):
        self.gone = True
        self.made().wait_send()


class Near:
    def __init__(self, links, src, dst):
        self.links, self.src, self.dst = links, src, dst
        self.slot = links.used_near
        links.used_near += 1

    def made(self):
        return pltpu.make_async_copy(self.src(), self.dst(), self.links.near_sems.at[self.slot])

    def start(self):
        self.made().start()

    def arrived(self):
        self.made().wait()


class Links:
    def __init__(self, send_sems, recv_sems, near_sems):
        self.send_sems, self.recv_sems, self.near_sems = send_sems, recv_sems, near_sems
        self.used, self.used_near, self.hops, self.ends = 0, 0, [], []

    def drain(self):
        for hop in self.hops:
            if not hop.gone:
                hop.left()
        for end in self.ends:
            end()


def lanes(at, size):
    return pl.ds(pl.multiple_of(at, 128), size)


def lines(at, size):
    return pl.ds(pl.multiple_of(at, 16), size)


HALVES = (pl.ds(0, 64), pl.ds(64, 64))


def gather_turns(links, me, shard, whole, outer, at=None):
    x, core, z, y = me
    rows, width = shard.shape
    half = width // 2
    inner = half - 2 * outer
    own = lanes(core * half + x * outer, outer + inner)
    crossing = lanes(core * half + x * (outer + inner), outer)
    full = lanes(core * half, half)

    def place_of(index):
        return lines(index * rows, rows) if at is None else lines(index * 128 + at, rows)

    mine = place_of(z * 2 + y)
    blocks = {}
    for k in range(4):
        source = ((z - k + 4) % 4) * 2
        blocks["z", k], blocks["y", k] = place_of(source + y), place_of(source + 1 - y)
    to_z = {k: device(x, core, (z + k) % 4, y) for k in (1, 2, 3)}
    to_y, to_x, to_core = device(x, core, z, 1 - y), device(1 - x, core, z, y), device(x, 1 - core, z, y)

    def from_shard(target):
        return Hop(links, lambda: shard.at[:, own], lambda: whole.at[mine, own], lambda: target)

    def pass_on(way, k, columns, target):
        def ref():
            return whole.at[blocks[way, k], columns]

        return Hop(links, ref, ref, lambda: target)

    keep = Near(links, lambda: shard, lambda: whole.at[mine, :])
    along_z = {k: from_shard(to_z[k]) for k in (1, 2, 3)}
    along_y = {0: from_shard(to_y)}
    for k in (1, 2, 3):
        along_y[k] = pass_on("z", k, own, to_y)
    order = [("z", 1), ("y", 0), ("z", 2), ("y", 1), ("z", 3), ("y", 2), ("y", 3)]
    crossed = [pass_on(way, k, crossing, to_x) for way, k in order] if outer else None
    handed = [pass_on(way, k, full, to_core) for way, k in order]

    def first():
        for k in (1, 2, 3):
            along_z[k].start()
        along_y[0].start()
        keep.start()

    def arrive(j):
        way, k = order[j]
        (along_z if way == "z" else along_y)[k].arrived()
        if way == "z":
            along_y[k].start()
        (crossed if outer else handed)[j].start()

    def hand_on(j):
        if outer:
            crossed[j].arrived()
            handed[j].start()

    def last():
        for hop in handed:
            hop.arrived()
        keep.arrived()

    return [
        first,
        lambda: [arrive(j) for j in (1, 0, 2, 4)],
        lambda: [arrive(j) for j in (3, 5, 6)] + [hand_on(j) for j in (1, 0, 2, 4)],
        lambda: [hand_on(j) for j in (3, 5, 6)],
        last,
    ]


GATHER_HOPS, GATHER_NEAR = 3 + 4 + 7 + 7, 1


def reduce_lands(rows, width=1024, far=True):
    half = width // 2
    outer = half // 4
    shapes = [
        (4, 2, rows, half), (4, 2, rows, outer), (4, rows, half - outer), (3, rows, half - outer), (rows, half - outer),
    ]
    if far:
        shapes.append((4, 2, rows, half))
    return [pltpu.VMEM(s, jnp.bfloat16) for s in shapes]


def reduce_turns(links, me, local, at, result, out, lands):
    x, core, z, y = me
    total, from_x, from_y, from_z, from_last = lands[:5]
    far = lands[5] if len(lands) > 5 else None
    rows, width = result.shape
    half = width // 2
    outer = half // 4
    wide = half - outer

    own, kept, given = lanes(x * outer, wide), lanes(x * wide, outer), lanes((1 - x) * wide, outer)
    sides, here = {True: lanes(core * half, half), False: lanes((1 - core) * half, half)}, pl.ds(at, rows)
    owners_of = [pl.ds(((z + t + 1) % 4) * 2, 2) for t in range(4)]
    other = 1 - y
    at_core, at_x, at_y = device(x, 1 - core, z, y), device(1 - x, core, z, y), device(x, core, z, other)
    at_z = [device(x, core, (z + t + 1) % 4, y) for t in range(3)]

    def owners(t, ours):
        return local.at[owners_of[t], here, sides[ours]]

    turns4 = range(4)
    load = [Near(links, lambda t=t: owners(t, True), lambda t=t: far.at[t]) for t in turns4] if far is not None else []
    to_core = [Hop(links, lambda t=t: owners(t, False), lambda t=t: total.at[t], lambda: at_core) for t in turns4]
    to_x = [Hop(links, lambda t=t: total.at[t, :, :, given], lambda t=t: from_x.at[t], lambda: at_x) for t in turns4]
    to_y = [Hop(links, lambda t=t: total.at[t, other, :, own], lambda t=t: from_y.at[t], lambda: at_y) for t in turns4]
    to_z = [Hop(links, lambda t=t: total.at[t, y, :, own], lambda t=t: from_z.at[t], lambda t=t: at_z[t]) for t in range(3)]
    to_last = Hop(links, lambda: total.at[3, y, :, own], lambda: from_last, lambda: at_x)
    mine = lambda: result.at[:, sides[True]]
    to_final = Hop(links, mine, mine, lambda: at_core)
    store = Near(links, lambda: result, lambda: out)
    links.ends.append(store.arrived)

    def add(index, landed):
        total[index] = (total[index].astype(jnp.float32) + landed.astype(jnp.float32)).astype(total.dtype)

    def first():
        for t in turns4:
            to_core[t].start()
        for near in load:
            near.start()

    def core_turn():
        for t in turns4:
            to_core[t].arrived()
            if far is None:
                to_core[t].left()
                add(t, owners(t, True)[...])
            else:
                load[t].arrived()
                add(t, far[t])
            to_x[t].start()

    def x_turn():
        for t in turns4:
            to_x[t].arrived()
            add((t, slice(None), slice(None), kept), from_x[t])
            to_y[t].start()

    def y_turn():
        for t in range(3):
            to_y[t].arrived()
            add((t, y, slice(None), own), from_y[t])
            to_z[t].start()

    def z_turn():
        to_y[3].arrived()
        everything = total[3, y, :, own].astype(jnp.float32) + from_y[3].astype(jnp.float32)
        for t in range(3):
            to_z[t].arrived()
            everything = everything + from_z[t].astype(jnp.float32)
        total[3, y, :, own] = everything.astype(total.dtype)
        to_last.start()

    def last_turn():
        to_last.arrived()
        middle = half - 2 * outer
        shared = total[3, y, :, lanes(outer, middle)].astype(jnp.float32) + from_last[:, lanes(x * outer, middle)].astype(jnp.float32)
        result[:, lanes(core * half + outer, middle)] = shared.astype(result.dtype)
        result[:, lanes(core * half + x * wide, outer)] = total[3, y, :, kept]
        result[:, lanes(core * half + (1 - x) * wide, outer)] = from_last[:, lanes((1 - x) * middle, outer)]
        to_final.start()

    def end():
        to_final.arrived()
        store.start()

    return [first, core_turn, x_turn, y_turn, z_turn, last_turn, end]


REDUCE_HOPS, REDUCE_NEAR = 4 + 4 + 4 + 3 + 2, 5


def merged(units, every, lag=1):
    turns = []
    for i, unit in enumerate(units):
        for k, turn in enumerate(unit):
            at = i * every + k * lag
            turns += [[] for _ in range(at + 1 - len(turns))]
            turns[at].insert(0, turn)
    return turns


def run(turn):
    for action in turn:
        action()


def semaphores(hops, near):
    return [pltpu.SemaphoreType.DMA((hops,)), pltpu.SemaphoreType.DMA((hops,)), pltpu.SemaphoreType.DMA((max(near, 1),))]


def exchange_small(small, small_all, links, me):
    x, core, z, y = me
    number = (x * 2 + core) * 8 + z * 2 + y
    keep = Near(links, lambda: small.at[z * 2 + y], lambda: small_all.at[number])
    few = [
        Hop(
            links,
            lambda k=k: small.at[(number + k) % 8],
            lambda: small_all.at[number],
            lambda k=k: (((number + k) % 32) // 8, (number + k) % 8),
        )
        for k in range(1, 32)
    ]

    def begin():
        keep.start()
        for hop in few:
            hop.start()

    def end():
        keep.arrived()
        for hop in few:
            hop.arrived()

    return begin, end


def factors_turns(links, me, factors, group, whole):
    x, core, z, y = me
    slots = factors.shape[0]
    mine = lambda: group.at[lines((x * 2 + core) * slots, slots), :]
    keep = Near(links, lambda: factors, mine)
    peers = [
        Hop(links, lambda: factors, mine, lambda i=i, j=j: device((x + i) % 2, (core + j) % 2, z, y)) for i, j in ((0, 1), (1, 0), (1, 1))
    ]

    def first():
        keep.start()
        for hop in peers:
            hop.start()

    def second():
        keep.arrived()
        for hop in peers:
            hop.arrived()

    turns = gather_turns(links, me, group, whole, 256)
    return [first, lambda: (second(), turns[0]())] + turns[1:]


FACTOR_HOPS, FACTOR_NEAR = 3 + GATHER_HOPS, 1 + GATHER_NEAR


def nt(a, b):
    return lax.dot_general(a, b, (((1,), (1,)), ((), ())), preferred_element_type=jnp.float32)


def tn(a, b):
    return lax.dot_general(a, b, (((0,), (0,)), ((), ())), preferred_element_type=jnp.float32)


def nn(a, b):
    return jnp.dot(a, b, preferred_element_type=jnp.float32)


def normalize(values):
    centred = values - jnp.mean(values, axis=1, keepdims=True)
    inverse = lax.rsqrt(jnp.mean(centred * centred, axis=1, keepdims=True) + EPSILON)
    return (centred * inverse, inverse)


def norm_back(grad_normed, normed, inverse):
    first_mean = jnp.mean(grad_normed, axis=1, keepdims=True)
    second_mean = jnp.mean(grad_normed * normed, axis=1, keepdims=True)
    return inverse * (grad_normed - first_mean - normed * second_mean)


def gelu_both(u):
    c = math.sqrt(2 / math.pi)
    square = u * u
    t = jnp.tanh(u * (c + (c * 0.044715) * square))
    half = 0.5 + 0.5 * t
    value = u * half
    return value, half + value * (1.0 - t) * (c + (3 * c * 0.044715) * square)


def loop(count, body):
    def step(i, carry):
        body(i)
        return carry

    lax.fori_loop(0, count, step, 0)


def attention_lanes(segment, slots):
    lane = jnp.arange(128) % 64
    hot = segment[:, None] == lane[None, :]
    listed = lane[None, :] <= slots
    query_lanes = (hot & listed).astype(jnp.bfloat16)
    ones = (lane >= LSE_LANE) & (lane < LSE_LANE + 3)
    key_lanes = jnp.where(listed & ~hot, -1e30, jnp.where(ones[None, :], 1.0, 0.0)).astype(jnp.bfloat16)
    return query_lanes, key_lanes


class Host:
    def __init__(self, links, turns, steps, per_step):
        self.links, self.turns, self.steps, self.per_step = links, turns, steps, per_step
        self.step = pl.program_id(0)

    def turn(self, index):
        for hook, turn in sorted(self.turns.items()):
            if hook < self.steps * self.per_step and hook % self.per_step == index:
                pl.when(self.step == hook // self.per_step)(functools.partial(run, turn))

    def finish(self):
        @pl.when(self.step == self.steps - 1)
        def _():
            for hook, turn in sorted(self.turns.items()):
                if hook >= self.steps * self.per_step:
                    run(turn)
            self.links.drain()


def timed(units, every, lags, first=0):
    starts = every if isinstance(every, tuple) else [int(first + every * i) for i in range(len(units))]
    return [(start + lag, turn) for start, unit in zip(starts, units) for lag, turn in zip(lags, unit)]


def placed(schedule):
    turns = {}
    for hook, turn in schedule:
        turns.setdefault(hook, []).insert(0, turn)
    return turns


class Idle:
    def turn(self, index):
        pass

    def finish(self):
        pass


ANY = pl.BlockSpec(memory_space=pl.ANY)
VMEM = pl.BlockSpec(memory_space=pltpu.VMEM)


def call(kernel, grid, inputs, outputs, scratch=()):
    made = pl.pallas_call(
        kernel,
        grid=grid,
        out_shape=[jax.ShapeDtypeStruct(shape, kind) for shape, kind, _ in outputs],
        in_specs=[spec for _, spec in inputs],
        out_specs=[spec for _, _, spec in outputs],
        scratch_shapes=list(scratch),
        compiler_params=pltpu.CompilerParams(has_side_effects=True, vmem_limit_bytes=VMEM_LIMIT),
    )
    return made(*[array for array, _ in inputs])


def exact(table, values):
    sums = None
    for _ in range(3):
        part = values.astype(jnp.bfloat16)
        values = values - part.astype(jnp.float32)
        sums = nn(table, part) if sums is None else sums + nn(table, part)
    return sums


def modulation_turns(links, me, parts, from_y, from_z, columns):
    x, core, z, y = me
    block = lambda t, side: parts.at[((z + t + 1) % 4) * 2 + side, :, columns]
    to_y = [Hop(links, lambda t=t: block(t, 1 - y), lambda t=t: from_y.at[t, :, columns], lambda: device(x, core, z, 1 - y)) for t in range(4)]
    to_z = [
        Hop(links, lambda t=t: block(t, y), lambda t=t: from_z.at[t, :, columns], lambda t=t: device(x, core, (z + t + 1) % 4, y))
        for t in range(3)
    ]

    def begin():
        for hop in to_y:
            hop.start()

    def middle():
        for t in range(3):
            to_y[t].arrived()
            block(t, y)[...] = (block(t, y)[...].astype(jnp.float32) + from_y[t, :, columns].astype(jnp.float32)).astype(parts.dtype)
            to_z[t].start()

    def end():
        to_y[3].arrived()
        total = block(3, y)[...].astype(jnp.float32) + from_y[3, :, columns].astype(jnp.float32)
        for t in range(3):
            to_z[t].arrived()
            total = total + from_z[t, :, columns].astype(jnp.float32)
        return total

    return begin, middle, end


def first_kernel(small, wmod_ref, wqkv, tok_ref, table_ref, small_all, wholes, hidden_ref, out_ref, unit_ref, landed, held, normed, *refs):
    parts, from_y, from_z, sems = refs[:2], refs[2:4], refs[4:6], refs[6:]
    me, links = place(), Links(*sems)
    x, core, z, y = me
    group = (x * 2 + core) * 8
    rows = tok_ref.shape[0]
    begin, end = exchange_small(small, landed, links, me)
    units = [
        gather_turns(links, me, wqkv.at[half, pl.ds(i * D, D)], held.at[i], 128 if half.start else 256, half.start)
        for i in range(3)
        for half in HALVES
    ]
    gather = merged(units, 1)
    halves = [modulation_turns(links, me, parts[i], from_y[i], from_z[i], pl.ds(0, 2 * D)) for i in (0, 1)]
    keep = [Near(links, lambda i=i: held.at[i], lambda i=i: wholes.at[i]) for i in range(3)]
    save = Near(links, lambda: landed, lambda: small_all)
    links.ends += [near.arrived for near in keep + [save]]

    def norm(first):
        def unit(u):
            at = pl.ds(pl.multiple_of(u * UNIT, UNIT), UNIT)
            normed[at, :] = normalize(tok_ref[at, :].astype(jnp.float32))[0]

        loop(rows // UNIT // 2, lambda i: unit(first + i))

    def settle(half):
        total = halves[half][2]()
        table = table_ref[...].astype(jnp.bfloat16)
        for f in range(4):
            bias = landed[group + 4 * half + f, :16, :].astype(jnp.float32)
            for i in range(4):
                at = (4 * f + i) * 128
                value = total[:, at : at + 128] + bias[i : i + 1, :]
                unit_ref[:, 2 * half * D + at : 2 * half * D + at + 128] = exact(table, value)

    def project(i):
        def block(r):
            here = pl.ds(pl.multiple_of(r * 256, 256), 256)
            out_ref[here, i * D : (i + 1) * D] = nn(hidden_ref[here, :], held[i]).astype(jnp.bfloat16)

        loop(rows // 256, block)

    begin()
    run(gather[0])
    norm(0)
    run(gather[1])
    norm(rows // UNIT // 2)
    end()
    save.start()
    for f in range(8):
        part = nn(landed[group + f, 16:, :], wmod_ref[...])
        for half in (0, 1):
            parts[half][f] = part[:, half * 2 * D : (half + 1) * 2 * D].astype(parts[half].dtype)
    halves[0][0]()
    run(gather[2])
    halves[0][1]()
    halves[1][0]()
    run(gather[3])
    settle(0)
    halves[1][1]()

    def shape(u):
        at = pl.ds(pl.multiple_of(u * UNIT, UNIT), UNIT)
        hidden_ref[at, :] = (normed[at, :] * (1.0 + unit_ref[pl.ds(u, 1), :D]) + unit_ref[pl.ds(u, 1), D : 2 * D]).astype(jnp.bfloat16)

    run(gather[4])
    loop(rows // UNIT, shape)
    run(gather[5])
    keep[0].start()
    project(0)
    run(gather[6])
    settle(1)
    run(gather[7])
    keep[1].start()
    project(1)
    run(gather[8])
    run(gather[9])
    keep[2].start()
    project(2)
    links.drain()


def first_all(small, w_mod, w_qkv, tokens, table):
    rows, (units, slots) = tokens.shape[0], table.shape
    b16, f32 = jnp.bfloat16, jnp.float32
    hops = 31 + 6 * GATHER_HOPS + 14
    return call(
        first_kernel,
        (),
        [(small, ANY), (w_mod, VMEM), (w_qkv, ANY), (tokens, VMEM), (table, VMEM)],
        [
            ((32,) + small.shape[1:], b16, ANY), ((3, D, D), b16, ANY), ((rows, D), b16, VMEM), ((rows, 3 * D), b16, VMEM),
            ((units, 4 * D), f32, VMEM),
        ],
        [
            pltpu.VMEM((32,) + small.shape[1:], b16), pltpu.VMEM((3, D, D), b16), pltpu.VMEM((rows, D), f32),
        ]
        + [pltpu.VMEM((count, slots, 2 * D), kind) for count in (8, 4, 3) for kind in (f32, b16)]
        + semaphores(hops, 1 + 6 * GATHER_NEAR + 4),
    )


def attend_kernel(shared, q_ref, k_ref, v_ref, ql_ref, kl_ref, *refs):
    if shared:
        shards, out_ref, qa_ref, wholes, *sems = refs
        me, links = place(), Links(*sems)
        units = [
            gather_turns(links, me, shards.at[i, half], wholes.at[i], 128 if half.start else 256, half.start)
            for i in range(shared)
            for half in HALVES
        ]
        host = Host(links, placed(timed(units, *ATTEND_GATHER)), D // 128, 4)
    else:
        (out_ref, qa_ref), host = refs, Idle()
    rows = q_ref.shape[0]
    block = min(ATTENTION_ROWS, rows)
    low = lax.broadcasted_iota(jnp.int32, (1, 128), 1) < HEAD_DIM
    lane = lax.broadcasted_iota(jnp.int32, (1, 128), 1) % HEAD_DIM
    keys, vals = [], []
    for own in (low, ~low):
        keys.append(jnp.where(own, k_ref[...], kl_ref[...]))
        vals.append(jnp.where(own, v_ref[...], jnp.bfloat16(1)))
    for at, first in enumerate(range(0, rows, block)):
        here = pl.ds(first, block)
        queries = q_ref[here, :] * jnp.bfloat16(HEAD_DIM**-0.5)
        mixed = []
        for head, own in enumerate((low, ~low)):
            host.turn(2 * at + head)
            asked = jnp.where(own, queries, ql_ref[here, :])
            scores = nt(asked, keys[head])
            top = jnp.max(scores, axis=1, keepdims=True)
            weight = jnp.exp(scores - top).astype(jnp.bfloat16)
            both = nn(weight, vals[head])
            mixed.append(both)
            log_total = -(top + jnp.log(both))
            first_part = log_total.astype(jnp.bfloat16)
            rest = log_total - first_part.astype(jnp.float32)
            second = rest.astype(jnp.bfloat16)
            third = (rest - second.astype(jnp.float32)).astype(jnp.bfloat16)
            for i, part in enumerate((first_part, second, third)):
                asked = jnp.where(~own & (lane == LSE_LANE + i), part, asked)
            qa_ref[head, here, :] = asked
        total = pltpu.roll(jnp.where(low, mixed[1], mixed[0]), HEAD_DIM, 1)
        out_ref[here, :] = (jnp.where(low, mixed[0], mixed[1]) / total).astype(jnp.bfloat16)
    host.finish()


def attend(projected, query_lanes, key_lanes, shards=None):
    rows, pairs = projected.shape[0], D // 128
    spec = lambda shift: pl.BlockSpec((rows, 128), lambda i: (0, i + shift))
    same = pl.BlockSpec((rows, 128), lambda i: (0, 0))
    inputs = [(projected, spec(0)), (projected, spec(pairs)), (projected, spec(2 * pairs)), (query_lanes, same), (key_lanes, same)]
    outputs = [((rows, D), jnp.bfloat16, spec(0)), ((HEADS, rows, 128), jnp.bfloat16, pl.BlockSpec((2, rows, 128), lambda i: (i, 0, 0)))]
    if shards is None:
        return call(functools.partial(attend_kernel, 0), (pairs,), inputs, outputs)
    units, depth, width = shards.shape
    return call(
        functools.partial(attend_kernel, units),
        (pairs,),
        inputs + [(shards, ANY)],
        outputs + [((units, 8 * depth, width), shards.dtype, ANY)],
        semaphores(2 * GATHER_HOPS * units, 2 * GATHER_NEAR * units),
    )


def attend_back_kernel(counts, k_ref, v_ref, kl_ref, qa_ref, out_ref, go_ref, *refs):
    units = sum(counts)
    if units:
        groups, refs = refs[: len(counts)], refs[len(counts) :]
        small, factors, grad_ref, results, small_all, factor_group, factor_all, kt_ref, dqt_ref, *refs = refs
        summed, lands, sems = refs[0], refs[1 : 1 + 12 * units], refs[1 + 12 * units :]
        me, links = place(), Links(*sems)
        begin, end = exchange_small(small, small_all, links, me)
        locals_ = [group.at[i] for group, count in zip(groups, counts) for i in range(count)]
        plans = [
            reduce_turns(
                links, me, locals_[i // 2], i % 2 * 64, summed.at[i // 2, HALVES[i % 2]], results.at[i // 2, HALVES[i % 2]], lands[6 * i : 6 * i + 6]
            )
            for i in range(2 * units)
        ]
        schedule = list(zip(BACK_FACTORS, factors_turns(links, me, factors, factor_group, factor_all)))
        schedule = [(0, begin)] + schedule + timed(plans, *BACK_REDUCE)
        links.ends += [end]
        host = Host(links, placed(schedule), D // 128, 4)
    else:
        (grad_ref, kt_ref, dqt_ref), host = refs, Idle()
    rows = k_ref.shape[0]
    block = min(ATTENTION_ROWS, rows)
    low = lax.broadcasted_iota(jnp.int32, (1, 128), 1) < HEAD_DIM
    grads = go_ref[...]
    product = pltpu.roll(-(grads.astype(jnp.float32) * out_ref[...].astype(jnp.float32)), HEAD_DIM, 1).astype(jnp.bfloat16)
    kt_ref[...] = k_ref[...].astype(jnp.float32).T.astype(jnp.bfloat16)
    given = [jnp.where(own, grads, product) for own in (low, ~low)]
    for at, first in enumerate(range(0, rows, block)):
        here = pl.ds(first, block)
        dks, dvs = [], []
        for head, own in enumerate((low, ~low)):
            host.turn(2 * at + head)
            keys = jnp.where(own, k_ref[here, :], kl_ref[here, :])
            vals = jnp.where(own, v_ref[here, :], jnp.bfloat16(1))
            probs = jnp.exp(nt(keys, qa_ref[head]))
            slopes = nt(vals, given[head])
            moved = (probs * slopes).astype(jnp.bfloat16)
            dvs.append(nn(probs.astype(jnp.bfloat16), grads))
            dks.append(nn(moved, qa_ref[head]))
            part = nn(kt_ref[head * HEAD_DIM : (head + 1) * HEAD_DIM, here], moved)
            where = pl.ds(head * HEAD_DIM, HEAD_DIM)
            if first == 0:
                dqt_ref[where, :] = part
            else:
                dqt_ref[where, :] += part
        grad_ref[1, here, :] = jnp.where(low, dks[0], dks[1]).astype(jnp.bfloat16)
        grad_ref[2, here, :] = jnp.where(low, dvs[0], dvs[1]).astype(jnp.bfloat16)
    grad_ref[0] = (dqt_ref[...].T * HEAD_DIM**-0.5).astype(jnp.bfloat16)
    host.finish()


def attend_back(projected, key_lanes, asked, attn_out, grad_attn, groups=(), small=None, factors=None):
    rows, pairs = projected.shape[0], D // 128
    spec = lambda shift: pl.BlockSpec((rows, 128), lambda i: (0, i + shift))
    same = pl.BlockSpec((rows, 128), lambda i: (0, 0))
    two = pl.BlockSpec((2, rows, 128), lambda i: (i, 0, 0))
    inputs = [(projected, spec(pairs)), (projected, spec(2 * pairs)), (key_lanes, same), (asked, two), (attn_out, spec(0)), (grad_attn, spec(0))]
    outputs = [((3, rows, D), jnp.bfloat16, pl.BlockSpec((3, rows, 128), lambda i: (0, 0, i)))]
    scratch = [pltpu.VMEM((128, rows), jnp.bfloat16), pltpu.VMEM((128, rows), jnp.float32)]
    counts = [g.shape[0] for g in groups]
    units = sum(counts)
    if units:
        inputs += [(g, ANY) for g in groups] + [(small, ANY), (factors, ANY)]
        slots, width = factors.shape
        outputs += [((units, 128, D), jnp.bfloat16, ANY), ((32,) + small.shape[1:], small.dtype, ANY)]
        outputs += [((4 * slots, width), factors.dtype, ANY), ((32 * slots, width), factors.dtype, ANY)]
        scratch += [pltpu.VMEM((units, 128, D), jnp.bfloat16)] + [land for _ in range(2 * units) for land in reduce_lands(64)]
        scratch += semaphores(31 + FACTOR_HOPS + 2 * REDUCE_HOPS * units, 1 + FACTOR_NEAR + 2 * REDUCE_NEAR * units)
    return call(functools.partial(attend_back_kernel, counts), (pairs,), inputs, outputs, scratch)


def before_kernel(attn_ref, tok_ref, cot_ref, wout_ref, bout_ref, scale_ref, shift_ref, live_ref, middle_ref, hidden_ref, two_ref, gbdown_ref):
    r = pl.program_id(0)
    rows = tok_ref.shape[0]
    units = rows // UNIT

    @pl.when(r == 0)
    def _():
        gbdown_ref[...] = jnp.zeros_like(gbdown_ref)

    middle_ref[...] = nn(attn_ref[...], wout_ref[0]) + bout_ref[...].astype(jnp.float32)
    for i in range(units):
        u = r * units + i
        at = pl.ds(i * UNIT, UNIT)
        live = live_ref[pl.ds(u, 1), :]
        value = tok_ref[at, :].astype(jnp.float32) + live * middle_ref[at, :]
        middle_ref[at, :] = value
        normed, _ = normalize(value)
        hidden_ref[at, :] = (normed * (1.0 + scale_ref[pl.ds(u, 1), :]) + shift_ref[pl.ds(u, 1), :]).astype(jnp.bfloat16)
        grad = (live * cot_ref[at, :].astype(jnp.float32)).astype(jnp.bfloat16)
        two_ref[at, :] = grad
        gbdown_ref[...] += jnp.sum(grad.astype(jnp.float32), axis=0, keepdims=True)


def before_mlp(attn_out, tokens, cotangent, weights, b_out, scale, shift, live):
    rows = tokens.shape[0]
    block = pl.BlockSpec((256, D), lambda r: (r, 0))
    once = lambda shape: pl.BlockSpec(shape, lambda r: (0,) * len(shape))
    units = once((rows // UNIT, D))
    return call(
        before_kernel,
        (rows // 256,),
        [(attn_out, block), (tokens, block), (cotangent, block), (weights, once((1, D, D))), (b_out, once((1, D))), (scale, units), (shift, units), (live, units)],
        [((rows, D), jnp.float32, block), ((rows, D), jnp.bfloat16, block), ((rows, D), jnp.bfloat16, block), ((1, D), jnp.float32, once((1, D)))],
    )


def mlp_kernel(early, hidden, two, bup_ref, weights, *refs):
    j = pl.program_id(0)
    rows = hidden.shape[0]
    late = FF_BLOCKS - early
    if late:
        shards, acc, back, gbup_ref, grads_ref, results, act, pre, held, made, summed, *refs = refs
        lands, sems = refs[: 20 * early], refs[20 * early :]
    else:
        acc, back, gbup_ref, grads_ref, act, pre, held, made, *sems = refs
    slots = made.shape[0]
    me, links = place(), Links(*sems)
    fetch = [[Near(links, lambda b=b, w=w: weights.at[1 + 2 * b + w], lambda b=b, w=w: held.at[b, w]) for w in (0, 1)] for b in range(early)]
    store = [Near(links, lambda b=b: made.at[b % slots], lambda b=b: grads_ref.at[b - FF_BLOCKS + grads_ref.shape[0]]) for b in range(FF_BLOCKS)]
    kept_blocks = range(FF_BLOCKS - grads_ref.shape[0], FF_BLOCKS)
    if late:
        gathers, reduces = [], []
        for i in range(4 * late):
            b, w, half = early + i // 4, i // 2 % 2, HALVES[i % 2]
            gathers.append(gather_turns(links, me, shards.at[i // 2, half], held.at[b, w], 128 if i % 2 else 256, half.start))
        for i in range(4 * early):
            b, w, half = i // 4, i // 2 % 2, HALVES[i % 2]
            reduces.append(
                reduce_turns(
                    links, me, made.at[b % slots, w], half.start, summed.at[2 * b + w, half], results.at[2 * b + w, half], lands[5 * i : 5 * i + 5]
                )
            )
        schedule = timed(gathers, *MLP_GATHER) + timed(reduces, *MLP_REDUCE)
        host = Host(links, placed(schedule), FF_BLOCKS, 16)
    else:
        host = Idle()

    @pl.when(j == 0)
    def _():
        for pair in fetch:
            for near in pair:
                near.start()

    host.turn(0)
    for b in range(early):

        @pl.when(j == b)
        def _():
            for near in fetch[b]:
                near.arrived()

    gbup_ref[...] = jnp.zeros_like(gbup_ref)
    up, down = held.at[j, 0], held.at[j, 1]
    block = rows // 4
    for r in range(4):
        if r:
            host.turn(2 * r)
        here = pl.ds(r * block, block)
        value, slope = gelu_both(nn(hidden[here, :], up[...]) + bup_ref[0].astype(jnp.float32))
        value = value.astype(jnp.bfloat16)
        grad = (nt(two[here, :], down[...]) * slope).astype(jnp.bfloat16)
        act[here, :] = value
        pre[here, :] = grad
        gbup_ref[0] += jnp.sum(grad.astype(jnp.float32), axis=0, keepdims=True)
        host.turn(2 * r + 1)
        forward, backward = nn(value, down[...]), nt(grad, up[...])

        @pl.when(j == 0)
        def _():
            acc[here, :] = forward
            back[here, :] = backward

        @pl.when(j > 0)
        def _():
            acc[here, :] += forward
            back[here, :] += backward

    slot = lax.rem(j, slots)
    for r in range(4):
        here = pl.ds(r * 256, 256)
        for w, (left, right) in enumerate(((hidden, pre), (act, two))):
            host.turn(8 + 2 * r + w)
            value = tn(left[:, here], right[...]).astype(jnp.bfloat16)
            for half in (0, 1):
                made[slot, w, 2 * r + half] = value[half * 128 : half * 128 + 128]
    for b in kept_blocks:
        pl.when(j == b)(store[b].start)

    @pl.when(j == FF_BLOCKS - 1)
    def _():
        for b in kept_blocks:
            store[b].arrived()

    host.finish()


def feed_forward(hidden, two, weights, b_up, shards=None):
    rows = hidden.shape[0]
    once = lambda shape: pl.BlockSpec(shape, lambda j: (0, 0), pipeline_mode=pl.Buffered(1))
    whole = once((rows, D))
    row = pl.BlockSpec((1, 1, D), lambda j: (j, 0, 0))
    f32, b16 = jnp.float32, jnp.bfloat16
    early = FF_BLOCKS if shards is None else EARLY
    late = FF_BLOCKS - early
    kept = late or FF_BLOCKS
    inputs = [(hidden, whole), (two, whole), (b_up, row), (weights, ANY)]
    outputs = [((rows, D), f32, whole), ((rows, D), f32, whole), ((FF_BLOCKS, 1, D), f32, row), ((kept, 2, 8, 128, D), b16, ANY)]
    slots = 2 if late else FF_BLOCKS
    scratch = [
        pltpu.VMEM((rows, D), b16), pltpu.VMEM((rows, D), b16), pltpu.VMEM((FF_BLOCKS, 2, D, D), b16), pltpu.VMEM((slots, 2, 8, 128, D), b16),
    ]
    hops, near = 1, 2 * early + FF_BLOCKS
    if late:
        inputs += [(shards, ANY)]
        outputs += [((2 * early, 128, D), b16, ANY)]
        scratch += [pltpu.VMEM((2 * early, 128, D), b16)] + [land for _ in range(4 * early) for land in reduce_lands(64, far=False)]
        hops = 4 * late * GATHER_HOPS + 4 * early * REDUCE_HOPS
        near += 4 * late * GATHER_NEAR + 4 * early * REDUCE_NEAR
    return call(functools.partial(mlp_kernel, early), (FF_BLOCKS,), inputs, outputs, scratch + semaphores(hops, near))


def after_kernel(
    middle_ref, acc_ref, back_ref, cot_ref, attn_ref, wout_ref, bdown_ref, scale_ref, live_ref,
    out_ref, mid_grad_ref, attn_grad_ref, gout_ref, gbout_ref, gscale_ref, gshift_ref, one_ref, total_ref,
):
    r = pl.program_id(0)
    rows = cot_ref.shape[0]
    units = rows // UNIT

    @pl.when(r == 0)
    def _():
        gbout_ref[...] = jnp.zeros_like(gbout_ref)
        total_ref[...] = jnp.zeros_like(total_ref)

    for i in range(units):
        u = r * units + i
        at = pl.ds(i * UNIT, UNIT)
        live = live_ref[pl.ds(u, 1), :]
        value = middle_ref[at, :]
        out_ref[at, :] = (value + live * (acc_ref[at, :] + bdown_ref[...].astype(jnp.float32))).astype(jnp.bfloat16)
        normed, inverse = normalize(value)
        grad = back_ref[at, :]
        gshift_ref[pl.ds(u, 1), :] = jnp.sum(grad, axis=0, keepdims=True)
        gscale_ref[pl.ds(u, 1), :] = jnp.sum(grad * normed, axis=0, keepdims=True)
        passed = cot_ref[at, :].astype(jnp.float32) + norm_back(grad * (1.0 + scale_ref[pl.ds(u, 1), :]), normed, inverse)
        mid_grad_ref[at, :] = passed
        one = (live * passed).astype(jnp.bfloat16)
        one_ref[at, :] = one
        gbout_ref[...] += jnp.sum(one.astype(jnp.float32), axis=0, keepdims=True)
    attn_grad_ref[...] = nt(one_ref[...], wout_ref[0]).astype(jnp.bfloat16)
    total_ref[...] += tn(attn_ref[...], one_ref[...])

    @pl.when(r == pl.num_programs(0) - 1)
    def _():
        for i in range(8):
            gout_ref[0, i] = total_ref[i * 128 : i * 128 + 128, :].astype(jnp.bfloat16)


def after_mlp(middle, acc, back, cotangent, attn_out, weights, b_down, scale, live):
    rows = middle.shape[0]
    block = pl.BlockSpec((256, D), lambda r: (r, 0))
    once = lambda shape: pl.BlockSpec(shape, lambda r: (0,) * len(shape))
    units, row = once((rows // UNIT, D)), once((1, D))
    f32, b16 = jnp.float32, jnp.bfloat16
    return call(
        after_kernel,
        (rows // 256,),
        [
            (middle, block), (acc, block), (back, block), (cotangent, block), (attn_out, block), (weights, once((1, D, D))),
            (b_down, row), (scale, units), (live, units),
        ],
        [
            ((rows, D), b16, block), ((rows, D), f32, block), ((rows, D), b16, block), ((1, 8, 128, D), b16, once((1, 8, 128, D))), ((1, D), f32, row),
            ((rows // UNIT, D), f32, units), ((rows // UNIT, D), f32, units),
        ],
        [pltpu.VMEM((256, D), b16), pltpu.VMEM((D, D), f32)],
    )


def head_kernel(tok_ref, scale_ref, shift_ref, w_ref, hidden_ref, out_ref):
    rows = tok_ref.shape[0]

    @pl.when(pl.program_id(0) == 0)
    def _():
        def unit(u):
            at = pl.ds(pl.multiple_of(u * UNIT, UNIT), UNIT)
            normed, _ = normalize(tok_ref[at, :].astype(jnp.float32))
            hidden_ref[at, :] = (normed * (1.0 + scale_ref[pl.ds(u, 1), :]) + shift_ref[pl.ds(u, 1), :]).astype(jnp.bfloat16)

        loop(rows // UNIT, unit)

    def block(r):
        here = pl.ds(pl.multiple_of(r * ROWS, ROWS), ROWS)
        out_ref[here, :] = nn(hidden_ref[here, :], w_ref[0]).astype(jnp.bfloat16)

    loop(rows // ROWS, block)


def project_in(tokens, scale, shift, w_qkv):
    rows = tokens.shape[0]
    whole = lambda shape: pl.BlockSpec(shape, lambda j: (0, 0))
    return pl.pallas_call(
        head_kernel,
        grid=(3,),
        out_shape=[jax.ShapeDtypeStruct((rows, D), jnp.bfloat16), jax.ShapeDtypeStruct((rows, 3 * D), jnp.bfloat16)],
        in_specs=[whole((rows, D)), whole((rows // UNIT, D)), whole((rows // UNIT, D)), pl.BlockSpec((1, D, D), lambda j: (j, 0, 0))],
        out_specs=[whole((rows, D)), pl.BlockSpec((rows, D), lambda j: (0, j))],
        compiler_params=pltpu.CompilerParams(vmem_limit_bytes=VMEM_LIMIT),
    )(tokens, scale, shift, w_qkv)


def tail_kernel(shared, grad_ref, hidden_ref, w_ref, tok_ref, scale_ref, *refs):
    p = pl.program_id(0)
    rows = tok_ref.shape[0]
    if shared:
        table_ref, results, gtok_ref, gscale_ref, gshift_ref, factor_group, factor_all, back, gw, summed, factors, *refs = refs
        lands, sems = refs[:30], refs[30:]
        me, links = place(), Links(*sems)
        schedule = []
        for i in range(6):
            half = HALVES[i % 2]
            unit = reduce_turns(
                links, me, gw.at[i // 2], half.start, summed.at[i // 2, half], results.at[i // 2, half], lands[5 * i : 5 * i + 5]
            )
            schedule += timed([unit], 0, TAIL_REDUCE, 4 * (i // 2 + 1) + 2 * (i % 2))
        turns = placed(schedule)
        host = Host(links, {h: t for h, t in turns.items() if h < 24}, 6, 4)
        rest = [turns[h] for h in sorted(turns) if h >= 24]
        spread = factors_turns(links, me, factors, factor_group, factor_all)
    else:
        gw, gtok_ref, gscale_ref, gshift_ref, back = refs
        host, rest = Idle(), []

    def products(r):
        value = tn(hidden_ref[:, r * 256 : r * 256 + 256], grad_ref[0]).astype(jnp.bfloat16)
        for half in (0, 1):
            gw[p if shared else 0, 2 * r + half] = value[half * 128 : half * 128 + 128]

    def way_back(r):
        here = pl.ds(r * (rows // 4), rows // 4)
        part = nt(grad_ref[0, here, :], w_ref[0])

        @pl.when(p == 3)
        def _():
            back[here, :] = part

        @pl.when(p > 3)
        def _():
            back[here, :] += part

    for r in range(4):
        host.turn(r)
        pl.when(p < 3)(functools.partial(products, r))
        pl.when(p >= 3)(functools.partial(way_back, r))

    @pl.when(p == pl.num_programs(0) - 1)
    def _():
        def unit(u):
            at = pl.ds(pl.multiple_of(u * UNIT, UNIT), UNIT)
            normed, inverse = normalize(tok_ref[at, :].astype(jnp.float32))
            grad = back[at, :]
            gshift_ref[pl.ds(u, 1), :] = jnp.sum(grad, axis=0, keepdims=True)
            gscale_ref[pl.ds(u, 1), :] = jnp.sum(grad * normed, axis=0, keepdims=True)
            passed = norm_back(grad * (1.0 + scale_ref[pl.ds(u, 1), :]), normed, inverse)
            gtok_ref[at, :] = passed.astype(jnp.bfloat16)

        for quarter in range(4):
            if quarter < len(rest):
                run(rest[quarter])
            loop(rows // UNIT // 4, lambda i: unit(quarter * (rows // UNIT // 4) + i))
        if shared:
            table = table_ref[...].astype(jnp.bfloat16)
            for i, ref in enumerate((gscale_ref, gshift_ref)):
                factors[:, i * D : (i + 1) * D] = exact(table, ref[...]).astype(jnp.bfloat16)
            left = rest[4:]
            for i in range(max(len(left), len(spread))):
                if i < len(spread):
                    spread[i]()
                if i < len(left):
                    run(left[i])

    host.finish()


def project_back(grad_proj, hidden, w_qkv, tokens, scale, table=None):
    rows = tokens.shape[0]
    once = lambda shape: pl.BlockSpec(shape, lambda p: (0, 0), pipeline_mode=pl.Buffered(1))
    units, whole = once((rows // UNIT, D)), once((rows, D))
    f32, b16 = jnp.float32, jnp.bfloat16
    block = pl.BlockSpec((1, rows, D), lambda p: (lax.rem(p, 3), 0, 0))
    inputs = [
        (grad_proj, block), (hidden, whole), (w_qkv, pl.BlockSpec((1, D, D), lambda p: (jnp.maximum(p - 3, 0), 0, 0))), (tokens, whole), (scale, units),
    ]
    outputs = [((rows, D), b16, whole), ((rows // UNIT, D), f32, units), ((rows // UNIT, D), f32, units)]
    scratch = [pltpu.VMEM((rows, D), f32)]
    shared = table is not None
    if shared:
        slots = table.shape[0]
        inputs += [(table, once(table.shape))]
        outputs = [((3, 128, D), b16, ANY)] + outputs
        outputs += [((4 * slots, 2 * D), b16, ANY), ((32 * slots, 2 * D), b16, ANY)]
        scratch += [pltpu.VMEM((3, 8, 128, D), b16), pltpu.VMEM((3, 128, D), b16), pltpu.VMEM((slots, 2 * D), b16)] + [land for _ in range(6) for land in reduce_lands(64, far=False)]
        scratch += semaphores(6 * REDUCE_HOPS + FACTOR_HOPS, 6 * REDUCE_NEAR + FACTOR_NEAR)
    else:
        outputs = [((3, 8, 128, D), b16, pl.BlockSpec((1, 8, 128, D), lambda p: (jnp.minimum(p, 2), 0, 0, 0)))] + outputs
    return call(functools.partial(tail_kernel, shared), (6,), inputs, outputs, scratch)


def tuned(sizes):
    return sizes == (4, 8)


def blocks_of(columns):
    return columns.reshape(columns.shape[0], FF_BLOCKS, -1).transpose(1, 0, 2)


def local(
    sizes, tokens, lengths, buckets, w_mod, b_mod, w_qkv, w_out, b_out, w_up, b_up, w_down, b_down, cotangent,
):
    rows, slots, n = tokens.shape[0], lengths.shape[1], sizes[1]
    own = tuned(sizes)
    segment, live, unit_table = layout(lengths[0], rows)
    feats = time_features(buckets[0]).astype(jnp.bfloat16)
    whole = lambda array: lax.all_gather(array, "fsdp", axis=0, tiled=True)
    if own:
        packed = jnp.concatenate([b_mod, b_out, b_up, b_down]).reshape(-1, 128)
        packed = jnp.pad(packed, ((0, 16 - packed.shape[0]), (0, 0)))
        by_owner = feats.reshape(slots, n, 128).transpose(1, 0, 2)
        small = jnp.concatenate([jnp.broadcast_to(packed, (n, 16, 128)), by_owner], axis=1)
        small_all, full_qkv, hidden_attn, projected, per_unit = first_all(small, w_mod, w_qkv, tokens, unit_table)
        of_group = lax.dynamic_slice(small_all, (lax.axis_index("dp") * n, 0, 0), (n, 16, 128))
        full_bout, full_bdown = of_group[:, 4].reshape(1, -1), of_group[:, 9].reshape(1, -1)
        full_bup = of_group[:, 5:9].transpose(1, 0, 2).reshape(FF_BLOCKS, 1, -1)
        every_feats = small_all[:, 16:].reshape(sizes[0], n, slots, 128).transpose(1, 0, 2, 3).reshape(-1, 128)
    else:
        full_mod, full_qkv, full_bmod, full_bout, full_bup, full_bdown = [whole(a) for a in (w_mod, w_qkv, b_mod, b_out, b_up, b_down)]
        full_bout, full_bdown, full_bup = full_bout[None], full_bdown[None], full_bup.reshape(FF_BLOCKS, 1, -1)
        every_feats = lax.all_gather(feats, ("dp", "fsdp"), axis=0, tiled=True)
        every_feats = lax.dynamic_slice(every_feats, (0, lax.axis_index("fsdp") * (D // n)), (every_feats.shape[0], D // n))
        modulation = jnp.dot(feats, full_mod, preferred_element_type=jnp.float32) + full_bmod
        per_unit = jnp.dot(unit_table, modulation, precision=HIGHEST)
        full_qkv = full_qkv.reshape(D, 3, D).transpose(1, 0, 2)
        hidden_attn, projected = project_in(tokens, per_unit[:, :D], per_unit[:, D : 2 * D], full_qkv)
    scale_one, _, scale_two, shift_two = [per_unit[:, i * D : (i + 1) * D] for i in range(4)]
    live_units = jnp.broadcast_to(live[:, None], (rows // UNIT, D))
    query_lanes, key_lanes = attention_lanes(jnp.repeat(segment, UNIT), slots)
    if own:
        ups = w_up.reshape(-1, n, FF_BLOCKS, 128).transpose(2, 0, 1, 3).reshape(FF_BLOCKS, 1, -1, D)
        downs = w_down.reshape(FF_BLOCKS, 1, -1, D)
        pairs = jnp.concatenate([ups, downs], axis=1).reshape(2 * FF_BLOCKS, -1, D)
        attn_out, asked, weights = attend(projected, query_lanes, key_lanes, jnp.concatenate([w_out[None], pairs[: 2 * EARLY]]))
        late = pairs[2 * EARLY :]
    else:
        attn_out, asked = attend(projected, query_lanes, key_lanes)
        pairs = jnp.stack([blocks_of(whole(w_up)), whole(w_down).reshape(FF_BLOCKS, D, D)], axis=1)
        weights, late = jnp.concatenate([whole(w_out)[None], pairs.reshape(2 * FF_BLOCKS, D, D)]), None
    middle, hidden_mlp, grad_two, grad_b_down = before_mlp(
        attn_out, tokens, cotangent, weights, full_bout, scale_two, shift_two, live_units
    )
    forward, backward, grad_b_up, grad_pairs, *totals_early = feed_forward(hidden_mlp, grad_two, weights, full_bup, late)
    output, grad_mid, grad_attn, grad_w_out, grad_b_out, grad_scale_two, grad_shift_two = after_mlp(
        middle, forward, backward, cotangent, attn_out, weights, full_bdown, scale_two, live_units
    )

    def factors_of(first, second):
        return jnp.dot(unit_table.T, jnp.concatenate([first, second], axis=1), precision=HIGHEST).astype(jnp.bfloat16)

    mod_two = factors_of(grad_scale_two, grad_shift_two)
    if own:
        sums = [grad_b_out.reshape(n, 1, 128), grad_b_up.reshape(FF_BLOCKS, n, 128).transpose(1, 0, 2), grad_b_down.reshape(n, 1, 128)]
        small = jnp.pad(jnp.concatenate(sums, axis=1), ((0, 0), (0, 2), (0, 0)))
        grad_proj, totals, small_all, _, mod_two = attend_back(
            projected, key_lanes, asked, attn_out, grad_attn, (grad_pairs.reshape(-1, 8, 128, D), grad_w_out), small, mod_two
        )
        total = jnp.sum(small_all, axis=0)
        sum_bout, sum_bup, sum_bdown = total[0], total[1:5].reshape(-1), total[5]
    else:
        grad_proj = attend_back(projected, key_lanes, asked, attn_out, grad_attn)[0]
    qkv_grads, through_norm, grad_scale_one, grad_shift_one, *factors = project_back(
        grad_proj, hidden_attn, full_qkv, tokens, scale_one, unit_table.T if own else None
    )
    grad_tokens = grad_mid + through_norm.astype(jnp.float32)
    if own:
        mod_one = factors[1]
    else:
        mod_one = factors_of(grad_scale_one, grad_shift_one)
        mod_one, mod_two = [lax.all_gather(m, ("dp", "fsdp"), axis=0, tiled=True) for m in (mod_one, mod_two)]
    sum_mod = jnp.concatenate(
        [jnp.einsum("sd,sc->dc", every_feats, m, preferred_element_type=jnp.float32) for m in (mod_one, mod_two)], axis=1
    )
    position, share = lax.axis_index("fsdp"), 4 * D // n
    chosen = jnp.where(position < n // 2, mod_one, mod_two)
    sum_bmod = jnp.sum(
        lax.dynamic_slice(chosen, (0, position % (n // 2) * share), (chosen.shape[0], share)), axis=0, dtype=jnp.float32
    )
    if own:
        totals, qkv_grads = totals.astype(jnp.float32), qkv_grads.astype(jnp.float32)
        pairs = jnp.concatenate([totals_early[0].astype(jnp.float32), totals[:-1]]).reshape(FF_BLOCKS, 2, 128, D)
        sum_up = pairs[:, 0].reshape(FF_BLOCKS, -1, n, 128).transpose(1, 2, 0, 3).reshape(w_up.shape)
        sum_down = pairs[:, 1].reshape(w_down.shape)
        sum_out = totals[-1]
        sum_qkv = qkv_grads.transpose(1, 0, 2).reshape(w_qkv.shape)
    else:
        summed = lambda a: lax.psum(lax.psum_scatter(a, "fsdp", scatter_dimension=0, tiled=True), "dp").astype(jnp.float32)
        sum_up = summed(grad_pairs[:, 0].reshape(FF_BLOCKS, D, D).transpose(1, 0, 2).reshape(D, -1))
        sum_down = summed(grad_pairs[:, 1].reshape(-1, D))
        sum_out, sum_qkv = summed(grad_w_out.reshape(D, D)), summed(qkv_grads.reshape(3, D, D).transpose(1, 0, 2).reshape(D, -1))
        sum_bout, sum_bup, sum_bdown = [summed(a.reshape(-1)) for a in (grad_b_out, grad_b_up, grad_b_down)]
    return output, grad_tokens, sum_mod, sum_bmod, sum_qkv, sum_out, sum_bout, sum_up, sum_bup, sum_down, sum_bdown


def solution(mesh):
    sizes = (mesh.shape["dp"], mesh.shape["fsdp"])
    rows, cut_rows, vector = P(("dp", "fsdp"), None), P("fsdp", None), P("fsdp")
    return jax.shard_map(
        functools.partial(local, sizes),
        mesh=mesh,
        in_specs=(rows, rows, rows, cut_rows, vector, cut_rows, cut_rows, vector, cut_rows, vector, cut_rows, vector, rows),
        out_specs=(rows, rows, cut_rows, vector, cut_rows, cut_rows, vector, cut_rows, vector, cut_rows, vector),
        check_vma=False,
    )
```
